32 devices in a mesh: dp: 16 (over z, x, core), tensor: 2 (over y).
Axes of the slice: x: 2, y: 2, z: 4, core: 2. Of those that a mesh axis runs over, the one named last changes fastest.
Arguments:
- layer_input: bfloat16 [16, 1024, 1024], P('dp', 'tensor'), may hold values from -6 to 6
- segments: int32 [16, 1024], P('dp'), may hold values from 0 to 3, never falling along the last dimension, each value on 1 to 512 neighbouring positions
- valid_mask: int32 [16, 1024], P('dp', 'tensor'), may hold values from 0 to 1, as said below
- teacher: bfloat16 [16, 1024, 1024], P('dp', 'tensor'), may hold values from -6 to 6
- out_grad: bfloat16 [16, 1024, 1024], P('dp', 'tensor'), may hold values from -6 to 6
- norm_gain: bfloat16 [1024], P('dp'), may hold values from 0.25 to 1.75
- w_query: bfloat16 [1024, 1024], P('dp', 'tensor'), may hold values from -0.1875 to 0.1875
- w_key: bfloat16 [1024, 1024], P('dp', 'tensor'), may hold values from -0.1875 to 0.1875
- w_value: bfloat16 [1024, 1024], P('dp', 'tensor'), may hold values from -0.1875 to 0.1875
- w_beta: bfloat16 [1024, 8], P('dp', 'tensor'), may hold values from -0.1875 to 0.1875
- conv_weight: bfloat16 [3, 4, 8, 128], P(None, None, 'tensor', 'dp'), may hold values from -3 to 3
- head_gain: bfloat16 [128], P('dp'), may hold values from 0.25 to 1.75
- w_out: bfloat16 [1024, 1024], P('tensor', 'dp'), may hold values from -0.1875 to 0.1875
- mlp_gain: bfloat16 [1024], P('dp'), may hold values from 0.25 to 1.75
- w_gate: bfloat16 [1024, 2816], P('dp', 'tensor'), may hold values from -0.1875 to 0.1875
- w_up: bfloat16 [1024, 2816], P('dp', 'tensor'), may hold values from -0.1875 to 0.1875
- w_down: bfloat16 [2816, 1024], P('tensor', 'dp'), may hold values from -0.109375 to 0.109375
Outputs:
- layer_output: bfloat16 [16, 1024, 1024], P('dp', 'tensor')
- teacher_loss: float32 [], replicated
- grad_input: float32 [16, 1024, 1024], P('dp', 'tensor')
- grad_norm_gain: float32 [1024], P('dp')
- grad_query: float32 [1024, 1024], P('dp', 'tensor')
- grad_key: float32 [1024, 1024], P('dp', 'tensor')
- grad_value: float32 [1024, 1024], P('dp', 'tensor')
- grad_beta: float32 [1024, 8], P('dp', 'tensor')
- grad_conv: float32 [3, 4, 8, 128], P(None, None, 'tensor', 'dp')
- grad_head_gain: float32 [128], P('dp')
- grad_out: float32 [1024, 1024], P('tensor', 'dp')
- grad_mlp_gain: float32 [1024], P('dp')
- grad_gate: float32 [1024, 2816], P('dp', 'tensor')
- grad_up: float32 [1024, 2816], P('dp', 'tensor')
- grad_down: float32 [2816, 1024], P('tensor', 'dp')
The draws below stay inside these ranges and needn't reach their ends.
Inputs may be any that keep to these rules, and one draw needn't show every extreme that they name: `segments`: document numbers start at 0 and never fall along a sequence; each of 0 to 3 is used, no document holds more than 512 tokens, and one holds exactly 512. `valid_mask`: the first token of every sequence is valid.
All inputs are finite; a program needn't handle non-finite values.
Results may differ from the reference program's by a relative error of at most 0.014.
Values may be sent and summed in bfloat16 or wider, within the bound.
A program may use at most 320 MiB of HBM per device.

```python
import math
import jax
import jax.numpy as jnp
import numpy as np
from jax import lax

D = 1024
H = 8
HD = 128
FF = 2816
TAPS = 4
BLOCK = 64
L = 1024
DOCS = 4
DOC_MAX = 512
SEQS = 16


def draw_valid_mask(key, part):
    index = jnp.arange(SEQS)
    bound = 250 + 500 * index // max(SEQS - 1, 1)
    drawn = jax.random.randint(key, (SEQS, L), 0, 1000)
    marks = (drawn < bound[:, None]).astype(jnp.int32)
    return marks.at[:, 0].set(1)


def block_scale(stream_key, extent, shards, smallest, largest):
    factor_of = 1.0
    for position, parts in shards:
        heights = jax.random.uniform(jax.random.fold_in(jax.random.fold_in(stream_key, 6), position), (parts,), jnp.float32, smallest / len(shards), largest / len(shards))
        factor_of = factor_of * jnp.repeat(jnp.exp(heights), extent[position] // parts).reshape((-1,) + (1,) * (len(extent) - 1 - position))
    return factor_of


def profile(amount, total, limit, skew):
    loads = [(1 << 20) // math.isqrt(standing ** skew) + 1 for standing in range(2, amount + 1)]
    spare, holding = total - limit - (amount - 1), [1] * (amount - 1)
    while spare > 0:
        movable = [i for i in range(amount - 1) if holding[i] < limit]
        whole, budget = sum([loads[i] for i in movable]), spare
        for i in movable:
            addition = min(limit - holding[i], max(1, budget * loads[i] // whole), spare)
            holding[i] = holding[i] + addition
            spare = spare - addition
    return np.array([limit] + holding)


def uneven(key, amount, total, limit, lean):
    if amount == 2:
        one = jax.random.randint(key, (), max(1, total - limit), min(limit, total - 1) + 1)
        return jnp.stack([one, total - one])
    sizes = jnp.asarray(profile(amount, total, limit, lean), jnp.int32)
    twos = (amount - 1) // 2
    giver, sink = sizes[1:1 + 2 * twos:2], sizes[2:2 + 2 * twos:2]
    margin = jnp.minimum(giver - 1, limit - sink)
    moved = jax.random.randint(jax.random.fold_in(key, 1), (twos,), 0, 1 << 20) % (margin + 1)
    sizes = sizes.at[1:1 + 2 * twos:2].set(giver - moved).at[2:2 + 2 * twos:2].set(sink + moved)
    return sizes[jax.random.permutation(jax.random.fold_in(key, 2), amount)]


def bell_draw(rng, shape, scale, most, split=(), kind=jnp.bfloat16):
    level = block_scale(rng, shape, split, -0.22, 0.18) if split else 1.0
    values = jax.random.normal(rng, shape, jnp.float32) * scale * level
    return jnp.minimum(jnp.maximum(values, -most), most).astype(kind)


def setup_inputs(seed: int = 0) -> dict:
    keys = jax.random.split(jax.random.key(seed), 18)
    layer_input = bell_draw(keys[0], (SEQS, L, D), 1.0, 6.0, ((0, 16), (1, 2)))
    segments = jax.vmap(lambda own: jnp.searchsorted(jnp.cumsum(uneven(own, DOCS, L, DOC_MAX, 0)), jnp.arange(L), side="right"))(jax.random.split(keys[1], SEQS)).reshape((SEQS, L)).astype(jnp.int32)
    valid_mask = draw_valid_mask(jax.random.fold_in(keys[17], 71), 0)
    teacher = bell_draw(keys[3], (SEQS, L, D), 1.0, 6.0, ((0, 16), (1, 2)))
    out_grad = bell_draw(keys[4], (SEQS, L, D), 1.0, 6.0, ((0, 16), (1, 2)))
    norm_gain = jnp.clip(1.0 + 0.15 * jax.random.normal(keys[5], (D,), jnp.float32), 0.25, 1.75).astype(jnp.bfloat16)
    w_query = bell_draw(keys[6], (D, D), D ** -0.5, 0.1875, ((0, 16), (1, 2)))
    w_key = bell_draw(keys[7], (D, D), D ** -0.5, 0.1875, ((0, 16), (1, 2)))
    w_value = bell_draw(keys[8], (D, D), D ** -0.5, 0.1875, ((0, 16), (1, 2)))
    w_beta = bell_draw(keys[9], (D, H), D ** -0.5, 0.1875, ((0, 16), (1, 2)))
    conv_weight = bell_draw(keys[10], (3, TAPS, H, HD), 0.5, 3.0, ((2, 2), (3, 16)))
    head_gain = jnp.clip(1.0 + 0.15 * jax.random.normal(keys[11], (HD,), jnp.float32), 0.25, 1.75).astype(jnp.bfloat16)
    w_out = bell_draw(keys[12], (D, D), D ** -0.5, 0.1875, ((0, 2), (1, 16)))
    mlp_gain = jnp.clip(1.0 + 0.15 * jax.random.normal(keys[13], (D,), jnp.float32), 0.25, 1.75).astype(jnp.bfloat16)
    w_gate = bell_draw(keys[14], (D, FF), D ** -0.5, 0.1875, ((0, 16), (1, 2)))
    w_up = bell_draw(keys[15], (D, FF), D ** -0.5, 0.1875, ((0, 16), (1, 2)))
    w_down = bell_draw(keys[16], (FF, D), FF ** -0.5, 0.109375, ((0, 2), (1, 16)))
    return dict(layer_input=layer_input, segments=segments, valid_mask=valid_mask, teacher=teacher, out_grad=out_grad, norm_gain=norm_gain, w_query=w_query, w_key=w_key, w_value=w_value, w_beta=w_beta, conv_weight=conv_weight, head_gain=head_gain, w_out=w_out, mlp_gain=mlp_gain, w_gate=w_gate, w_up=w_up, w_down=w_down)


highest = lax.Precision.HIGHEST

@jax.custom_vjp
def low(v):
    return lax.optimization_barrier(v.astype(jnp.bfloat16)).astype(jnp.float32)

@jax.custom_vjp
def low_back(v):
    return v

def low_keep(v):
    return (low(v), None)

def low_pass(kept, grad):
    return (grad,)

def back_keep(v):
    return (v, None)

def back_low(kept, grad):
    return (low(grad),)
low.defvjp(low_keep, low_pass)
low_back.defvjp(back_keep, back_low)

def shifted(values, offset, fill):
    widths = [(0, 0)] * values.ndim
    widths[1] = (offset, 0)
    return jnp.pad(values[:, :values.shape[1] - offset], widths, constant_values=fill)

def conv_keeps(segment):
    return [(shifted(segment, offset, -1) == segment).astype(jnp.float32)[..., None] for offset in range(TAPS)]

def conv_mix(linear, taps, keeps):
    total = linear * taps[0]
    for offset in range(1, TAPS):
        total = total + taps[offset] * shifted(linear, offset, 0.0) * keeps[offset]
    return total

def unit_rows(values, factor):
    return values * lax.rsqrt(lax.optimization_barrier(jnp.sum(values * values, -1, keepdims=True)) + 1e-06) * factor

def advance(state, inputs):
    feed, pull, keep = inputs
    updated = keep[:, None, None, None] * state + feed - jnp.einsum('bhef,bhfg->bheg', pull, state, precision=highest)
    return (updated, state)

def delta_rule(queries, keys_in, values_in, strength, segment, block):
    batch, length, heads, width = queries.shape
    number = length // block
    total = batch * number

    def by_blocks(values):
        return values.reshape((total, block) + values.shape[2:])
    q_b = by_blocks(queries)
    k_b = by_blocks(keys_in)
    v_b = by_blocks(values_in)
    s_b = by_blocks(strength)
    seg = by_blocks(segment)
    ends = segment.reshape(batch, number, block)[:, :, -1]
    previous = jnp.concatenate([jnp.full((batch, 1), -1, jnp.int32), ends[:, :-1].astype(jnp.int32)], 1).reshape(total)
    same = (seg[:, :, None] == seg[:, None, :]).astype(jnp.float32)
    first_mask = (seg == previous[:, None]).astype(jnp.float32)
    last_mask = (seg == seg[:, -1:]).astype(jnp.float32)
    rows = jnp.arange(block)[:, None]
    cols = jnp.arange(block)[None, :]
    strict = (rows > cols).astype(jnp.float32)
    inclusive = (rows >= cols).astype(jnp.float32)
    kk_prod = jnp.einsum('bihe,bjhe->bhij', k_b, k_b, precision=highest)
    strength_t = jnp.transpose(s_b, (0, 2, 1))
    system = jnp.eye(block, dtype=jnp.float32) + strength_t[..., None] * (kk_prod * (same * strict)[:, None])
    keys_t = jnp.transpose(k_b, (0, 2, 1, 3))
    values_t = jnp.transpose(v_b, (0, 2, 1, 3))
    right = strength_t[..., None] * jnp.concatenate([values_t, first_mask[:, None, :, None] * keys_t], -1)
    solved = lax.linalg.triangular_solve(system, right, left_side=True, lower=True, unit_diagonal=True)
    plain = solved[..., :width]
    along = solved[..., width:]
    scores = jnp.einsum('bihe,bjhe->bhij', q_b, k_b, precision=highest) * (same * inclusive)[:, None]
    last_keys = keys_t * last_mask[:, None, :, None]
    feed = jnp.einsum('bhie,bhif->bhef', last_keys, plain, precision=highest)
    pull = jnp.einsum('bhie,bhif->bhef', last_keys, along, precision=highest)
    keep = first_mask[:, -1]

    def by_turns(values):
        return jnp.moveaxis(values.reshape((batch, number) + values.shape[1:]), 1, 0)
    start = jnp.zeros((batch, heads, width, width), jnp.float32)
    ending, befores = lax.scan(jax.checkpoint(advance), start, (by_turns(feed), by_turns(pull), by_turns(keep)))
    befores = jnp.moveaxis(befores, 0, 1).reshape(total, heads, width, width)
    queries_t = jnp.transpose(q_b, (0, 2, 1, 3))
    reach = first_mask[:, None, :, None] * queries_t - jnp.einsum('bhij,bhje->bhie', scores, along, precision=highest)
    outputs = jnp.einsum('bhie,bhef->bhif', reach, befores, precision=highest) + jnp.einsum('bhij,bhjf->bhif', scores, plain, precision=highest)
    return jnp.transpose(outputs, (0, 2, 1, 3)).reshape(batch, length, heads, width)

def mixer(linears, taps, head_gain, keeps, segment, heads, block):
    q_lin, k_lin, v_lin, b_lin = linears
    batch, length, channels = q_lin.shape
    width = channels // heads

    def prepare(linear, index):
        return jax.nn.silu(conv_mix(linear, taps[index], keeps)).reshape(batch, length, heads, width)
    queries = unit_rows(prepare(q_lin, 0), width ** (-0.5))
    keys_in = unit_rows(prepare(k_lin, 1), 1.0)
    values_in = prepare(v_lin, 2)
    strength = jax.nn.sigmoid(b_lin)
    mixed = delta_rule(queries, keys_in, values_in, strength, segment, block)
    normed = mixed * lax.rsqrt(lax.optimization_barrier(jnp.mean(mixed * mixed, -1, keepdims=True)) + 1e-05) * head_gain
    return normed.reshape(batch, length, channels)

def block_forward(params, inputs, segment):
    gain_one, w_q, w_k, w_v, w_b, conv_full, gain_head, w_o, gain_two, w_g, w_u, w_d = params

    def project(left, right):
        return jnp.einsum('bld,de->ble', left, right, precision=highest)
    unit_one = inputs * lax.rsqrt(lax.optimization_barrier(jnp.mean(inputs * inputs, -1, keepdims=True)) + 1e-05)
    normed_one = low(unit_one * gain_one)
    linears = (low_back(project(normed_one, w_q)), low_back(project(normed_one, w_k)), low_back(project(normed_one, w_v)), low_back(project(normed_one, w_b)))
    taps = conv_full.reshape(3, conv_full.shape[1], -1)
    mixed = mixer(linears, taps, gain_head, conv_keeps(segment), segment, H, BLOCK)
    hidden = inputs + low_back(project(low(mixed), w_o))
    unit_two = hidden * lax.rsqrt(lax.optimization_barrier(jnp.mean(hidden * hidden, -1, keepdims=True)) + 1e-05)
    normed_two = low(unit_two * gain_two)
    gate = low_back(project(normed_two, w_g))
    upper = low_back(project(normed_two, w_u))
    inner = low(jax.nn.silu(gate) * upper)
    return hidden + low_back(project(inner, w_d))

def reference(layer_input, segments, valid_mask, teacher, out_grad, norm_gain, w_query, w_key, w_value, w_beta, conv_weight, head_gain, w_out, mlp_gain, w_gate, w_up, w_down):
    params = tuple((p.astype(jnp.float32) for p in (norm_gain, w_query, w_key, w_value, w_beta, conv_weight, head_gain, w_out, mlp_gain, w_gate, w_up, w_down)))
    group = math.gcd(SEQS, max(1, 4096 // L))
    groups = SEQS // group

    def grouped(values):
        return values.reshape((groups, group) + values.shape[1:])
    mask = valid_mask.astype(jnp.float32)
    total_valid = jnp.sum(mask)
    targets = teacher.astype(jnp.float32)

    def forward(inputs, weights):

        def step_group(carry, pieces):
            inputs_g, segment_g, mask_g, target_g = pieces
            outputs_g = block_forward(weights, inputs_g, segment_g)
            differ = outputs_g - target_g
            return (carry + jnp.sum(mask_g[..., None] * differ * differ), outputs_g)
        total, outputs = lax.scan(jax.checkpoint(step_group), jnp.zeros((), jnp.float32), (grouped(inputs), grouped(segments), grouped(mask), grouped(targets)))
        return (outputs.reshape(inputs.shape), total / (D * total_valid))
    (outputs, loss_value), pullback = jax.vjp(forward, layer_input.astype(jnp.float32), params)
    loss_weight = jnp.asarray(SEQS * L * D / 8.0, jnp.float32)
    grad_input, grads = pullback((out_grad.astype(jnp.float32), loss_weight))
    g_norm, g_query, g_key, g_value, g_beta, g_conv, g_head, g_out, g_mlp, g_gate, g_up, g_down = grads
    return (outputs.astype(jnp.bfloat16), loss_value, grad_input, g_norm, g_query, g_key, g_value, g_beta, g_conv, g_head, g_out, g_mlp, g_gate, g_up, g_down)
```

```python
import functools

import jax
import jax.numpy as jnp
from jax import lax
from jax.experimental import pallas as pl
from jax.experimental.pallas import tpu as pltpu
from jax.sharding import PartitionSpec as P

F32, BF16 = jnp.float32, jnp.bfloat16
MESH = pl.DeviceIdType.MESH
CHUNK = 128
HALO = 16
WIDTH = 128
PAIR = 2
TAPS = 4
VMEM_LIMIT = 60 * 1024 * 1024


def contract(left, right, dim_left, dim_right):
    return lax.dot_general(
        left.astype(BF16),
        right.astype(BF16),
        (((dim_left,), (dim_right,)), ((), ())),
        preferred_element_type=F32,
    )


def mm(left, right):
    return contract(left, right, 1, 0)


def mm_t(left, right):
    return contract(left, right, 1, 1)


def t_mm(left, right):
    return contract(left, right, 0, 0)


def tri_inverse(system, rows, cols):
    eye = (rows == cols).astype(F32)
    inverse = eye
    size = 1
    while size < CHUNK:
        link = (
            (rows // (2 * size) == cols // (2 * size))
            & ((rows // size) % 2 == 1)
            & ((cols // size) % 2 == 0)
        )
        part = jnp.where(link, system, 0.0)
        if size == 1:
            inverse = eye - part
        else:
            inverse = inverse - mm(inverse, mm(part, inverse))
        size *= 2
    return inverse


def conv_of(lin_ref, base, lanes, taps, row, keeps, tokens):
    total = lin_ref[0, base : base + tokens, lanes] * taps[row : row + 1]
    for off in range(1, TAPS):
        total = total + taps[row + off : row + off + 1] * (
            lin_ref[0, base - off : base - off + tokens, lanes] * keeps[off]
        )
    return total


def head_column(aux, lane):
    lanes = lax.broadcasted_iota(jnp.int32, aux.shape, 1)
    return jnp.sum(jnp.where(lanes == lane, aux, 0.0), axis=1, keepdims=True)


def greet(partner):
    barrier = pltpu.get_barrier_semaphore()
    pl.semaphore_signal(
        barrier, inc=1, device_id={"tensor": partner}, device_id_type=MESH
    )
    pl.semaphore_wait(barrier, 1)


def chunk_masks(aux, seg_row, at):
    rows = lax.broadcasted_iota(jnp.int32, (CHUNK, CHUNK), 0)
    cols = lax.broadcasted_iota(jnp.int32, (CHUNK, CHUNK), 1)
    same = aux[at : at + CHUNK, 0:1] == seg_row[0:1, at : at + CHUNK]
    return same & (rows > cols), same & (rows >= cols), rows, cols


def mixer_fwd_kernel(
    tokens, q_ref, k_ref, v_ref, aux_ref, seg_ref, taps_ref, gain_ref,
    onb_ref, o_ref, n_ref, t_ref, s_ref,
    state, outbox, inbox, send_sem, recv_sem,
):
    step = pl.program_id(0)
    mine = lax.axis_index("tensor")
    chunks = tokens // CHUNK

    @pl.when(step == 0)
    def _():
        greet(1 - mine)

    def hand_over(head):
        return pltpu.make_async_remote_copy(
            src_ref=outbox.at[head],
            dst_ref=inbox.at[head],
            send_sem=send_sem.at[head],
            recv_sem=recv_sem.at[head],
            device_id={"tensor": 1 - mine},
            device_id_type=MESH,
        )

    aux = aux_ref[...]
    seg_row = seg_ref[...]
    keeps = [None] + [aux[:, 2 + off : 3 + off] for off in range(1, TAPS)]
    heads = []
    for sub in range(PAIR):
        lanes = slice(sub * WIDTH, (sub + 1) * WIDTH)
        taps = taps_ref[:, lanes]
        beta = head_column(aux, 16 + step * PAIR + sub)
        acts = []
        for index, ref in enumerate((q_ref, k_ref, v_ref)):
            mixed = conv_of(ref, HALO, lanes, taps, index * TAPS, keeps, tokens)
            acts.append(mixed * jax.nn.sigmoid(mixed))
        q = acts[0] * (
            lax.rsqrt(jnp.sum(acts[0] * acts[0], -1, keepdims=True) + 1e-06) * WIDTH ** (-0.5)
        )
        k = acts[1] * lax.rsqrt(jnp.sum(acts[1] * acts[1], -1, keepdims=True) + 1e-06)
        heads.append((q, k, acts[2], beta))
    inner = []
    for sub in range(PAIR):
        q, k, v, beta = heads[sub]
        for c in range(chunks):
            at = c * CHUNK
            strict, inclusive, rows, cols = chunk_masks(aux, seg_row, at)
            kc, qc = k[at : at + CHUNK], q[at : at + CHUNK]
            system = jnp.where(strict, beta[at : at + CHUNK] * mm_t(kc, kc), 0.0)
            inverse = tri_inverse(system, rows, cols).astype(BF16)
            t_ref[sub, c] = inverse
            inner.append((inverse, jnp.where(inclusive, mm_t(qc, kc), 0.0).astype(BF16)))

    @pl.when(mine == 0)
    def _():
        state[...] = jnp.zeros_like(state)

    @pl.when(mine == 1)
    def _():
        for sub in range(PAIR):
            head = step * PAIR + sub
            hand_over(head).wait_recv()
            state[sub] = inbox[head]

    carried = [state[sub] for sub in range(PAIR)]
    for c in range(chunks):
        at = c * CHUNK
        first = aux[at : at + CHUNK, 1:2]
        last = aux[at : at + CHUNK, 2:3]
        keep = aux[at + CHUNK - 1 : at + CHUNK, 1:2]
        for sub in range(PAIR):
            q, k, v, beta = heads[sub]
            inverse, scores = inner[sub * chunks + c]
            kc, qc = k[at : at + CHUNK], q[at : at + CHUNK]
            before = carried[sub].astype(BF16)
            s_ref[sub, c] = before
            rhs = beta[at : at + CHUNK] * (v[at : at + CHUNK] - first * mm(kc, before))
            new = mm(inverse, rhs).astype(BF16)
            n_ref[sub, c] = new
            out = first * mm(qc, before) + mm(scores, new)
            lanes = slice(sub * WIDTH, (sub + 1) * WIDTH)
            o_ref[0, at : at + CHUNK, lanes] = out
            scale = lax.rsqrt(jnp.mean(out * out, -1, keepdims=True) + 1e-05)
            onb_ref[0, at : at + CHUNK, lanes] = (out * scale * gain_ref[0:1]).astype(BF16)
            carried[sub] = keep * carried[sub] + t_mm(last * kc, new)

    @pl.when(mine == 0)
    def _():
        for sub in range(PAIR):
            head = step * PAIR + sub
            outbox[head] = carried[sub]
            hand_over(head).start()

    @pl.when((step == pl.num_programs(0) - 1) & (mine == 0))
    def _():
        for head in range(outbox.shape[0]):
            hand_over(head).wait_send()


def mixer_bwd_kernel(
    tokens, q_ref, k_ref, v_ref, aux_ref, seg_ref, taps_ref, gain_ref,
    o_ref, n_ref, t_ref, s_ref, donb_ref,
    dlin_ref, dbl_ref, dtaps_ref, dgain_ref,
    state, extended, outbox, inbox, tailbox, headbox, send_sem, recv_sem, tail_send, tail_recv,
):
    step = pl.program_id(0)
    mine = lax.axis_index("tensor")
    chunks = tokens // CHUNK

    @pl.when(step == 0)
    def _():
        greet(1 - mine)
        dbl_ref[...] = jnp.zeros_like(dbl_ref)
        dgain_ref[...] = jnp.zeros_like(dgain_ref)

    def hand_over(head):
        return pltpu.make_async_remote_copy(
            src_ref=outbox.at[head],
            dst_ref=inbox.at[head],
            send_sem=send_sem.at[head],
            recv_sem=recv_sem.at[head],
            device_id={"tensor": 1 - mine},
            device_id_type=MESH,
        )

    def hand_tail(head):
        return pltpu.make_async_remote_copy(
            src_ref=tailbox.at[head],
            dst_ref=headbox.at[head],
            send_sem=tail_send.at[head],
            recv_sem=tail_recv.at[head],
            device_id={"tensor": 1 - mine},
            device_id_type=MESH,
        )

    aux = aux_ref[...]
    seg_row = seg_ref[...]
    keeps = [None] + [aux[:tokens, 2 + off : 3 + off] for off in range(1, TAPS)]
    heads, inner = [], []
    for sub in range(PAIR):
        lanes = slice(sub * WIDTH, (sub + 1) * WIDTH)
        taps = taps_ref[:, lanes]
        beta = head_column(aux[:tokens], 16 + step * PAIR + sub)
        mixes, sigs, acts = [], [], []
        for index, ref in enumerate((q_ref, k_ref, v_ref)):
            mixed = conv_of(ref, HALO, lanes, taps, index * TAPS, keeps, tokens)
            mixes.append(mixed)
            sigs.append(jax.nn.sigmoid(mixed))
            acts.append(mixed * sigs[-1])
        rho_q = lax.rsqrt(jnp.sum(acts[0] * acts[0], -1, keepdims=True) + 1e-06)
        rho_k = lax.rsqrt(jnp.sum(acts[1] * acts[1], -1, keepdims=True) + 1e-06)
        q = acts[0] * (rho_q * WIDTH ** (-0.5))
        k = acts[1] * rho_k
        out = o_ref[0, :, lanes]
        don = donb_ref[0, :, lanes]
        scale = lax.rsqrt(jnp.mean(out * out, -1, keepdims=True) + 1e-05)
        dgain_ref[0:1] += jnp.sum(don * out * scale, 0, keepdims=True)
        du = don * gain_ref[0:1]
        dout = scale * du - out * (scale * scale * scale) * jnp.mean(
            out * du, -1, keepdims=True
        )
        heads.append((q, k, acts, beta, mixes, sigs, rho_q, rho_k, dout))
        for c in range(chunks):
            at = c * CHUNK
            strict, inclusive, _, _ = chunk_masks(aux, seg_row, at)
            first = aux[at : at + CHUNK, 1:2]
            kc, qc = k[at : at + CHUNK], q[at : at + CHUNK]
            do = dout[at : at + CHUNK]
            before, new = s_ref[sub, c], n_ref[sub, c]
            kk = mm_t(kc, kc)
            scores = jnp.where(inclusive, mm_t(qc, kc), 0.0)
            dscores = jnp.where(inclusive, mm_t(do, new), 0.0)
            dq = first * mm_t(do, before) + mm(dscores, kc)
            dk = t_mm(dscores, qc)
            gap = acts[2][at : at + CHUNK] - first * mm(kc, before)
            inner.append(
                (kk, strict, t_mm(scores, do), t_mm(first * qc, do), dq, dk, gap)
            )

    @pl.when(mine == 1)
    def _():
        state[...] = jnp.zeros_like(state)

    @pl.when(mine == 0)
    def _():
        for sub in range(PAIR):
            head = step * PAIR + sub
            hand_over(head).wait_recv()
            state[sub] = inbox[head]

    carried = [state[sub] for sub in range(PAIR)]
    pieces = [[None] * chunks for _ in range(PAIR)]
    for c in reversed(range(chunks)):
        at = c * CHUNK
        first = aux[at : at + CHUNK, 1:2]
        last = aux[at : at + CHUNK, 2:3]
        keep = aux[at + CHUNK - 1 : at + CHUNK, 1:2]
        for sub in range(PAIR):
            q, k, acts, beta = heads[sub][:4]
            kk, strict, pulled, reached, dq, dk, gap = inner[sub * chunks + c]
            kc = k[at : at + CHUNK]
            bc = beta[at : at + CHUNK]
            before, new = s_ref[sub, c], n_ref[sub, c]
            after = carried[sub].astype(BF16)
            dnew = pulled + mm(last * kc, after)
            back = t_mm(t_ref[sub, c], dnew)
            dv = bc * back
            dks = -(first * dv)
            carried[sub] = keep * carried[sub] + reached + t_mm(kc, dks)
            dsystem = jnp.where(strict, -mm_t(back, new), 0.0)
            dbeta = jnp.sum(back * gap, -1, keepdims=True) + jnp.sum(
                dsystem * kk, -1, keepdims=True
            )
            grow = bc * dsystem
            dk = (
                dk
                + last * mm_t(new, after)
                + mm_t(dks, before)
                + mm(grow, kc)
                + t_mm(grow, kc)
            )
            pieces[sub][c] = (dq, dk, dv, dbeta)

    @pl.when(mine == 1)
    def _():
        for sub in range(PAIR):
            head = step * PAIR + sub
            outbox[head] = carried[sub]
            hand_over(head).start()

    lane_ids = lax.broadcasted_iota(jnp.int32, (tokens, WIDTH), 1)
    for sub in range(PAIR):
        head = step * PAIR + sub
        q, k, acts, beta, mixes, sigs, rho_q, rho_k, dout = heads[sub]
        dq, dk, dv, dbeta = (
            jnp.concatenate([pieces[sub][c][item] for c in range(chunks)], 0)
            for item in range(4)
        )
        dbl_ref[...] += jnp.where(lane_ids == head, dbeta * beta * (1.0 - beta), 0.0)
        dq = dq * WIDTH ** (-0.5)
        dacts = (
            rho_q * dq
            - acts[0] * (rho_q * rho_q * rho_q) * jnp.sum(acts[0] * dq, -1, keepdims=True),
            rho_k * dk
            - acts[1] * (rho_k * rho_k * rho_k) * jnp.sum(acts[1] * dk, -1, keepdims=True),
            dv,
        )
        for index in range(3):
            sig = sigs[index]
            dmix = dacts[index] * sig * (1.0 + mixes[index] * (1.0 - sig))
            extended[sub, index, 0:tokens] = dmix
            tailbox[head, index] = dmix[0:8]

    @pl.when(mine == 1)
    def _():
        extended[:, :, tokens : tokens + 8] = jnp.zeros((PAIR, 3, 8, WIDTH), F32)
        for sub in range(PAIR):
            hand_tail(step * PAIR + sub).start()

    @pl.when(mine == 0)
    def _():
        for sub in range(PAIR):
            head = step * PAIR + sub
            hand_tail(head).wait_recv()
            extended[sub, :, tokens : tokens + 8] = headbox[head]

    later = [None] + [aux[:, 5 + off : 6 + off] for off in range(1, TAPS)]
    refs = (q_ref, k_ref, v_ref)
    for sub in range(PAIR):
        lanes = slice(sub * WIDTH, (sub + 1) * WIDTH)
        taps = taps_ref[:, lanes]
        for index in range(3):
            row = index * TAPS
            dmix = extended[sub, index, 0:tokens]
            dlin = dmix * taps[row : row + 1]
            dtaps_ref[row : row + 1, lanes] = jnp.sum(
                dmix * refs[index][0, HALO : HALO + tokens, lanes], 0, keepdims=True
            )
            for off in range(1, TAPS):
                dlin = dlin + taps[row + off : row + off + 1] * (
                    extended[sub, index, off : off + tokens] * later[off]
                )
                dtaps_ref[row + off : row + off + 1, lanes] = jnp.sum(
                    dmix * keeps[off] * refs[index][0, HALO - off : HALO - off + tokens, lanes],
                    0,
                    keepdims=True,
                )
            dlin_ref[0, index, :, lanes] = dlin.astype(BF16)
        dtaps_ref[12:16, lanes] = jnp.zeros((4, WIDTH), F32)

    @pl.when((step == pl.num_programs(0) - 1) & (mine == 1))
    def _():
        for head in range(outbox.shape[0]):
            hand_over(head).wait_send()
            hand_tail(head).wait_send()


def mixer_specs(rows, half_heads):
    per_half = half_heads // PAIR
    lanes = PAIR * WIDTH

    def at(offset):
        return pl.BlockSpec(
            (1, rows, lanes), lambda i: (i // per_half, 0, offset * per_half + i % per_half)
        )

    return [at(0), at(1), at(2)]


def mixer_fwd(linear, aux, seg_row, taps, gain):
    halves, rows, cols = linear.shape
    tokens = rows - HALO
    half_heads = cols // 3 // WIDTH
    heads = halves * half_heads
    per_half = half_heads // PAIR
    chunks = tokens // CHUNK
    lanes = PAIR * WIDTH

    def whole(shape):
        return pl.BlockSpec(shape, lambda i: (0,) * len(shape))

    token_spec = pl.BlockSpec((1, tokens, lanes), lambda i: (i // per_half, 0, i % per_half))
    square = pl.BlockSpec((PAIR, chunks, CHUNK, WIDTH), lambda i: (i, 0, 0, 0))
    square_shape = jax.ShapeDtypeStruct((heads, chunks, CHUNK, WIDTH), BF16)
    return pl.pallas_call(
        functools.partial(mixer_fwd_kernel, tokens),
        grid=(heads // PAIR,),
        in_specs=mixer_specs(rows, half_heads)
        + [
            whole(aux.shape),
            whole(seg_row.shape),
            pl.BlockSpec((16, lanes), lambda i: (0, i)),
            whole(gain.shape),
        ],
        out_specs=[token_spec, token_spec, square, square, square],
        out_shape=[
            jax.ShapeDtypeStruct((halves, tokens, half_heads * WIDTH), BF16),
            jax.ShapeDtypeStruct((halves, tokens, half_heads * WIDTH), F32),
            square_shape,
            square_shape,
            square_shape,
        ],
        scratch_shapes=[
            pltpu.VMEM((PAIR, WIDTH, WIDTH), F32),
            pltpu.VMEM((heads, WIDTH, WIDTH), F32),
            pltpu.VMEM((heads, WIDTH, WIDTH), F32),
            pltpu.SemaphoreType.DMA((heads,)),
            pltpu.SemaphoreType.DMA((heads,)),
        ],
        compiler_params=pltpu.CompilerParams(
            collective_id=0, has_side_effects=True, vmem_limit_bytes=VMEM_LIMIT
        ),
        name="mixer_fwd",
    )(linear, linear, linear, aux, seg_row, taps, gain)


def mixer_bwd(linear, aux, seg_row, taps, gain, out, new, inverse, before, donb):
    halves, rows, cols = linear.shape
    tokens = rows - HALO
    half_heads = cols // 3 // WIDTH
    heads = halves * half_heads
    per_half = half_heads // PAIR
    chunks = tokens // CHUNK
    lanes = PAIR * WIDTH

    def whole(shape):
        return pl.BlockSpec(shape, lambda i: (0,) * len(shape))

    token_spec = pl.BlockSpec((1, tokens, lanes), lambda i: (i // per_half, 0, i % per_half))
    square = pl.BlockSpec((PAIR, chunks, CHUNK, WIDTH), lambda i: (i, 0, 0, 0))
    taps_spec = pl.BlockSpec((16, lanes), lambda i: (0, i))
    return pl.pallas_call(
        functools.partial(mixer_bwd_kernel, tokens),
        grid=(heads // PAIR,),
        in_specs=mixer_specs(rows, half_heads)
        + [
            whole(aux.shape),
            whole(seg_row.shape),
            taps_spec,
            whole(gain.shape),
            token_spec,
            square,
            square,
            square,
            token_spec,
        ],
        out_specs=[
            pl.BlockSpec(
                (1, 3, tokens, lanes), lambda i: (i // per_half, 0, 0, i % per_half)
            ),
            whole((tokens, WIDTH)),
            taps_spec,
            whole((8, WIDTH)),
        ],
        out_shape=[
            jax.ShapeDtypeStruct((halves, 3, tokens, half_heads * WIDTH), BF16),
            jax.ShapeDtypeStruct((tokens, WIDTH), F32),
            jax.ShapeDtypeStruct((16, heads * WIDTH), F32),
            jax.ShapeDtypeStruct((8, WIDTH), F32),
        ],
        scratch_shapes=[
            pltpu.VMEM((PAIR, WIDTH, WIDTH), F32),
            pltpu.VMEM((PAIR, 3, tokens + 8, WIDTH), F32),
            pltpu.VMEM((heads, WIDTH, WIDTH), F32),
            pltpu.VMEM((heads, WIDTH, WIDTH), F32),
            pltpu.VMEM((heads, 3, 8, WIDTH), F32),
            pltpu.VMEM((heads, 3, 8, WIDTH), F32),
            pltpu.SemaphoreType.DMA((heads,)),
            pltpu.SemaphoreType.DMA((heads,)),
            pltpu.SemaphoreType.DMA((heads,)),
            pltpu.SemaphoreType.DMA((heads,)),
        ],
        compiler_params=pltpu.CompilerParams(
            collective_id=1, has_side_effects=True, vmem_limit_bytes=VMEM_LIMIT
        ),
        name="mixer_bwd",
    )(linear, linear, linear, aux, seg_row, taps, gain, out, new, inverse, before, donb)


def product(left, right):
    return jnp.dot(left, right, preferred_element_type=F32)


def back_product(left, right):
    return lax.dot_general(left, right, (((1,), (1,)), ((), ())), preferred_element_type=F32)


def transposed(left, right):
    return lax.dot_general(left, right, (((0,), (0,)), ((), ())), preferred_element_type=F32)


def norm_back(d_rows, unit, rho, gain_f):
    d_unit = d_rows * gain_f
    d_input = rho * (d_unit - unit * jnp.mean(d_unit * unit, -1, keepdims=True))
    return (d_input, jnp.sum(d_rows * unit, 0))


def mixer_tables(segments, length, beta, tokens):
    mine = lax.axis_index("tensor")
    seg = segments[0]
    position = jnp.arange(length)

    def behind(off):
        return jnp.where(position >= off, jnp.roll(seg, off), -1)

    ends = jnp.repeat(seg[CHUNK - 1 :: CHUNK], CHUNK)
    previous = jnp.where(position >= CHUNK, jnp.roll(ends, CHUNK), -1)
    columns = [seg, seg == previous, seg == ends]
    keeps = [behind(off) == seg for off in range(1, TAPS)]
    columns += keeps
    for off in range(1, TAPS):
        columns.append(jnp.where(position < length - off, jnp.roll(keeps[off - 1], -off), False))
    table = jnp.stack([c.astype(F32) for c in columns], 1)
    table = lax.dynamic_slice_in_dim(table, mine * tokens, tokens, 0)
    aux = jnp.concatenate(
        [
            table,
            jnp.zeros((tokens, 16 - table.shape[1]), F32),
            beta,
            jnp.zeros((tokens, WIDTH - 16 - beta.shape[1]), F32),
        ],
        1,
    )
    row = lax.dynamic_slice_in_dim(seg.astype(F32), mine * tokens, tokens, 0)
    return aux, jnp.broadcast_to(row[None], (8, tokens))


def local(
    layer_input, segments, valid_mask, teacher, out_grad, norm_gain, w_query, w_key, w_value,
    w_beta, conv_weight, head_gain, w_out, mlp_gain, w_gate, w_up, w_down,
):
    both = ("tensor", "dp")
    parts, halves = lax.axis_size("dp"), lax.axis_size("tensor")
    tokens, width_d = layer_input.shape[1:]
    length = segments.shape[1]
    tokens_all = tokens * parts * halves
    half_heads = w_beta.shape[1]
    heads = half_heads * halves
    half_cols = w_query.shape[1]
    half_units = w_gate.shape[1]

    small = jnp.concatenate(
        [w_beta.reshape(-1), conv_weight.reshape(-1), norm_gain, mlp_gain, head_gain]
    )
    small = lax.all_gather(small, both, axis=0, tiled=False)
    first_w = lax.all_gather(
        jnp.concatenate([w_query, w_key, w_value], 1), both, axis=0, tiled=True
    ).reshape(halves, width_d, 3 * half_cols)
    second_w = lax.all_gather(
        jnp.concatenate([w_out.T, w_gate, w_up, w_down.T], 1), both, axis=0, tiled=True
    ).reshape(halves, width_d, half_cols + 3 * half_units)
    w_o = second_w[:, :, :half_cols]
    w_gu = second_w[:, :, half_cols : half_cols + 2 * half_units]
    w_d = second_w[:, :, half_cols + 2 * half_units :]

    small = small.reshape(halves, parts, -1)
    sizes = [w_beta.size, conv_weight.size, norm_gain.size, mlp_gain.size, head_gain.size]
    marks = [sum(sizes[:i]) for i in range(6)]
    beta_w, conv_w, gain_one, gain_two, gain_head = (
        small[:, :, marks[i] : marks[i + 1]] for i in range(5)
    )
    beta_w = beta_w.reshape(halves, width_d, half_heads).transpose(1, 0, 2).reshape(width_d, heads)
    taps = conv_w.reshape((halves, parts) + conv_weight.shape).transpose(2, 3, 0, 4, 1, 5)
    taps = taps.reshape(12, heads * WIDTH).astype(F32)
    taps = jnp.concatenate([taps, jnp.zeros((4, heads * WIDTH), F32)], 0)
    gain_one = gain_one[0].reshape(1, width_d).astype(F32)
    gain_two = gain_two[0].reshape(1, width_d).astype(F32)
    gain_head = jnp.broadcast_to(gain_head[0].reshape(1, WIDTH).astype(F32), (8, WIDTH))

    inputs = layer_input[0].astype(F32)
    rho_one = lax.rsqrt(jnp.mean(inputs * inputs, -1, keepdims=True) + 1e-05)
    unit_one = inputs * rho_one
    normed_one = (unit_one * gain_one).astype(BF16)
    halo = lax.ppermute(normed_one[-HALO:], "tensor", [(0, 1), (1, 0)])
    spread = jnp.concatenate([halo, normed_one], 0)
    linear = jnp.einsum("td,jdc->jtc", spread, first_w, preferred_element_type=F32)
    strength = jax.nn.sigmoid(product(normed_one, beta_w))
    aux, seg_row = mixer_tables(segments, length, strength, tokens)
    onb, out, new, inverse, before = mixer_fwd(linear, aux, seg_row, taps, gain_head)
    attention = sum(back_product(onb[j], w_o[j]) for j in range(halves))
    hidden = inputs + attention
    rho_two = lax.rsqrt(jnp.mean(hidden * hidden, -1, keepdims=True) + 1e-05)
    unit_two = hidden * rho_two
    normed_two = (unit_two * gain_two).astype(BF16)
    mlp_rows = 0.0
    kept = []
    for j in range(halves):
        gate = product(normed_two, w_gu[j, :, :half_units])
        upper = product(normed_two, w_gu[j, :, half_units:])
        sig = jax.nn.sigmoid(gate)
        active = gate * sig
        inner = (active * upper).astype(BF16)
        mlp_rows = mlp_rows + back_product(inner, w_d[j])
        kept.append((gate, upper, sig, active, inner))
    outputs = hidden + mlp_rows
    mask = valid_mask[0].astype(F32)[:, None]
    differ = outputs - teacher[0].astype(F32)
    valid_sum = lax.psum(jnp.sum(mask), ("dp", "tensor"))
    square_sum = lax.psum(jnp.sum(mask * differ * differ), ("dp", "tensor"))
    loss_value = square_sum / (width_d * valid_sum)
    d_out = out_grad[0].astype(F32) + mask * differ * (tokens_all / 4.0) / valid_sum
    d_mlp = d_out.astype(BF16)
    d_two = 0.0
    grads = []
    for j in range(halves):
        gate, upper, sig, active, inner = kept[j]
        d_inner = product(d_mlp, w_d[j])
        d_gate = (d_inner * upper * sig * (1.0 + gate * (1.0 - sig))).astype(BF16)
        d_upper = (d_inner * active).astype(BF16)
        d_two = (
            d_two
            + back_product(d_gate, w_gu[j, :, :half_units])
            + back_product(d_upper, w_gu[j, :, half_units:])
        )
        grads.append(
            [
                transposed(normed_two, d_gate),
                transposed(normed_two, d_upper),
                transposed(d_mlp, inner),
            ]
        )
    d_norm_two, grad_gain_two = norm_back(d_two, unit_two, rho_two, gain_two)
    d_hidden = d_out + d_norm_two
    d_attention = d_hidden.astype(BF16)
    donb = jnp.stack([product(d_attention, w_o[j]) for j in range(halves)])
    for j in range(halves):
        grads[j].insert(0, transposed(d_attention, onb[j]))
    second_g = jnp.stack([jnp.concatenate([g.astype(BF16) for g in grads[j]], 1) for j in range(halves)])
    second_g = lax.psum_scatter(
        second_g.reshape(halves * width_d, -1), both, scatter_dimension=0, tiled=True
    ).astype(F32)
    dlin, dbl, dtaps, dgain = mixer_bwd(
        linear, aux, seg_row, taps, gain_head, out, new, inverse, before, donb
    )
    d_beta = dbl[:, :heads].astype(BF16)
    d_one = back_product(d_beta, beta_w)
    first_g = []
    for j in range(halves):
        row = []
        for c in range(3):
            d_one = d_one + back_product(
                dlin[j, c], first_w[j, :, c * half_cols : (c + 1) * half_cols]
            )
            row.append(transposed(normed_one, dlin[j, c]).astype(BF16))
        first_g.append(jnp.concatenate(row, 1))
    first_g = lax.psum_scatter(
        jnp.concatenate(first_g, 0), both, scatter_dimension=0, tiled=True
    ).astype(F32)
    grad_beta = transposed(normed_one, d_beta)
    d_norm_one, grad_gain_one = norm_back(d_one, unit_one, rho_one, gain_one)
    d_input = d_hidden + d_norm_one

    tail = jnp.concatenate(
        [
            grad_beta.reshape(-1),
            dtaps[:12].reshape(-1),
            grad_gain_one,
            grad_gain_two,
            dgain[0],
        ]
    )
    tail = lax.psum(tail, ("dp", "tensor"))
    tail_sizes = [width_d * heads, 12 * heads * WIDTH, width_d, width_d, WIDTH]
    cuts = [sum(tail_sizes[:i]) for i in range(6)]
    g_beta, g_conv, g_one, g_two, g_head = (tail[cuts[i] : cuts[i + 1]] for i in range(5))
    d_at, t_at = lax.axis_index("dp"), lax.axis_index("tensor")

    def own(values, dim, at, size):
        return lax.dynamic_slice_in_dim(values, at * size, size, dim)

    g_beta = own(g_beta.reshape(width_d, heads), 0, d_at, w_beta.shape[0])
    g_beta = own(g_beta, 1, t_at, half_heads)
    g_conv = own(g_conv.reshape(3, TAPS, heads, WIDTH), 2, t_at, half_heads)
    g_conv = own(g_conv, 3, d_at, conv_weight.shape[3])
    g_one = own(g_one, 0, d_at, norm_gain.shape[0])
    g_two = own(g_two, 0, d_at, mlp_gain.shape[0])
    g_head = own(g_head, 0, d_at, head_gain.shape[0])
    return (
        outputs.astype(BF16)[None],
        loss_value,
        d_input[None],
        g_one,
        first_g[:, :half_cols],
        first_g[:, half_cols : 2 * half_cols],
        first_g[:, 2 * half_cols :],
        g_beta,
        g_conv,
        g_head,
        second_g[:, :half_cols].T,
        g_two,
        second_g[:, half_cols : half_cols + half_units],
        second_g[:, half_cols + half_units : half_cols + 2 * half_units],
        second_g[:, half_cols + 2 * half_units :].T,
    )


def solution(mesh):
    in_specs = (
        P("dp", "tensor", None),
        P("dp", None),
        P("dp", "tensor"),
        P("dp", "tensor", None),
        P("dp", "tensor", None),
        P("dp"),
        P("dp", "tensor"),
        P("dp", "tensor"),
        P("dp", "tensor"),
        P("dp", "tensor"),
        P(None, None, "tensor", "dp"),
        P("dp"),
        P("tensor", "dp"),
        P("dp"),
        P("dp", "tensor"),
        P("dp", "tensor"),
        P("tensor", "dp"),
    )
    out_specs = (
        P("dp", "tensor", None),
        P(),
        P("dp", "tensor", None),
        P("dp"),
        P("dp", "tensor"),
        P("dp", "tensor"),
        P("dp", "tensor"),
        P("dp", "tensor"),
        P(None, None, "tensor", "dp"),
        P("dp"),
        P("tensor", "dp"),
        P("dp"),
        P("dp", "tensor"),
        P("dp", "tensor"),
        P("tensor", "dp"),
    )
    return jax.shard_map(local, mesh=mesh, in_specs=in_specs, out_specs=out_specs, check_vma=False)
```

```python
import collections
import functools
import itertools

import jax
import jax.numpy as jnp
from jax import lax
from jax.experimental import pallas as pl
from jax.experimental.pallas import tpu as pltpu
from jax.sharding import PartitionSpec as P

F32, BF16 = jnp.float32, jnp.bfloat16
MESH = pl.DeviceIdType.MESH
CHUNK = 128
HALO = 16
WIDTH = 128
PAIR = 2
EARLY = 4
TAPS = 4
VMEM_LIMIT = 60 * 1024 * 1024

GRID = (4, 2, 2)
DEPTH = GRID[0] - 1 + 2
LAGS = DEPTH + 2
LINKS = [("z", 1), ("z", -1), ("x", 0), ("y", 0)]
Tiles = collections.namedtuple(
    "Tiles", ["array", "order", "row", "rows", "col", "stride", "cols", "count", "start"]
)


def on_grid():
    return lax.axis_size("dp") == GRID[0] * GRID[1] * GRID[2] and lax.axis_size("tensor") == 2


def position():
    mine = lax.axis_index("dp")
    _, size_x, size_c = GRID
    return {
        "y": lax.axis_index("tensor"),
        "z": mine // (size_x * size_c),
        "x": (mine // size_c) % size_x,
        "c": mine % size_c,
    }


def device_of(at):
    _, size_x, size_c = GRID
    return {"dp": (at["z"] * size_x + at["x"]) * size_c + at["c"], "tensor": at["y"]}


def inside(z):
    return (z >= 0) & (z < GRID[0])


def across(at, link):
    axis, way = link
    return dict(at, z=at["z"] + way) if axis == "z" else dict(at, **{axis: 1 - at[axis]})


def greet_all(at):
    barrier = pltpu.get_barrier_semaphore()
    for link in (("x", 0), ("y", 0), ("c", 0)):
        pl.semaphore_signal(
            barrier, inc=1, device_id=device_of(across(at, link)), device_id_type=MESH
        )
    for way in (-1, 1):

        @pl.when(inside(at["z"] + way))
        def _():
            pl.semaphore_signal(
                barrier,
                inc=1,
                device_id=device_of(across(at, ("z", way))),
                device_id_type=MESH,
            )

    peers = 3 + inside(at["z"] - 1).astype(jnp.int32) + inside(at["z"] + 1).astype(jnp.int32)
    pl.semaphore_wait(barrier, peers)


def remote(src, dst, send_sem, recv_sem, to):
    return pltpu.make_async_remote_copy(
        src_ref=src, dst_ref=dst, send_sem=send_sem, recv_sem=recv_sem,
        device_id=device_of(to), device_id_type=MESH,
    )


def offsets(lag):
    every = itertools.product(range(1 - GRID[0], GRID[0]), (0, 1), (0, 1))
    return [off for off in every if abs(off[0]) + off[1] + off[2] == lag]


def moved(at, off):
    return dict(
        at,
        z=at["z"] + off[0],
        x=1 - at["x"] if off[1] else at["x"],
        y=1 - at["y"] if off[2] else at["y"],
    )


def last_axis(order, off):
    shifts = {"z": off[0], "x": off[1], "y": off[2]}
    return max([order.index(axis) for axis in order if shifts[axis]], default=-1)


def onward(order, off):
    last = last_axis(order, off)
    out = []
    if last >= 0 and order[last] == "z":
        out.append(("z", 1 if off[0] < 0 else -1))
    for axis in order[last + 1 :]:
        out += [("z", 1), ("z", -1)] if axis == "z" else [(axis, 0)]
    return out


def backward_link(order, off):
    axis = order[last_axis(order, off)]
    return (axis, (1 if off[0] > 0 else -1) if axis == "z" else 0)


def block_id(at):
    return (at["z"] * GRID[1] + at["x"]) * 2 + at["y"]


def inbox_id(order, link, at):
    if link[0] == "y" or (link[0] == "z" and order[0] != "y"):
        return at["z"] * 2 + at["x"]
    return at["z"] * 2 + at["y"]


def when(test, action):
    if test is None:
        action()
    else:
        pl.when(test)(action)


def both(first, second):
    if first is None or second is None:
        return second if first is None else first
    return first & second


def split_tiles(cols, rows, unit=WIDTH, array=0, start=0):
    half = rows // 2
    count = cols // (3 * unit)
    out = [
        Tiles(array, "zxy", 0, half, 0, 3 * unit, unit, count, start),
        Tiles(array, "zyx", half, half, 0, 3 * unit, unit, count, start),
        Tiles(array, "xzy", 0, half, unit, 3 * unit, 2 * unit, count, start),
        Tiles(array, "yzx", half, half, unit, 3 * unit, 2 * unit, count, start),
    ]
    rest = cols - 3 * unit * count
    if rest:
        out.append(Tiles(array, "xzy", 0, half, cols - rest, rest, rest, 1, start))
        out.append(Tiles(array, "yzx", half, half, cols - rest, rest, rest, 1, start))
    return out


def window(tile, group):
    start = tile.col + group * tile.stride
    if not isinstance(start, int):
        start = pl.multiple_of(start, 128)
    return pl.ds(tile.row, tile.rows), pl.ds(start, tile.cols)


def steps_of(tiles):
    return max(tile.start + tile.count for tile in tiles) + LAGS - 1


def first_slots(tiles):
    return [sum(tile.count for tile in tiles[:i]) for i in range(len(tiles))]


class Gather:
    def __init__(self, tiles, shards, fulls, sems):
        self.tiles, self.shards, self.fulls = tiles, shards, fulls
        self.send_sem, self.recv_sem, self.core_send, self.core_recv, self.own_sem = sems
        self.at = position()
        self.steps = steps_of(tiles)

    @staticmethod
    def sems(tiles, arrays):
        slots = sum(tile.count for tile in tiles)
        return [
            pltpu.SemaphoreType.DMA((len(tiles), 2, len(LINKS), 16)),
            pltpu.SemaphoreType.DMA((slots, 16)),
            pltpu.SemaphoreType.DMA((slots,)),
            pltpu.SemaphoreType.DMA((slots,)),
            pltpu.SemaphoreType.DMA((arrays,)),
        ]

    def begin(self):
        at = self.at
        copies = [
            pltpu.make_async_copy(
                shard, full.at[at["y"], at["z"], at["x"], at["c"]], self.own_sem.at[i]
            )
            for i, (shard, full) in enumerate(zip(self.shards, self.fulls))
        ]
        for copy in copies:
            copy.start()
        greet_all(at)
        for copy in copies:
            copy.wait()

    def copy(self, index, group, slot, src, link, own):
        tile = self.tiles[index]
        rows, cols = window(tile, group)
        full = self.fulls[tile.array].at[src["y"], src["z"], src["x"], src["c"], rows, cols]
        return remote(
            self.shards[tile.array].at[rows, cols] if own else full,
            full,
            self.send_sem.at[index, group % 2, LINKS.index(link), block_id(src)],
            self.recv_sem.at[slot, block_id(src)],
            across(self.at, link),
        )

    def visit(self, index, group, slot, lag):
        at, tile = self.at, self.tiles[index]
        for off in offsets(lag) if lag <= DEPTH else ():
            src = moved(at, off)

            def handle():
                if lag:
                    self.copy(index, group, slot, src, LINKS[-1], False).wait_recv()
                for link in onward(tile.order, off):

                    def send():
                        one = self.copy(index, group, slot, src, link, lag == 0)
                        pl.when(group >= 2)(one.wait_send)
                        one.start()

                    when(inside(at["z"] + link[1]) if link[0] == "z" else None, send)

            when(inside(src["z"]) if off[0] else None, handle)
        if lag >= DEPTH:
            rows, cols = window(tile, group)
            part = self.fulls[tile.array].at[:, :, :, at["c"], rows, cols]
            pair = remote(
                part, part, self.core_send.at[slot], self.core_recv.at[slot], across(at, ("c", 0))
            )
            pair.start() if lag == DEPTH else pair.wait()

    def step(self, step):
        for lag in range(LAGS):
            for index, (tile, first) in enumerate(zip(self.tiles, first_slots(self.tiles))):
                group = step - lag - tile.start
                pl.when((group >= 0) & (group < tile.count))(
                    functools.partial(self.visit, index, group, first + group, lag)
                )

    def finish(self):
        for index, tile in enumerate(self.tiles):
            for group in range(max(0, tile.count - 2), tile.count):
                for off in [off for lag in range(DEPTH + 1) for off in offsets(lag)]:
                    src = moved(self.at, off)
                    here = inside(src["z"]) if off[0] else None
                    for link in onward(tile.order, off):
                        there = inside(self.at["z"] + link[1]) if link[0] == "z" else None
                        one = self.copy(index, group, 0, src, link, False)
                        when(both(here, there), one.wait_send)


class Scatter:
    def __init__(self, tiles, grads, put, boxes, sems):
        self.tiles, self.grads, self.put = tiles, grads, put
        count = len(tiles)
        self.sums, self.pairs, self.inbox = boxes[:count], boxes[count : 2 * count], boxes[2 * count :]
        self.send_sem, self.recv_sem, self.core_send, self.core_recv, self.own_sem = sems
        self.at = position()
        self.steps = steps_of(tiles)

    @staticmethod
    def boxes(tiles, dtypes):
        whole, part = [], []
        for tile in tiles:
            dtype = dtypes[tile.array]
            whole.append(
                pltpu.VMEM((tile.count, 2) + GRID[:2] + (tile.rows, tile.cols), dtype)
            )
            part.append(pltpu.VMEM((tile.count, len(LINKS), 8, tile.rows, tile.cols), dtype))
        return whole + whole + part

    @staticmethod
    def sems(tiles):
        slots = sum(tile.count for tile in tiles)
        return [
            pltpu.SemaphoreType.DMA((len(tiles), 2, 16)),
            pltpu.SemaphoreType.DMA((slots, len(LINKS), 8)),
            pltpu.SemaphoreType.DMA((slots,)),
            pltpu.SemaphoreType.DMA((slots,)),
            pltpu.SemaphoreType.DMA((slots,)),
        ]

    def begin(self):
        greet_all(self.at)

    def copy(self, index, group, slot, dest, link, label):
        tile = self.tiles[index]
        box = inbox_id(tile.order, label, dest)
        return remote(
            self.sums[index].at[group, dest["y"], dest["z"], dest["x"]],
            self.inbox[index].at[group, LINKS.index(label), box],
            self.send_sem.at[index, group % 2, block_id(dest)],
            self.recv_sem.at[slot, LINKS.index(label), box],
            across(self.at, link),
        )

    def visit(self, index, group, slot, stage):
        at, tile = self.at, self.tiles[index]
        rows, cols = window(tile, group)
        grad, sums = self.grads[tile.array], self.sums[index]
        if stage <= 1:
            pair = remote(
                grad.at[:, :, :, 1 - at["c"], rows, cols],
                self.pairs[index].at[group],
                self.core_send.at[slot],
                self.core_recv.at[slot],
                across(at, ("c", 0)),
            )
            own = pltpu.make_async_copy(
                grad.at[:, :, :, at["c"], rows, cols], sums.at[group], self.own_sem.at[slot]
            )
        if stage == 0:
            pair.start()
            own.start()
            return
        if stage == 1:
            own.wait()
            pair.wait()
            sums[group] = (
                sums[group].astype(F32) + self.pairs[index][group].astype(F32)
            ).astype(sums.dtype)
        lag = DEPTH + 1 - stage
        for off in offsets(lag):
            dest = moved(at, off)

            def handle():
                spot = (group, dest["y"], dest["z"], dest["x"])

                def add(links):
                    total = sums[spot].astype(F32)
                    for link in links:
                        self.copy(index, group, slot, dest, link, link).wait_recv()
                        box = inbox_id(tile.order, link, dest)
                        total = total + self.inbox[index][group, LINKS.index(link), box].astype(F32)
                    return total

                fixed = [link for link in onward(tile.order, off) if link[0] != "z"]
                for link in onward(tile.order, off):
                    if link[0] == "z":

                        @pl.when(inside(at["z"] + link[1]))
                        def _():
                            sums[spot] = add([link]).astype(sums.dtype)

                if lag == 0:
                    self.put(tile, group, add(fixed))
                    return
                if fixed:
                    sums[spot] = add(fixed).astype(sums.dtype)
                link = backward_link(tile.order, off)
                one = self.copy(index, group, slot, dest, link, (link[0], -link[1]))
                pl.when(group >= 2)(one.wait_send)
                one.start()

            when(inside(dest["z"]) if off[0] else None, handle)

    def step(self, step):
        for stage in range(LAGS):
            for index, (tile, first) in enumerate(zip(self.tiles, first_slots(self.tiles))):
                group = step - stage - tile.start
                pl.when((group >= 0) & (group < tile.count))(
                    functools.partial(self.visit, index, group, first + group, stage)
                )

    def finish(self):
        for index, tile in enumerate(self.tiles):
            for group in range(max(0, tile.count - 2), tile.count):
                for off in [off for lag in range(1, DEPTH + 1) for off in offsets(lag)]:
                    dest = moved(self.at, off)
                    link = backward_link(tile.order, off)
                    one = self.copy(index, group, 0, dest, link, (link[0], -link[1]))
                    when(inside(dest["z"]) if off[0] else None, one.wait_send)


def run_all(moves):
    moves.begin()
    lax.fori_loop(0, moves.steps, lambda step, _: (moves.step(step), 0)[1], 0)
    moves.finish()


def gather_kernel(tiles, arrays, *refs):
    run_all(Gather(tiles, refs[:arrays], refs[arrays : 2 * arrays], refs[2 * arrays :]))


def gather(shards, tiles, ident):
    halves = lax.axis_size("tensor")
    if not on_grid():
        return [
            lax.all_gather(shard, ("tensor", "dp"), axis=0, tiled=False).reshape(
                (halves, -1) + shard.shape[1:]
            )
            for shard in shards
        ]
    hbm = pl.BlockSpec(memory_space=pl.ANY)
    arrays = len(shards)
    fulls = pl.pallas_call(
        functools.partial(gather_kernel, tiles, arrays),
        in_specs=[hbm] * arrays,
        out_specs=[hbm] * arrays,
        out_shape=[
            jax.ShapeDtypeStruct((halves,) + GRID + shard.shape, shard.dtype) for shard in shards
        ],
        scratch_shapes=Gather.sems(tiles, arrays),
        compiler_params=pltpu.CompilerParams(collective_id=ident, has_side_effects=True),
        name="gather",
    )(*shards)
    return [full.reshape(halves, -1, full.shape[-1]) for full in fulls]


def scatter_kernel(tiles, groups, *refs):
    boxes = 3 * len(tiles)
    grads, outs, rest = refs[:3], refs[3:11], refs[11:]
    gate, upper, down, out, query, key, value, small = outs

    def put(tile, group, total):
        rows = pl.ds(tile.row, tile.rows)
        if tile.array == 2:
            small[...] = total
            return
        if tile.count == 1 and tile.array == 0:
            out[rows, 3 * WIDTH :] = total
            return
        thirds = (gate, upper, down) if tile.array == 0 else (query, key, value)
        offset = tile.col // WIDTH
        width = tile.cols // WIDTH

        def inner():
            lanes = pl.ds(pl.multiple_of(group * WIDTH, WIDTH), WIDTH)
            for i in range(width):
                thirds[offset + i][rows, lanes] = total[:, i * WIDTH : (i + 1) * WIDTH]

        if tile.array == 1:
            inner()
            return
        pl.when(group < groups)(inner)

        @pl.when(group == groups)
        def _():
            out[rows, tile.col : tile.col + tile.cols] = total

    run_all(Scatter(tiles, grads, put, rest[:boxes], rest[boxes:]))


def scatter(second, first, small, ident):
    halves = lax.axis_size("tensor")
    parts = lax.axis_size("dp")
    rows = second.shape[1] // parts
    groups = second.shape[2] // (3 * WIDTH) - 1
    half_cols = second.shape[2] - groups * 3 * WIDTH
    if not on_grid():
        second, first, small = (
            lax.psum_scatter(
                grad.reshape(-1, grad.shape[-1]), ("tensor", "dp"), scatter_dimension=0, tiled=True
            ).astype(F32)
            for grad in (second, first, small)
        )
        return (
            thirds_of(second[:, : groups * 3 * WIDTH])
            + (second[:, groups * 3 * WIDTH :],)
            + thirds_of(first)
            + (small,)
        )
    grads = [grad.reshape((2,) + GRID + (-1, grad.shape[-1])) for grad in (second, first, small)]
    tiles = split_tiles(second.shape[2], rows)
    tiles += split_tiles(first.shape[2], rows, array=1, start=tiles[0].count)
    small_rows = grads[2].shape[-2]
    tiles.append(Tiles(2, "zxy", 0, small_rows, 0, WIDTH, WIDTH, 1, 0))
    hbm = pl.BlockSpec(memory_space=pl.ANY)
    shapes = [(rows, groups * WIDTH)] * 3 + [(rows, half_cols)]
    shapes += [(rows, first.shape[2] // 3)] * 3 + [(small_rows, WIDTH)]
    return pl.pallas_call(
        functools.partial(scatter_kernel, tiles, groups),
        in_specs=[hbm] * 3,
        out_specs=[pl.BlockSpec(memory_space=pltpu.VMEM)] * len(shapes),
        out_shape=[jax.ShapeDtypeStruct(shape, F32) for shape in shapes],
        scratch_shapes=Scatter.boxes(tiles, [grad.dtype for grad in grads]) + Scatter.sems(tiles),
        compiler_params=pltpu.CompilerParams(
            collective_id=ident, has_side_effects=True, vmem_limit_bytes=VMEM_LIMIT
        ),
        name="scatter",
    )(*grads)


def contract(left, right, dim_left, dim_right):
    return lax.dot_general(
        left.astype(BF16),
        right.astype(BF16),
        (((dim_left,), (dim_right,)), ((), ())),
        preferred_element_type=F32,
    )


def mm(left, right):
    return contract(left, right, 1, 0)


def mm_t(left, right):
    return contract(left, right, 1, 1)


def t_mm(left, right):
    return contract(left, right, 0, 0)


def tri_inverses(systems):
    rows = lax.broadcasted_iota(jnp.int32, (CHUNK, CHUNK), 0)
    cols = lax.broadcasted_iota(jnp.int32, (CHUNK, CHUNK), 1)
    inverses = None
    size = 1
    while size < CHUNK:
        link = (
            (rows // (2 * size) == cols // (2 * size))
            & ((rows // size) % 2 == 1)
            & ((cols // size) % 2 == 0)
        )
        parts = [jnp.where(link, system, 0.0) for system in systems]
        if size == 1:
            eye = (rows == cols).astype(F32)
            inverses = [eye - part for part in parts]
        else:
            lows = [inverse.astype(BF16) for inverse in inverses]
            middles = [mm(part, low) for part, low in zip(parts, lows)]
            inverses = [
                inverse - mm(low, middle)
                for inverse, low, middle in zip(inverses, lows, middles)
            ]
        size *= 2
    return inverses


def conv_of(lin_ref, base, lanes, taps, row, keeps, tokens):
    total = lin_ref[0, base : base + tokens, lanes] * taps[row : row + 1]
    for off in range(1, TAPS):
        total = total + taps[row + off : row + off + 1] * (
            lin_ref[0, base - off : base - off + tokens, lanes] * keeps[off]
        )
    return total


def third(sub, index):
    first = (sub * 3 + index) * WIDTH
    return slice(first, first + WIDTH)


def head_column(aux, lane):
    lanes = lax.broadcasted_iota(jnp.int32, aux.shape, 1)
    return jnp.sum(jnp.where(lanes == lane, aux, 0.0), axis=1, keepdims=True)


def greet(partner):
    barrier = pltpu.get_barrier_semaphore()
    pl.semaphore_signal(
        barrier, inc=1, device_id={"tensor": partner}, device_id_type=MESH
    )
    pl.semaphore_wait(barrier, 1)


def chunk_masks(aux, seg_row, at):
    rows = lax.broadcasted_iota(jnp.int32, (CHUNK, CHUNK), 0)
    cols = lax.broadcasted_iota(jnp.int32, (CHUNK, CHUNK), 1)
    same = aux[at : at + CHUNK, 0:1] == seg_row[0:1, at : at + CHUNK]
    return same & (rows > cols), same & (rows >= cols)


def mixer_fwd_kernel(
    tokens, lin_ref, aux_ref, seg_ref, taps_ref, gain_ref,
    onb_ref, o_ref, n_ref, t_ref, s_ref,
    state, outbox, inbox, send_sem, recv_sem,
):
    step = pl.program_id(0)
    mine = lax.axis_index("tensor")
    chunks = tokens // CHUNK

    @pl.when(step == 0)
    def _():
        greet(1 - mine)

    def hand_over(head):
        return pltpu.make_async_remote_copy(
            src_ref=outbox.at[head],
            dst_ref=inbox.at[head],
            send_sem=send_sem.at[head],
            recv_sem=recv_sem.at[head],
            device_id={"tensor": 1 - mine},
            device_id_type=MESH,
        )

    aux = aux_ref[...]
    seg_row = seg_ref[...]
    keeps = [None] + [aux[:, 2 + off : 3 + off] for off in range(1, TAPS)]
    heads = []
    for sub in range(PAIR):
        lanes = slice(sub * WIDTH, (sub + 1) * WIDTH)
        taps = taps_ref[:, lanes]
        beta = head_column(aux, 16 + step * PAIR + sub)
        acts = []
        for index in range(3):
            mixed = conv_of(lin_ref, HALO, third(sub, index), taps, index * TAPS, keeps, tokens)
            acts.append(mixed * jax.nn.sigmoid(mixed))
        q = acts[0] * (
            lax.rsqrt(jnp.sum(acts[0] * acts[0], -1, keepdims=True) + 1e-06) * WIDTH ** (-0.5)
        )
        k = acts[1] * lax.rsqrt(jnp.sum(acts[1] * acts[1], -1, keepdims=True) + 1e-06)
        heads.append((q, k, acts[2], beta))
    spots = [(sub, c) for sub in range(PAIR) for c in range(chunks)]
    masks = [chunk_masks(aux, seg_row, c * CHUNK) for c in range(chunks)]

    def cut(values, c):
        return values[c * CHUNK : (c + 1) * CHUNK]

    lows = [(q.astype(BF16), k.astype(BF16)) for q, k, _, _ in heads]
    systems = [
        jnp.where(
            masks[c][0],
            cut(heads[sub][3], c) * mm_t(cut(lows[sub][1], c), cut(lows[sub][1], c)),
            0.0,
        )
        for sub, c in spots
    ]
    scores_of = [
        jnp.where(masks[c][1], mm_t(cut(lows[sub][0], c), cut(lows[sub][1], c)), 0.0).astype(BF16)
        for sub, c in spots
    ]
    inner = []
    for (sub, c), inverse, scores in zip(spots, tri_inverses(systems), scores_of):
        inverse = inverse.astype(BF16)
        t_ref[sub, c] = inverse
        inner.append((inverse, scores))

    @pl.when(mine == 0)
    def _():
        state[...] = jnp.zeros_like(state)

    @pl.when(mine == 1)
    def _():
        for sub in range(PAIR):
            head = step * PAIR + sub
            hand_over(head).wait_recv()
            state[sub] = inbox[head]

    carried = [state[sub] for sub in range(PAIR)]
    for c in range(chunks):
        at = c * CHUNK
        first = aux[at : at + CHUNK, 1:2]
        last = aux[at : at + CHUNK, 2:3]
        keep = aux[at + CHUNK - 1 : at + CHUNK, 1:2]
        subs = range(PAIR)
        befores = [carried[sub].astype(BF16) for sub in subs]
        reads = [
            mm(jnp.concatenate([cut(lows[sub][1], c), cut(lows[sub][0], c)], 0), befores[sub])
            for sub in subs
        ]
        news = [
            mm(
                inner[sub * chunks + c][0],
                cut(heads[sub][3], c) * (cut(heads[sub][2], c) - first * reads[sub][:CHUNK]),
            ).astype(BF16)
            for sub in subs
        ]
        carried = [
            keep * carried[sub] + t_mm(last * cut(heads[sub][1], c), news[sub]) for sub in subs
        ]
        outs = [
            first * reads[sub][CHUNK:] + mm(inner[sub * chunks + c][1], news[sub]) for sub in subs
        ]
        for sub in subs:
            s_ref[sub, c] = befores[sub]
            n_ref[sub, c] = news[sub]
            lanes = slice(sub * WIDTH, (sub + 1) * WIDTH)
            out = outs[sub]
            o_ref[0, at : at + CHUNK, lanes] = out
            scale = lax.rsqrt(jnp.mean(out * out, -1, keepdims=True) + 1e-05)
            onb_ref[0, at : at + CHUNK, lanes] = (out * scale * gain_ref[0:1]).astype(BF16)

    @pl.when(mine == 0)
    def _():
        for sub in range(PAIR):
            head = step * PAIR + sub
            outbox[head] = carried[sub]
            hand_over(head).start()

    @pl.when((step == pl.num_programs(0) - 1) & (mine == 0))
    def _():
        for head in range(outbox.shape[0]):
            hand_over(head).wait_send()


def mixer_bwd_kernel(
    tokens, lin_ref, aux_ref, seg_ref, taps_ref, gain_ref,
    o_ref, n_ref, t_ref, s_ref, donb_ref,
    dlin_ref, dbl_ref, dtaps_ref, dgain_ref,
    state, extended, outbox, inbox, tailbox, headbox, send_sem, recv_sem, tail_send, tail_recv,
):
    step = pl.program_id(0)
    mine = lax.axis_index("tensor")
    chunks = tokens // CHUNK

    @pl.when(step == 0)
    def _():
        greet(1 - mine)
        dbl_ref[...] = jnp.zeros_like(dbl_ref)
        dgain_ref[...] = jnp.zeros_like(dgain_ref)

    def hand_over(head):
        return pltpu.make_async_remote_copy(
            src_ref=outbox.at[head],
            dst_ref=inbox.at[head],
            send_sem=send_sem.at[head],
            recv_sem=recv_sem.at[head],
            device_id={"tensor": 1 - mine},
            device_id_type=MESH,
        )

    def hand_tail(head):
        return pltpu.make_async_remote_copy(
            src_ref=tailbox.at[head],
            dst_ref=headbox.at[head],
            send_sem=tail_send.at[head],
            recv_sem=tail_recv.at[head],
            device_id={"tensor": 1 - mine},
            device_id_type=MESH,
        )

    aux = aux_ref[...]
    seg_row = seg_ref[...]
    keeps = [None] + [aux[:tokens, 2 + off : 3 + off] for off in range(1, TAPS)]
    heads, inner = [], []
    for sub in range(PAIR):
        lanes = slice(sub * WIDTH, (sub + 1) * WIDTH)
        taps = taps_ref[:, lanes]
        beta = head_column(aux[:tokens], 16 + step * PAIR + sub)
        mixes, sigs, acts = [], [], []
        for index in range(3):
            mixed = conv_of(lin_ref, HALO, third(sub, index), taps, index * TAPS, keeps, tokens)
            mixes.append(mixed)
            sigs.append(jax.nn.sigmoid(mixed))
            acts.append(mixed * sigs[-1])
        rho_q = lax.rsqrt(jnp.sum(acts[0] * acts[0], -1, keepdims=True) + 1e-06)
        rho_k = lax.rsqrt(jnp.sum(acts[1] * acts[1], -1, keepdims=True) + 1e-06)
        q = acts[0] * (rho_q * WIDTH ** (-0.5))
        k = acts[1] * rho_k
        out = o_ref[0, :, lanes]
        don = donb_ref[0, :, lanes]
        scale = lax.rsqrt(jnp.mean(out * out, -1, keepdims=True) + 1e-05)
        dgain_ref[0:1] += jnp.sum(don * out * scale, 0, keepdims=True)
        du = don * gain_ref[0:1]
        dout = scale * du - out * (scale * scale * scale) * jnp.mean(
            out * du, -1, keepdims=True
        )
        heads.append((q, k, acts, beta, mixes, sigs, rho_q, rho_k, dout))
    spots = [(sub, c) for sub in range(PAIR) for c in range(chunks)]
    masks = [chunk_masks(aux, seg_row, c * CHUNK) for c in range(chunks)]
    firsts = [aux[c * CHUNK : (c + 1) * CHUNK, 1:2] for c in range(chunks)]

    def cut(values, c):
        return values[c * CHUNK : (c + 1) * CHUNK]

    lows = [
        (q.astype(BF16), k.astype(BF16), dout.astype(BF16))
        for q, k, _, _, _, _, _, _, dout in heads
    ]
    grams = [
        mm_t(jnp.concatenate([cut(lows[s][1], c), cut(lows[s][0], c)], 0), cut(lows[s][1], c))
        for s, c in spots
    ]
    turned = [
        mm_t(cut(lows[s][2], c), jnp.concatenate([n_ref[s, c], s_ref[s, c]], 0)) for s, c in spots
    ]
    scores_of = [
        jnp.where(masks[c][1], gram[CHUNK:], 0.0).astype(BF16)
        for (s, c), gram in zip(spots, grams)
    ]
    dscores_of = [
        jnp.where(masks[c][1], turn[:, :CHUNK], 0.0).astype(BF16)
        for (s, c), turn in zip(spots, turned)
    ]
    reads = [mm(cut(lows[s][1], c), s_ref[s, c]) for s, c in spots]
    pulls = [t_mm(scores, cut(lows[s][2], c)) for (s, c), scores in zip(spots, scores_of)]
    reaches = [
        t_mm(firsts[c] * cut(heads[s][0], c), cut(lows[s][2], c)) for s, c in spots
    ]
    dqs = [
        firsts[c] * turn[:, CHUNK:] + mm(dscores, cut(lows[s][1], c))
        for (s, c), turn, dscores in zip(spots, turned, dscores_of)
    ]
    dks = [t_mm(dscores, cut(lows[s][0], c)) for (s, c), dscores in zip(spots, dscores_of)]
    gaps = [
        cut(heads[s][2][2], c) - firsts[c] * read for (s, c), read in zip(spots, reads)
    ]
    inner = [
        (gram[:CHUNK], masks[c][0], pull, reach, dq, dk, gap)
        for (s, c), gram, pull, reach, dq, dk, gap in zip(
            spots, grams, pulls, reaches, dqs, dks, gaps
        )
    ]

    @pl.when(mine == 1)
    def _():
        state[...] = jnp.zeros_like(state)

    @pl.when(mine == 0)
    def _():
        for sub in range(PAIR):
            head = step * PAIR + sub
            hand_over(head).wait_recv()
            state[sub] = inbox[head]

    carried = [state[sub] for sub in range(PAIR)]
    pieces = [[None] * chunks for _ in range(PAIR)]
    for c in reversed(range(chunks)):
        at = c * CHUNK
        first = aux[at : at + CHUNK, 1:2]
        last = aux[at : at + CHUNK, 2:3]
        keep = aux[at + CHUNK - 1 : at + CHUNK, 1:2]
        subs = range(PAIR)
        parts = [inner[sub * chunks + c] for sub in subs]
        betas = [cut(heads[sub][3], c) for sub in subs]
        afters = [carried[sub].astype(BF16) for sub in subs]
        dnews = [
            parts[sub][2] + mm(last * cut(heads[sub][1], c), afters[sub]) for sub in subs
        ]
        backs = [t_mm(t_ref[sub, c], dnews[sub]) for sub in subs]
        dvs = [betas[sub] * backs[sub] for sub in subs]
        dreads = [(-(first * dvs[sub])).astype(BF16) for sub in subs]
        carried = [
            keep * carried[sub] + parts[sub][3] + t_mm(cut(lows[sub][1], c), dreads[sub])
            for sub in subs
        ]
        for sub in subs:
            kk, strict, _, _, dq, dk, gap = parts[sub]
            before, new = s_ref[sub, c], n_ref[sub, c]
            kc = cut(lows[sub][1], c)
            back = backs[sub]
            dsystem = jnp.where(strict, -mm_t(back, new), 0.0)
            dbeta = jnp.sum(back * gap + dsystem * kk, -1, keepdims=True)
            grow = (betas[sub] * dsystem).astype(BF16)
            dk = (
                dk
                + last * mm_t(new, afters[sub])
                + mm_t(dreads[sub], before)
                + mm(grow, kc)
                + t_mm(grow, kc)
            )
            pieces[sub][c] = (dq, dk, dvs[sub], dbeta)

    @pl.when(mine == 1)
    def _():
        for sub in range(PAIR):
            head = step * PAIR + sub
            outbox[head] = carried[sub]
            hand_over(head).start()

    lane_ids = lax.broadcasted_iota(jnp.int32, (tokens, WIDTH), 1)
    for sub in range(PAIR):
        head = step * PAIR + sub
        q, k, acts, beta, mixes, sigs, rho_q, rho_k, dout = heads[sub]
        dq, dk, dv, dbeta = (
            jnp.concatenate([pieces[sub][c][item] for c in range(chunks)], 0)
            for item in range(4)
        )
        dbl_ref[...] += jnp.where(lane_ids == head, dbeta * beta * (1.0 - beta), 0.0)
        dq = dq * WIDTH ** (-0.5)
        dacts = (
            rho_q * dq
            - acts[0] * (rho_q * rho_q * rho_q) * jnp.sum(acts[0] * dq, -1, keepdims=True),
            rho_k * dk
            - acts[1] * (rho_k * rho_k * rho_k) * jnp.sum(acts[1] * dk, -1, keepdims=True),
            dv,
        )
        for index in range(3):
            sig = sigs[index]
            dmix = dacts[index] * sig * (1.0 + mixes[index] * (1.0 - sig))
            extended[sub, index, 0:tokens] = dmix
            tailbox[head, index] = dmix[0:8]

    @pl.when(mine == 1)
    def _():
        extended[:, :, tokens : tokens + 8] = jnp.zeros((PAIR, 3, 8, WIDTH), F32)
        for sub in range(PAIR):
            hand_tail(step * PAIR + sub).start()

    @pl.when(mine == 0)
    def _():
        for sub in range(PAIR):
            head = step * PAIR + sub
            hand_tail(head).wait_recv()
            extended[sub, :, tokens : tokens + 8] = headbox[head]

    later = [None] + [aux[:, 5 + off : 6 + off] for off in range(1, TAPS)]
    for sub in range(PAIR):
        lanes = slice(sub * WIDTH, (sub + 1) * WIDTH)
        taps = taps_ref[:, lanes]
        for index in range(3):
            row = index * TAPS
            dmix = extended[sub, index, 0:tokens]
            dlin = dmix * taps[row : row + 1]
            dtaps_ref[row : row + 1, lanes] = jnp.sum(
                dmix * lin_ref[0, HALO : HALO + tokens, third(sub, index)], 0, keepdims=True
            )
            for off in range(1, TAPS):
                dlin = dlin + taps[row + off : row + off + 1] * (
                    extended[sub, index, off : off + tokens] * later[off]
                )
                dtaps_ref[row + off : row + off + 1, lanes] = jnp.sum(
                    dmix
                    * keeps[off]
                    * lin_ref[0, HALO - off : HALO - off + tokens, third(sub, index)],
                    0,
                    keepdims=True,
                )
            dlin_ref[0, :, third(sub, index)] = dlin.astype(BF16)
        dtaps_ref[12:16, lanes] = jnp.zeros((4, WIDTH), F32)

    @pl.when((step == pl.num_programs(0) - 1) & (mine == 1))
    def _():
        for head in range(outbox.shape[0]):
            hand_over(head).wait_send()
            hand_tail(head).wait_send()


def mixer_fwd(linear, aux, seg_row, taps, gain):
    halves, rows, cols = linear.shape
    tokens = rows - HALO
    half_heads = cols // 3 // WIDTH
    heads = halves * half_heads
    per_half = half_heads // PAIR
    chunks = tokens // CHUNK
    lanes = PAIR * WIDTH

    def whole(shape):
        return pl.BlockSpec(shape, lambda i: (0,) * len(shape))

    token_spec = pl.BlockSpec((1, tokens, lanes), lambda i: (i // per_half, 0, i % per_half))
    square = pl.BlockSpec((PAIR, chunks, CHUNK, WIDTH), lambda i: (i, 0, 0, 0))
    square_shape = jax.ShapeDtypeStruct((heads, chunks, CHUNK, WIDTH), BF16)
    return pl.pallas_call(
        functools.partial(mixer_fwd_kernel, tokens),
        grid=(heads // PAIR,),
        in_specs=[
            pl.BlockSpec((1, rows, 3 * lanes), lambda i: (i // per_half, 0, i % per_half)),
            whole(aux.shape),
            whole(seg_row.shape),
            pl.BlockSpec((16, lanes), lambda i: (0, i)),
            whole(gain.shape),
        ],
        out_specs=[token_spec, token_spec, square, square, square],
        out_shape=[
            jax.ShapeDtypeStruct((halves, tokens, half_heads * WIDTH), BF16),
            jax.ShapeDtypeStruct((halves, tokens, half_heads * WIDTH), F32),
            square_shape,
            square_shape,
            square_shape,
        ],
        scratch_shapes=[
            pltpu.VMEM((PAIR, WIDTH, WIDTH), F32),
            pltpu.VMEM((heads, WIDTH, WIDTH), F32),
            pltpu.VMEM((heads, WIDTH, WIDTH), F32),
            pltpu.SemaphoreType.DMA((heads,)),
            pltpu.SemaphoreType.DMA((heads,)),
        ],
        compiler_params=pltpu.CompilerParams(
            collective_id=0, has_side_effects=True, vmem_limit_bytes=VMEM_LIMIT
        ),
        name="mixer_fwd",
    )(linear, aux, seg_row, taps, gain)


def mixer_bwd(linear, aux, seg_row, taps, gain, out, new, inverse, before, donb):
    halves, rows, cols = linear.shape
    tokens = rows - HALO
    half_heads = cols // 3 // WIDTH
    heads = halves * half_heads
    per_half = half_heads // PAIR
    chunks = tokens // CHUNK
    lanes = PAIR * WIDTH

    def whole(shape):
        return pl.BlockSpec(shape, lambda i: (0,) * len(shape))

    token_spec = pl.BlockSpec((1, tokens, lanes), lambda i: (i // per_half, 0, i % per_half))
    square = pl.BlockSpec((PAIR, chunks, CHUNK, WIDTH), lambda i: (i, 0, 0, 0))
    taps_spec = pl.BlockSpec((16, lanes), lambda i: (0, i))
    return pl.pallas_call(
        functools.partial(mixer_bwd_kernel, tokens),
        grid=(heads // PAIR,),
        in_specs=[
            pl.BlockSpec((1, rows, 3 * lanes), lambda i: (i // per_half, 0, i % per_half)),
            whole(aux.shape),
            whole(seg_row.shape),
            taps_spec,
            whole(gain.shape),
            token_spec,
            square,
            square,
            square,
            token_spec,
        ],
        out_specs=[
            pl.BlockSpec((1, tokens, 3 * lanes), lambda i: (i // per_half, 0, i % per_half)),
            whole((tokens, WIDTH)),
            taps_spec,
            whole((8, WIDTH)),
        ],
        out_shape=[
            jax.ShapeDtypeStruct((halves, tokens, cols), BF16),
            jax.ShapeDtypeStruct((tokens, WIDTH), F32),
            jax.ShapeDtypeStruct((16, heads * WIDTH), F32),
            jax.ShapeDtypeStruct((8, WIDTH), F32),
        ],
        scratch_shapes=[
            pltpu.VMEM((PAIR, WIDTH, WIDTH), F32),
            pltpu.VMEM((PAIR, 3, tokens + 8, WIDTH), F32),
            pltpu.VMEM((heads, WIDTH, WIDTH), F32),
            pltpu.VMEM((heads, WIDTH, WIDTH), F32),
            pltpu.VMEM((heads, 3, 8, WIDTH), F32),
            pltpu.VMEM((heads, 3, 8, WIDTH), F32),
            pltpu.SemaphoreType.DMA((heads,)),
            pltpu.SemaphoreType.DMA((heads,)),
            pltpu.SemaphoreType.DMA((heads,)),
            pltpu.SemaphoreType.DMA((heads,)),
        ],
        compiler_params=pltpu.CompilerParams(
            collective_id=1, has_side_effects=True, vmem_limit_bytes=VMEM_LIMIT
        ),
        name="mixer_bwd",
    )(linear, aux, seg_row, taps, gain, out, new, inverse, before, donb)


def mlp_kernel(
    count, inputs_ref, onb_ref, weight_ref, *refs,
):
    wo_refs, refs = refs[:4], refs[4:]
    gain_ref, mask_ref, teacher_ref, cot_ref, coef_ref = refs[:5]
    out_ref, square_ref, early_ref, grad_ref, donb_ref, dhidden_ref, dgain_ref = refs[5:12]
    hidden, normed, normed_t, total, dtotal, dmlp, dmlp_t, gates, uppers, inners = refs[12:]
    step = pl.program_id(0)
    unit = WIDTH

    def out_weight(half):
        return jnp.concatenate([ref[half] for ref in wo_refs], 1)

    def rho_of(values):
        return lax.rsqrt(jnp.mean(values * values, -1, keepdims=True) + 1e-05)

    def spans(first, parts):
        return [weight_ref[half, :, (first + part) * unit : (first + part + 1) * unit]
                for half in range(2) for part in range(parts)]

    @pl.when(step == 0)
    def _():
        rows = inputs_ref[...].astype(F32)
        for half in range(2):
            rows = rows + mm_t(onb_ref[half], out_weight(half))
        hidden[...] = rows
        xn = rows * rho_of(rows) * gain_ref[0:1]
        normed[...] = xn.astype(BF16)
        normed_t[...] = xn.T.astype(BF16)
        total[...] = jnp.zeros_like(total)

    @pl.when(step < count)
    def _():
        both_w = jnp.concatenate(spans(0, 2), 1)
        gu = mm(normed[...], both_w)
        gate = jnp.concatenate([gu[:, 0:unit], gu[:, 2 * unit : 3 * unit]], 1)
        upper = jnp.concatenate([gu[:, unit : 2 * unit], gu[:, 3 * unit :]], 1)
        gates[step] = gate
        uppers[step] = upper
        inner = (gate * jax.nn.sigmoid(gate) * upper).astype(BF16)
        inners[step] = inner
        total[...] += mm_t(inner, jnp.concatenate(spans(2, 1), 1))

    @pl.when(step == count - 1)
    def _():
        rows = hidden[...] + total[...]
        out_ref[...] = rows.astype(BF16)
        differ = rows - teacher_ref[...].astype(F32)
        masked = mask_ref[...] * differ
        square_ref[...] = jnp.sum(
            (masked * differ).reshape(-1, 8, rows.shape[1]), 0
        )
        dout = cot_ref[...].astype(F32) + masked * coef_ref[0:1, 0:1]
        dhidden_ref[...] = dout
        dmlp[...] = dout.astype(BF16)
        dmlp_t[...] = dout.T.astype(BF16)
        dtotal[...] = jnp.zeros_like(dtotal)

    @pl.when((step >= count) & (step < 2 * count))
    def _():
        tile = step - count
        dinner = mm(dmlp[...], jnp.concatenate(spans(2, 1), 1))
        gate, upper = gates[tile], uppers[tile]
        sig = jax.nn.sigmoid(gate)
        dgate = (dinner * upper * sig * (1.0 + gate * (1.0 - sig))).astype(BF16)
        dupper = (dinner * (gate * sig)).astype(BF16)
        dgu = jnp.concatenate(
            [dgate[:, :unit], dupper[:, :unit], dgate[:, unit:], dupper[:, unit:]], 1
        )
        dtotal[...] += mm_t(dgu, jnp.concatenate(spans(0, 2), 1))
        grown = mm(normed_t[...], dgu).astype(BF16)
        down = mm(dmlp_t[...], inners[tile]).astype(BF16)

        def put(ref):
            for half in range(2):
                ref[half, :, 0 : 2 * unit] = grown[:, half * 2 * unit : (half + 1) * 2 * unit]
                ref[half, :, 2 * unit :] = down[:, half * unit : (half + 1) * unit]

        pl.when(tile < EARLY)(functools.partial(put, early_ref))
        pl.when(tile >= EARLY)(functools.partial(put, grad_ref))

    @pl.when(step == 2 * count)
    def _():
        rows = hidden[...]
        rho = rho_of(rows)
        unit_rows = rows * rho
        drows = dtotal[...]
        du = drows * gain_ref[0:1]
        dgain_ref[...] = jnp.sum((drows * unit_rows).reshape(-1, 8, rows.shape[1]), 0)
        dh = dhidden_ref[...] + rho * (du - unit_rows * jnp.mean(du * unit_rows, -1, keepdims=True))
        dhidden_ref[...] = dh
        dattn = dh.astype(BF16)
        dmlp_t[...] = dh.T.astype(BF16)
        for half in range(2):
            donb_ref[half] = mm(dattn, out_weight(half))
            grad_ref[half] = mm(dmlp_t[...], onb_ref[half, :, 0 : 3 * unit]).astype(BF16)

    @pl.when(step == 2 * count + 1)
    def _():
        for half in range(2):
            grad_ref[half, :, 0:unit] = mm(dmlp_t[...], onb_ref[half, :, 3 * unit :]).astype(BF16)


def mlp(inputs, onb, weights, gain, mask, teacher, cotangent, coef):
    tokens, width_d = inputs.shape
    halves, _, cols = weights.shape
    half_cols = onb.shape[2]
    count = (cols - half_cols) // (3 * WIDTH)
    first_out = count * 3

    def whole(shape):
        return pl.BlockSpec(shape, lambda i: (0,) * len(shape))

    def tile(i):
        return (0, 0, jnp.where(i < count, i, jnp.minimum(i - count, count - 1)))

    wide = (halves, width_d, 3 * WIDTH)
    return pl.pallas_call(
        functools.partial(mlp_kernel, count),
        grid=(2 * count + 2,),
        in_specs=[whole(inputs.shape), whole(onb.shape), pl.BlockSpec(wide, tile)]
        + [
            pl.BlockSpec((halves, width_d, WIDTH), functools.partial(lambda n, i: (0, 0, n), first_out + n))
            for n in range(4)
        ]
        + [whole(gain.shape), whole(mask.shape), whole(teacher.shape), whole(cotangent.shape), whole(coef.shape)],
        out_specs=[
            whole((tokens, width_d)),
            whole((8, width_d)),
            pl.BlockSpec(wide, lambda i: (0, 0, jnp.clip(i - count, 0, EARLY - 1))),
            pl.BlockSpec(wide, lambda i: (0, 0, jnp.maximum(i - count - EARLY, 0))),
            whole((halves, tokens, half_cols)),
            whole((tokens, width_d)),
            whole((8, width_d)),
        ],
        out_shape=[
            jax.ShapeDtypeStruct((tokens, width_d), BF16),
            jax.ShapeDtypeStruct((8, width_d), F32),
            jax.ShapeDtypeStruct((halves, width_d, EARLY * 3 * WIDTH), BF16),
            jax.ShapeDtypeStruct((halves, width_d, cols - EARLY * 3 * WIDTH), BF16),
            jax.ShapeDtypeStruct((halves, tokens, half_cols), F32),
            jax.ShapeDtypeStruct((tokens, width_d), F32),
            jax.ShapeDtypeStruct((8, width_d), F32),
        ],
        scratch_shapes=[
            pltpu.VMEM((tokens, width_d), F32),
            pltpu.VMEM((tokens, width_d), BF16),
            pltpu.VMEM((width_d, tokens), BF16),
            pltpu.VMEM((tokens, width_d), F32),
            pltpu.VMEM((tokens, width_d), F32),
            pltpu.VMEM((tokens, width_d), BF16),
            pltpu.VMEM((width_d, tokens), BF16),
            pltpu.VMEM((count, tokens, 2 * WIDTH), F32),
            pltpu.VMEM((count, tokens, 2 * WIDTH), F32),
            pltpu.VMEM((count, tokens, 2 * WIDTH), BF16),
        ],
        compiler_params=pltpu.CompilerParams(vmem_limit_bytes=VMEM_LIMIT),
        name="mlp",
    )(inputs, onb, weights, weights, weights, weights, weights, gain, mask, teacher, cotangent, coef)


def project_back_kernel(
    dlin_ref, weight_ref, inputs_ref, gain_ref, dbl_ref, beta_ref, dhidden_ref,
    grad_ref, dinput_ref, dgain_ref, dbeta_ref,
    normed_t, total,
):
    step = pl.program_id(0)

    def unit():
        rows = inputs_ref[...].astype(F32)
        rho = lax.rsqrt(jnp.mean(rows * rows, -1, keepdims=True) + 1e-05)
        return rows * rho, rho

    @pl.when(step == 0)
    def _():
        normed_t[...] = (unit()[0] * gain_ref[0:1]).T.astype(BF16)
        dbl = dbl_ref[...].astype(BF16)
        total[...] = mm_t(dbl, beta_ref[...])
        dbeta_ref[...] = mm(normed_t[...], dbl)

    total[...] += mm_t(dlin_ref[0], weight_ref[0])
    grad_ref[0] = mm(normed_t[...], dlin_ref[0]).astype(BF16)

    @pl.when(step == pl.num_programs(0) - 1)
    def _():
        rows, rho = unit()
        drows = total[...]
        du = drows * gain_ref[0:1]
        dgain_ref[...] = jnp.sum((drows * rows).reshape(-1, 8, rows.shape[1]), 0)
        dinput_ref[...] = dhidden_ref[...] + rho * (
            du - rows * jnp.mean(du * rows, -1, keepdims=True)
        )


def project_back(dlin, weights, inputs, gain, dbl, beta_w, dhidden):
    halves, tokens, cols = dlin.shape
    width_d = inputs.shape[1]
    kinds = 2
    part = cols // kinds

    def whole(shape):
        return pl.BlockSpec(shape, lambda i: (0,) * len(shape))

    columns = pl.BlockSpec((1, width_d, part), lambda i: (i // kinds, 0, i % kinds))
    return pl.pallas_call(
        project_back_kernel,
        grid=(halves * kinds,),
        in_specs=[
            pl.BlockSpec((1, tokens, part), lambda i: (i // kinds, 0, i % kinds)),
            columns,
            whole(inputs.shape),
            whole(gain.shape),
            whole(dbl.shape),
            whole(beta_w.shape),
            whole(dhidden.shape),
        ],
        out_specs=[columns, whole(dhidden.shape), whole((8, width_d)), whole((width_d, WIDTH))],
        out_shape=[
            jax.ShapeDtypeStruct((halves, width_d, cols), BF16),
            jax.ShapeDtypeStruct((tokens, width_d), F32),
            jax.ShapeDtypeStruct((8, width_d), F32),
            jax.ShapeDtypeStruct((width_d, WIDTH), F32),
        ],
        scratch_shapes=[
            pltpu.VMEM((width_d, tokens), BF16),
            pltpu.VMEM((tokens, width_d), F32),
        ],
        compiler_params=pltpu.CompilerParams(vmem_limit_bytes=VMEM_LIMIT),
        name="project_back",
    )(dlin, weights, inputs, gain, dbl, beta_w, dhidden)


def mixer_tables(segments, length, beta, tokens):
    mine = lax.axis_index("tensor")
    seg = segments[0]
    position = jnp.arange(length)

    def behind(off):
        return jnp.where(position >= off, jnp.roll(seg, off), -1)

    ends = jnp.repeat(seg[CHUNK - 1 :: CHUNK], CHUNK)
    previous = jnp.where(position >= CHUNK, jnp.roll(ends, CHUNK), -1)
    columns = [seg, seg == previous, seg == ends]
    keeps = [behind(off) == seg for off in range(1, TAPS)]
    columns += keeps
    for off in range(1, TAPS):
        columns.append(jnp.where(position < length - off, jnp.roll(keeps[off - 1], -off), False))
    table = jnp.stack([c.astype(F32) for c in columns], 1)
    table = lax.dynamic_slice_in_dim(table, mine * tokens, tokens, 0)
    aux = jnp.concatenate(
        [
            table,
            jnp.zeros((tokens, 16 - table.shape[1]), F32),
            beta,
            jnp.zeros((tokens, WIDTH - 16 - beta.shape[1]), F32),
        ],
        1,
    )
    row = lax.dynamic_slice_in_dim(seg.astype(F32), mine * tokens, tokens, 0)
    return aux, jnp.broadcast_to(row[None], (8, tokens))


def by_thirds(first, second, third_one):
    rows = first.shape[0]
    tiles = jnp.stack([a.reshape(rows, -1, WIDTH) for a in (first, second, third_one)], 2)
    return tiles.reshape(rows, -1)


def thirds_of(values):
    rows = values.shape[0]
    tiles = values.reshape(rows, -1, 3, WIDTH)
    return tuple(tiles[:, :, i].reshape(rows, -1) for i in range(3))


def padded_rows(parts, multiple):
    flat = jnp.concatenate([p.reshape(-1) for p in parts])
    size = -(-flat.shape[0] // (multiple * WIDTH)) * multiple * WIDTH
    return jnp.pad(flat, (0, size - flat.shape[0])).reshape(-1, WIDTH)


def local(
    layer_input, segments, valid_mask, teacher, out_grad, norm_gain, w_query, w_key, w_value,
    w_beta, conv_weight, head_gain, w_out, mlp_gain, w_gate, w_up, w_down,
):
    parts, halves = lax.axis_size("dp"), lax.axis_size("tensor")
    tokens, width_d = layer_input.shape[1:]
    length = segments.shape[1]
    tokens_all = tokens * parts * halves
    half_heads = w_beta.shape[1]
    heads = half_heads * halves
    half_cols = w_query.shape[1]
    rows = w_query.shape[0]
    inputs_low = layer_input[0]

    valid = jnp.sum(valid_mask)
    counts = jnp.stack([valid // 64, valid % 64]).astype(BF16)
    small_parts = [w_beta, conv_weight, norm_gain, mlp_gain, head_gain, counts]
    small = padded_rows(small_parts, 16)
    first_shard = by_thirds(w_query, w_key, w_value)
    second_shard = jnp.concatenate([by_thirds(w_gate, w_up, w_down.T), w_out.T], 1)
    first_w, small = gather(
        [first_shard, small],
        split_tiles(3 * half_cols, rows)
        + [Tiles(1, "zxy", 0, small.shape[0], 0, WIDTH, WIDTH, 1, 0)],
        2,
    )
    second_w = lax.all_gather(second_shard, ("tensor", "dp"), axis=0, tiled=True).reshape(
        halves, width_d, second_shard.shape[1]
    )

    small = small.reshape(halves, parts, -1)
    marks = [0]
    for part in small_parts:
        marks.append(marks[-1] + part.size)
    beta_w, conv_w, gain_one, gain_two, gain_head, counts = (
        small[:, :, marks[i] : marks[i + 1]] for i in range(len(small_parts))
    )
    beta_w = beta_w.reshape(halves, width_d, half_heads).transpose(1, 0, 2).reshape(width_d, heads)
    beta_w = jnp.pad(beta_w, ((0, 0), (0, WIDTH - heads)))
    taps = conv_w.reshape((halves, parts) + conv_weight.shape).transpose(2, 3, 0, 4, 1, 5)
    taps = taps.reshape(12, heads * WIDTH).astype(F32)
    taps = jnp.concatenate([taps, jnp.zeros((4, heads * WIDTH), F32)], 0)
    gain_one = jnp.broadcast_to(gain_one[0].reshape(1, width_d).astype(F32), (8, width_d))
    gain_two = jnp.broadcast_to(gain_two[0].reshape(1, width_d).astype(F32), (8, width_d))
    gain_head = jnp.broadcast_to(gain_head[0].reshape(1, WIDTH).astype(F32), (8, WIDTH))
    counts = jnp.sum(counts.astype(F32), (0, 1))
    valid_sum = counts[0] * 64.0 + counts[1]

    halo = lax.ppermute(inputs_low[-HALO:], "tensor", [(0, 1), (1, 0)])
    spread = jnp.concatenate([halo, inputs_low], 0).astype(F32)
    rho_one = lax.rsqrt(jnp.mean(spread * spread, -1, keepdims=True) + 1e-05)
    spread = (spread * rho_one * gain_one[0:1]).astype(BF16)
    linear = jnp.einsum("td,jdc->jtc", spread, first_w, preferred_element_type=F32)
    strength = jax.nn.sigmoid(
        jnp.dot(spread[HALO:], beta_w[:, :heads], preferred_element_type=F32)
    )
    aux, seg_row = mixer_tables(segments, length, strength, tokens)
    onb, out, new, inverse, before = mixer_fwd(linear, aux, seg_row, taps, gain_head)
    coef = jnp.broadcast_to((tokens_all / 4.0) / valid_sum, (8, WIDTH))
    mask = valid_mask[0].astype(F32)[:, None]
    outputs, squares, early_g, second_g, donb, d_hidden, grad_gain_two = mlp(
        inputs_low, onb, second_w, gain_two, mask, teacher[0], out_grad[0], coef
    )
    early_g = lax.psum_scatter(
        early_g.reshape(halves * width_d, -1), ("tensor", "dp"), scatter_dimension=0, tiled=True
    ).astype(F32)
    dlin, dbl, dtaps, dgain = mixer_bwd(
        linear, aux, seg_row, taps, gain_head, out, new, inverse, before, donb
    )
    first_g, d_input, grad_gain_one, grad_beta = project_back(
        dlin, first_w, inputs_low, gain_one, dbl, beta_w, d_hidden
    )

    def shares(values):
        return jnp.broadcast_to(values.reshape(1, parts, -1), (halves, parts, values.size // parts))

    tail_parts = [
        grad_beta[:, :heads].reshape(parts, rows, halves, half_heads).transpose(2, 0, 1, 3),
        dtaps[:12]
        .reshape(12, halves, half_heads, parts, WIDTH // parts)
        .transpose(1, 3, 0, 2, 4),
        shares(jnp.sum(grad_gain_one, 0)),
        shares(jnp.sum(grad_gain_two, 0)),
        shares(dgain[0]),
        jnp.broadcast_to(jnp.sum(squares), (halves, parts, 1)),
    ]
    tail = jnp.concatenate([p.reshape(halves, parts, -1) for p in tail_parts], 2)
    tail_rows = -(-tail.shape[2] // (8 * WIDTH)) * 8
    tail = jnp.pad(tail, ((0, 0), (0, 0), (0, tail_rows * WIDTH - tail.shape[2])))
    g_gate, g_up, g_down, g_out, g_query, g_key, g_value, tail = scatter(
        second_g, first_g, tail.reshape(halves, parts * tail_rows, WIDTH), 3
    )
    g_gate, g_up, g_down = (
        jnp.concatenate(pair, 1) for pair in zip(thirds_of(early_g), (g_gate, g_up, g_down))
    )
    tail = tail.reshape(-1)
    sizes = [w_beta.size, conv_weight.size, norm_gain.size, mlp_gain.size, head_gain.size, 1]
    cuts = [sum(sizes[:i]) for i in range(7)]
    g_beta, g_conv, g_one, g_two, g_head, squares = (tail[cuts[i] : cuts[i + 1]] for i in range(6))
    return (
        outputs[None],
        squares[0] / (width_d * valid_sum),
        d_input[None],
        g_one,
        g_query,
        g_key,
        g_value,
        g_beta.reshape(w_beta.shape),
        g_conv.reshape(conv_weight.shape),
        g_head,
        g_out.T,
        g_two,
        g_gate,
        g_up,
        g_down.T,
    )


def solution(mesh):
    in_specs = (
        P("dp", "tensor", None),
        P("dp", None),
        P("dp", "tensor"),
        P("dp", "tensor", None),
        P("dp", "tensor", None),
        P("dp"),
        P("dp", "tensor"),
        P("dp", "tensor"),
        P("dp", "tensor"),
        P("dp", "tensor"),
        P(None, None, "tensor", "dp"),
        P("dp"),
        P("tensor", "dp"),
        P("dp"),
        P("dp", "tensor"),
        P("dp", "tensor"),
        P("tensor", "dp"),
    )
    out_specs = (
        P("dp", "tensor", None),
        P(),
        P("dp", "tensor", None),
        P("dp"),
        P("dp", "tensor"),
        P("dp", "tensor"),
        P("dp", "tensor"),
        P("dp", "tensor"),
        P(None, None, "tensor", "dp"),
        P("dp"),
        P("tensor", "dp"),
        P("dp"),
        P("dp", "tensor"),
        P("dp", "tensor"),
        P("tensor", "dp"),
    )
    return jax.shard_map(local, mesh=mesh, in_specs=in_specs, out_specs=out_specs, check_vma=False)
```

```python
import collections
import functools

import jax
import jax.numpy as jnp
from jax import lax
from jax.experimental import pallas as pl
from jax.experimental.pallas import tpu as pltpu
from jax.sharding import PartitionSpec as P

F32, BF16 = jnp.float32, jnp.bfloat16
MESH = pl.DeviceIdType.MESH
CHUNK = 128
HALO = 16
WIDTH = 128
PAIR = 2
MOVES = 2
TAPS = 4
VMEM_LIMIT = 60 * 1024 * 1024

GRID = (4, 2, 2)
DEPTH = GRID[0] - 1 + 2
LAGS = DEPTH + 2
Tiles = collections.namedtuple(
    "Tiles", ["array", "order", "row", "rows", "col", "stride", "cols", "count", "start"]
)


def on_grid():
    return lax.axis_size("dp") == GRID[0] * GRID[1] * GRID[2] and lax.axis_size("tensor") == 2


def position():
    mine = lax.axis_index("dp")
    _, size_x, size_c = GRID
    return {
        "y": lax.axis_index("tensor"),
        "z": mine // (size_x * size_c),
        "x": (mine // size_c) % size_x,
        "c": mine % size_c,
    }


def device_of(at):
    _, size_x, size_c = GRID
    return {"dp": (at["z"] * size_x + at["x"]) * size_c + at["c"], "tensor": at["y"]}


def inside(z):
    return (z >= 0) & (z < GRID[0])


def across(at, link):
    axis, way = link
    return dict(at, z=at["z"] + way) if axis == "z" else dict(at, **{axis: 1 - at[axis]})


def greet_all(at):
    barrier = pltpu.get_barrier_semaphore()
    for link in (("x", 0), ("y", 0), ("c", 0)):
        pl.semaphore_signal(
            barrier, inc=1, device_id=device_of(across(at, link)), device_id_type=MESH
        )
    for way in (-1, 1):

        @pl.when(inside(at["z"] + way))
        def _():
            pl.semaphore_signal(
                barrier,
                inc=1,
                device_id=device_of(across(at, ("z", way))),
                device_id_type=MESH,
            )

    peers = 3 + inside(at["z"] - 1).astype(jnp.int32) + inside(at["z"] + 1).astype(jnp.int32)
    pl.semaphore_wait(barrier, peers)


def remote(src, dst, send_sem, recv_sem, to):
    return pltpu.make_async_remote_copy(
        src_ref=src, dst_ref=dst, send_sem=send_sem, recv_sem=recv_sem,
        device_id=device_of(to), device_id_type=MESH,
    )


def when(test, action):
    if test is None:
        action()
    else:
        pl.when(test)(action)


def both(first, second):
    if first is None or second is None:
        return second if first is None else first
    return first & second


def split_tiles(cols, rows, unit=WIDTH, array=0, start=0):
    half = rows // 2
    count = cols // (3 * unit)
    out = [
        Tiles(array, "zxy", 0, half, 0, 3 * unit, unit, count, start),
        Tiles(array, "zyx", half, half, 0, 3 * unit, unit, count, start),
        Tiles(array, "xzy", 0, half, unit, 3 * unit, 2 * unit, count, start),
        Tiles(array, "yzx", half, half, unit, 3 * unit, 2 * unit, count, start),
    ]
    rest = cols - 3 * unit * count
    if rest:
        out.append(Tiles(array, "xzy", 0, half, cols - rest, rest, rest, 1, start))
        out.append(Tiles(array, "yzx", half, half, cols - rest, rest, rest, 1, start))
    return out


def window(tile, group):
    start = tile.col + group * tile.stride
    if not isinstance(start, int):
        start = pl.multiple_of(start, 128)
    return pl.ds(tile.row, tile.rows), pl.ds(start, tile.cols)


def steps_of(tiles):
    return max(tile.start + tile.count for tile in tiles) + LAGS - 1


def first_slots(tiles):
    return [sum(tile.count for tile in tiles[:i]) for i in range(len(tiles))]


def order_of(tile):
    first, last = [axis for axis in tile.order if axis != "z"]
    return first, last, tile.order[0] == "z"


def distances():
    return range(1 - GRID[0], GRID[0])


def ways(distance):
    return (1, -1) if distance == 0 else ((1,) if distance < 0 else (-1,))


class Gather:
    def __init__(self, tiles, shards, fulls, sems):
        self.tiles, self.shards, self.fulls = tiles, shards, fulls
        self.send_sem, self.recv_sem, self.core_send, self.core_recv, self.own_sem = sems
        self.at = position()
        self.steps = steps_of(tiles)

    @staticmethod
    def sems(tiles, arrays):
        slots = sum(tile.count for tile in tiles)
        return [
            pltpu.SemaphoreType.DMA((len(tiles), 2, 4, GRID[0])),
            pltpu.SemaphoreType.DMA((slots, 3, GRID[0])),
            pltpu.SemaphoreType.DMA((slots,)),
            pltpu.SemaphoreType.DMA((slots,)),
            pltpu.SemaphoreType.DMA((arrays,)),
        ]

    def begin(self):
        at = self.at
        copies = [
            pltpu.make_async_copy(
                shard, full.at[at["y"], at["z"], at["x"], at["c"]], self.own_sem.at[i]
            )
            for i, (shard, full) in enumerate(zip(self.shards, self.fulls))
        ]
        for copy in copies:
            copy.start()
        greet_all(at)
        for copy in copies:
            copy.wait()

    def copy(self, index, group, slot, z, link, own=False):
        at, tile = self.at, self.tiles[index]
        first, last, z_first = order_of(tile)
        rows, cols = window(tile, group)
        pair = link == 3 or (link < 2 and not z_first)
        spot = {"y": at["y"], "x": at["x"]}
        if pair:
            spot[first] = slice(None)
        ref = self.fulls[tile.array].at[spot["y"], z, spot["x"], at["c"], rows, cols]
        to = ("z", 1 - 2 * link) if link < 2 else (first if link == 2 else last, 0)
        return remote(
            self.shards[tile.array].at[rows, cols] if own else ref,
            ref,
            self.send_sem.at[index, group % 2, link, z],
            self.recv_sem.at[slot, max(link - 1, 0), z],
            across(at, to),
        )

    def send(self, index, group, slot, z, link, own=False):
        def go():
            one = self.copy(index, group, slot, z, link, own)
            pl.when(group >= 2)(one.wait_send)
            one.start()

        when(inside(self.at["z"] + 1 - 2 * link) if link < 2 else None, go)

    def visit(self, index, group, slot, lag):
        at, tile = self.at, self.tiles[index]
        _, _, z_first = order_of(tile)
        offset = 0 if z_first else 1
        for far in distances():
            z = at["z"] + far

            def handle():
                if z_first and lag == abs(far):
                    if far:
                        self.copy(index, group, slot, z, 0).wait_recv()
                    for way in ways(far):
                        self.send(index, group, slot, z, (1 - way) // 2, far == 0)
                    self.send(index, group, slot, z, 2, far == 0)
                if z_first and lag == abs(far) + 1:
                    self.copy(index, group, slot, z, 2).wait_recv()
                    self.send(index, group, slot, z, 3)
                if not z_first and far == 0 and lag == 0:
                    self.send(index, group, slot, z, 2, True)
                if not z_first and lag == abs(far) + 1:
                    self.copy(index, group, slot, z, 0 if far else 2).wait_recv()
                    for way in ways(far):
                        self.send(index, group, slot, z, (1 - way) // 2)
                    self.send(index, group, slot, z, 3)
                if lag == abs(far) + 2:
                    self.copy(index, group, slot, z, 3).wait_recv()

            if any(lag == abs(far) + more for more in range(3)):
                when(inside(z) if far else None, handle)
        if lag >= DEPTH:
            rows, cols = window(tile, group)
            part = self.fulls[tile.array].at[:, :, :, at["c"], rows, cols]
            pair = remote(
                part, part, self.core_send.at[slot], self.core_recv.at[slot], across(at, ("c", 0))
            )
            pair.start() if lag == DEPTH else pair.wait()

    def step(self, step):
        for lag in range(LAGS):
            for index, (tile, first) in enumerate(zip(self.tiles, first_slots(self.tiles))):
                group = step - lag - tile.start
                pl.when((group >= 0) & (group < tile.count))(
                    functools.partial(self.visit, index, group, first + group, lag)
                )

    def finish(self):
        for index, tile in enumerate(self.tiles):
            _, _, z_first = order_of(tile)
            for group in range(max(0, tile.count - 2), tile.count):
                for far in distances():
                    z = self.at["z"] + far
                    here = inside(z) if far else None
                    for way in ways(far):
                        one = self.copy(index, group, 0, z, (1 - way) // 2)
                        when(both(here, inside(self.at["z"] + way)), one.wait_send)
                    if z_first or far == 0:
                        when(here, self.copy(index, group, 0, z, 2).wait_send)
                    when(here, self.copy(index, group, 0, z, 3).wait_send)


class Scatter:
    def __init__(self, tiles, grads, put, boxes, sems):
        self.tiles, self.grads, self.put = tiles, grads, put
        self.sums, self.pairs, self.from_z, self.from_first, self.from_last = (
            boxes[i * len(tiles) : (i + 1) * len(tiles)] for i in range(5)
        )
        self.send_sem, self.recv_sem, self.core_send, self.core_recv, self.own_sem = sems
        self.at = position()
        self.steps = steps_of(tiles)

    @staticmethod
    def boxes(tiles, dtypes):
        whole, from_z, from_first, from_last = [], [], [], []
        for tile in tiles:
            z_first = order_of(tile)[2]
            dtype, shape = dtypes[tile.array], (tile.rows, tile.cols)
            whole.append(pltpu.VMEM((tile.count, 2) + GRID[:2] + shape, dtype))
            from_z.append(
                pltpu.VMEM((tile.count, 2, GRID[0]) + (() if z_first else (2,)) + shape, dtype)
            )
            from_first.append(
                pltpu.VMEM((tile.count,) + ((GRID[0],) if z_first else ()) + shape, dtype)
            )
            from_last.append(pltpu.VMEM((tile.count, GRID[0], 2) + shape, dtype))
        return whole + whole + from_z + from_first + from_last

    @staticmethod
    def sems(tiles):
        slots = sum(tile.count for tile in tiles)
        return [
            pltpu.SemaphoreType.DMA((len(tiles), 2, 3, GRID[0])),
            pltpu.SemaphoreType.DMA((slots, 4, GRID[0])),
            pltpu.SemaphoreType.DMA((slots,)),
            pltpu.SemaphoreType.DMA((slots,)),
            pltpu.SemaphoreType.DMA((slots,)),
        ]

    def begin(self):
        greet_all(self.at)

    def spot(self, index, group, z, kind, other=False):
        first, last, z_first = order_of(self.tiles[index])
        spot = {"y": self.at["y"], "x": self.at["x"]}
        if kind == "last" or (kind == "z" and not z_first):
            spot[first] = slice(None)
        if other:
            axis = first if kind == "first" else last
            spot[axis] = 1 - self.at[axis]
        return (group, spot["y"], z, spot["x"])

    def copy(self, index, group, slot, z, kind, way=0):
        first, last, z_first = order_of(self.tiles[index])
        if kind == "z":
            label = (1 + way) // 2
            to, dst = ("z", way), self.from_z[index].at[group, label, z]
        elif kind == "first":
            label, to = 2, (first, 0)
            dst = self.from_first[index].at[(group, z) if z_first else group]
        else:
            label, to, dst = 3, (last, 0), self.from_last[index].at[group, z]
        return remote(
            self.sums[index].at[self.spot(index, group, z, kind, kind != "z")],
            dst,
            self.send_sem.at[index, group % 2, max(label - 1, 0), z],
            self.recv_sem.at[slot, label, z],
            across(self.at, to),
        )

    def send(self, index, group, slot, z, kind, way=0):
        one = self.copy(index, group, slot, z, kind, way)
        pl.when(group >= 2)(one.wait_send)
        one.start()

    def add(self, index, group, slot, z, kind, way=0):
        self.copy(index, group, slot, z, kind, -way).wait_recv()
        z_first = order_of(self.tiles[index])[2]
        if kind == "z":
            came = self.from_z[index][group, (1 - way) // 2, z]
        elif kind == "first":
            came = self.from_first[index][(group, z) if z_first else group]
        else:
            came = self.from_last[index][group, z]
        spot = self.spot(index, group, z, kind)
        total = self.sums[index][spot].astype(F32) + came.astype(F32)
        self.sums[index][spot] = total.astype(self.sums[index].dtype)

    def visit(self, index, group, slot, stage):
        at, tile = self.at, self.tiles[index]
        rows, cols = window(tile, group)
        grad, sums = self.grads[tile.array], self.sums[index]
        _, _, z_first = order_of(tile)
        if stage <= 1:
            pair = remote(
                grad.at[:, :, :, 1 - at["c"], rows, cols],
                self.pairs[index].at[group],
                self.core_send.at[slot],
                self.core_recv.at[slot],
                across(at, ("c", 0)),
            )
            own = pltpu.make_async_copy(
                grad.at[:, :, :, at["c"], rows, cols], sums.at[group], self.own_sem.at[slot]
            )
        if stage == 0:
            pair.start()
            own.start()
            return
        if stage == 1:
            own.wait()
            pair.wait()
            sums[group] = (
                sums[group].astype(F32) + self.pairs[index][group].astype(F32)
            ).astype(sums.dtype)
        lag = DEPTH + 1 - stage

        def along_z(z, far):
            for way in ways(far):
                pl.when(inside(at["z"] + way))(
                    functools.partial(self.add, index, group, slot, z, "z", way)
                )
            if far:
                self.send(index, group, slot, z, "z", 1 if far > 0 else -1)

        for far in distances():
            z = at["z"] + far

            def handle():
                if lag == abs(far) + 2:
                    self.send(index, group, slot, z, "last")
                if lag == abs(far) + 1:
                    self.add(index, group, slot, z, "last")
                    if z_first:
                        self.send(index, group, slot, z, "first")
                    else:
                        along_z(z, far)
                        if far == 0:
                            self.send(index, group, slot, z, "first")
                if lag == abs(far) and (z_first or far == 0):
                    self.add(index, group, slot, z, "first")
                    if z_first:
                        along_z(z, far)
                    if far == 0:
                        self.put(tile, group, sums[group, at["y"], at["z"], at["x"]].astype(F32))

            if any(lag == abs(far) + more for more in range(3)):
                when(inside(z) if far else None, handle)

    def step(self, step):
        for stage in range(LAGS):
            for index, (tile, first) in enumerate(zip(self.tiles, first_slots(self.tiles))):
                group = step - stage - tile.start
                pl.when((group >= 0) & (group < tile.count))(
                    functools.partial(self.visit, index, group, first + group, stage)
                )

    def finish(self):
        for index, tile in enumerate(self.tiles):
            z_first = order_of(tile)[2]
            for group in range(max(0, tile.count - 2), tile.count):
                for far in distances():
                    z = self.at["z"] + far
                    here = inside(z) if far else None
                    if far:
                        one = self.copy(index, group, 0, z, "z", 1 if far > 0 else -1)
                        when(here, one.wait_send)
                    if z_first or far == 0:
                        when(here, self.copy(index, group, 0, z, "first").wait_send)
                    when(here, self.copy(index, group, 0, z, "last").wait_send)


def run_all(moves):
    moves.begin()
    lax.fori_loop(0, moves.steps, lambda step, _: (moves.step(step), 0)[1], 0)
    moves.finish()


def gather_kernel(tiles, arrays, *refs):
    run_all(Gather(tiles, refs[:arrays], refs[arrays : 2 * arrays], refs[2 * arrays :]))


def gather(shards, tiles, ident):
    halves = lax.axis_size("tensor")
    if not on_grid():
        return [
            lax.all_gather(shard, ("tensor", "dp"), axis=0, tiled=False).reshape(
                (halves, -1) + shard.shape[1:]
            )
            for shard in shards
        ]
    hbm = pl.BlockSpec(memory_space=pl.ANY)
    arrays = len(shards)
    fulls = pl.pallas_call(
        functools.partial(gather_kernel, tiles, arrays),
        in_specs=[hbm] * arrays,
        out_specs=[hbm] * arrays,
        out_shape=[
            jax.ShapeDtypeStruct((halves,) + GRID + shard.shape, shard.dtype) for shard in shards
        ],
        scratch_shapes=Gather.sems(tiles, arrays),
        compiler_params=pltpu.CompilerParams(collective_id=ident, has_side_effects=True),
        name="gather",
    )(*shards)
    return [full.reshape(halves, -1, full.shape[-1]) for full in fulls]


def put_turns(turns, rest, columns):
    def put(tile, group, total):
        rows = pl.ds(tile.row, tile.rows)
        for i in range(tile.cols // WIDTH):
            piece = total[:, i * WIDTH : (i + 1) * WIDTH]
            at = tile.col // WIDTH + i
            column = at + group * (tile.stride // WIDTH)

            def inner():
                lanes = pl.multiple_of(lax.div(column, len(turns)) * WIDTH, WIDTH)
                turns[at % len(turns)][rows, pl.ds(lanes, WIDTH)] = piece

            if rest is None:
                inner()
                continue
            if tile.count > 1 or at < columns:
                pl.when(column < columns)(inner)

            @pl.when(column >= columns)
            def _():
                lanes = pl.multiple_of((column - columns) * WIDTH, WIDTH)
                rest[rows, pl.ds(lanes, WIDTH)] = piece

    return put


def scatter_kernel(tiles, first_ref, small_grad_ref, query, key, value, small_ref, *rest):
    boxes = 5 * len(tiles)
    turns = put_turns((query, key, value), None, 0)

    def put(tile, group, total):
        if tile.array == 1:
            small_ref[...] = total
        else:
            turns(tile, group, total)

    run_all(Scatter(tiles, [first_ref, small_grad_ref], put, rest[:boxes], rest[boxes:]))


def blocks_of(grad):
    return grad.reshape((2,) + GRID + (-1, grad.shape[-1]))


def plain_scatter(grad):
    return lax.psum_scatter(
        grad.reshape(-1, grad.shape[-1]), ("tensor", "dp"), scatter_dimension=0, tiled=True
    ).astype(F32)


def scatter(first, small, ident):
    rows = first.shape[1] // lax.axis_size("dp")
    if not on_grid():
        return apart(plain_scatter(first), 3) + (plain_scatter(small),)
    grads = [blocks_of(first), blocks_of(small)]
    tiles = split_tiles(first.shape[2], rows)
    small_rows = grads[1].shape[-2]
    tiles.append(Tiles(1, "zxy", 0, small_rows, 0, WIDTH, WIDTH, 1, 0))
    hbm = pl.BlockSpec(memory_space=pl.ANY)
    shapes = [(rows, first.shape[2] // 3)] * 3 + [(small_rows, WIDTH)]
    return pl.pallas_call(
        functools.partial(scatter_kernel, tiles),
        in_specs=[hbm] * 2,
        out_specs=[pl.BlockSpec(memory_space=pltpu.VMEM)] * len(shapes),
        out_shape=[jax.ShapeDtypeStruct(shape, F32) for shape in shapes],
        scratch_shapes=Scatter.boxes(tiles, [grad.dtype for grad in grads]) + Scatter.sems(tiles),
        compiler_params=pltpu.CompilerParams(
            collective_id=ident, has_side_effects=True, vmem_limit_bytes=VMEM_LIMIT
        ),
        name="scatter",
    )(*grads)


def contract(left, right, dim_left, dim_right):
    return lax.dot_general(
        left.astype(BF16),
        right.astype(BF16),
        (((dim_left,), (dim_right,)), ((), ())),
        preferred_element_type=F32,
    )


def mm(left, right):
    return contract(left, right, 1, 0)


def mm_t(left, right):
    return contract(left, right, 1, 1)


def t_mm(left, right):
    return contract(left, right, 0, 0)


def tri_inverses(systems):
    rows = lax.broadcasted_iota(jnp.int32, (CHUNK, CHUNK), 0)
    cols = lax.broadcasted_iota(jnp.int32, (CHUNK, CHUNK), 1)
    inverses = None
    size = 1
    while size < CHUNK:
        link = (
            (rows // (2 * size) == cols // (2 * size))
            & ((rows // size) % 2 == 1)
            & ((cols // size) % 2 == 0)
        )
        parts = [jnp.where(link, system, 0.0) for system in systems]
        if size == 1:
            eye = (rows == cols).astype(F32)
            inverses = [eye - part for part in parts]
        else:
            lows = [inverse.astype(BF16) for inverse in inverses]
            middles = [mm(part, low) for part, low in zip(parts, lows)]
            inverses = [
                inverse - mm(low, middle)
                for inverse, low, middle in zip(inverses, lows, middles)
            ]
        size *= 2
    return inverses


def conv_of(lin_ref, base, lanes, taps, row, keeps, tokens):
    total = lin_ref[0, base : base + tokens, lanes] * taps[row : row + 1]
    for off in range(1, TAPS):
        total = total + taps[row + off : row + off + 1] * (
            lin_ref[0, base - off : base - off + tokens, lanes] * keeps[off]
        )
    return total


def third(sub, index):
    first = (sub * 3 + index) * WIDTH
    return slice(first, first + WIDTH)


def head_column(aux, lane):
    lanes = lax.broadcasted_iota(jnp.int32, aux.shape, 1)
    return jnp.sum(jnp.where(lanes == lane, aux, 0.0), axis=1, keepdims=True)


def greet(partner):
    barrier = pltpu.get_barrier_semaphore()
    pl.semaphore_signal(
        barrier, inc=1, device_id={"tensor": partner}, device_id_type=MESH
    )
    pl.semaphore_wait(barrier, 1)


def chunk_masks(aux, seg_row, at):
    rows = lax.broadcasted_iota(jnp.int32, (CHUNK, CHUNK), 0)
    cols = lax.broadcasted_iota(jnp.int32, (CHUNK, CHUNK), 1)
    same = aux[at : at + CHUNK, 0:1] == seg_row[0:1, at : at + CHUNK]
    return same & (rows > cols), same & (rows >= cols)


def mixer_fwd_kernel(
    tokens, lin_ref, aux_ref, seg_ref, taps_ref, gain_ref,
    onb_ref, o_ref, n_ref, t_ref, s_ref,
    state, outbox, inbox, send_sem, recv_sem,
):
    step = pl.program_id(0)
    mine = lax.axis_index("tensor")
    chunks = tokens // CHUNK

    @pl.when(step == 0)
    def _():
        greet(1 - mine)

    def hand_over(head):
        return pltpu.make_async_remote_copy(
            src_ref=outbox.at[head],
            dst_ref=inbox.at[head],
            send_sem=send_sem.at[head],
            recv_sem=recv_sem.at[head],
            device_id={"tensor": 1 - mine},
            device_id_type=MESH,
        )

    aux = aux_ref[...]
    seg_row = seg_ref[...]
    keeps = [None] + [aux[:, 2 + off : 3 + off] for off in range(1, TAPS)]
    heads = []
    for sub in range(PAIR):
        lanes = slice(sub * WIDTH, (sub + 1) * WIDTH)
        taps = taps_ref[:, lanes]
        beta = head_column(aux, 16 + step * PAIR + sub)
        acts = []
        for index in range(3):
            mixed = conv_of(lin_ref, HALO, third(sub, index), taps, index * TAPS, keeps, tokens)
            acts.append(mixed * jax.nn.sigmoid(mixed))
        q = acts[0] * (
            lax.rsqrt(jnp.sum(acts[0] * acts[0], -1, keepdims=True) + 1e-06) * WIDTH ** (-0.5)
        )
        k = acts[1] * lax.rsqrt(jnp.sum(acts[1] * acts[1], -1, keepdims=True) + 1e-06)
        heads.append((q, k, acts[2], beta))
    spots = [(sub, c) for sub in range(PAIR) for c in range(chunks)]
    masks = [chunk_masks(aux, seg_row, c * CHUNK) for c in range(chunks)]

    def cut(values, c):
        return values[c * CHUNK : (c + 1) * CHUNK]

    lows = [(q.astype(BF16), k.astype(BF16)) for q, k, _, _ in heads]
    systems = [
        jnp.where(
            masks[c][0],
            cut(heads[sub][3], c) * mm_t(cut(lows[sub][1], c), cut(lows[sub][1], c)),
            0.0,
        )
        for sub, c in spots
    ]
    scores_of = [
        jnp.where(masks[c][1], mm_t(cut(lows[sub][0], c), cut(lows[sub][1], c)), 0.0).astype(BF16)
        for sub, c in spots
    ]
    inner = []
    for (sub, c), inverse, scores in zip(spots, tri_inverses(systems), scores_of):
        inverse = inverse.astype(BF16)
        t_ref[sub, c] = inverse
        inner.append((inverse, scores))

    @pl.when(mine == 0)
    def _():
        state[...] = jnp.zeros_like(state)

    @pl.when(mine == 1)
    def _():
        for sub in range(PAIR):
            head = step * PAIR + sub
            hand_over(head).wait_recv()
            state[sub] = inbox[head]

    carried = [state[sub] for sub in range(PAIR)]
    for c in range(chunks):
        at = c * CHUNK
        first = aux[at : at + CHUNK, 1:2]
        last = aux[at : at + CHUNK, 2:3]
        keep = aux[at + CHUNK - 1 : at + CHUNK, 1:2]
        subs = range(PAIR)
        befores = [carried[sub].astype(BF16) for sub in subs]
        reads = [
            mm(jnp.concatenate([cut(lows[sub][1], c), cut(lows[sub][0], c)], 0), befores[sub])
            for sub in subs
        ]
        news = [
            mm(
                inner[sub * chunks + c][0],
                cut(heads[sub][3], c) * (cut(heads[sub][2], c) - first * reads[sub][:CHUNK]),
            ).astype(BF16)
            for sub in subs
        ]
        carried = [
            keep * carried[sub] + t_mm(last * cut(heads[sub][1], c), news[sub]) for sub in subs
        ]
        outs = [
            first * reads[sub][CHUNK:] + mm(inner[sub * chunks + c][1], news[sub]) for sub in subs
        ]
        for sub in subs:
            s_ref[sub, c] = befores[sub]
            n_ref[sub, c] = news[sub]
            lanes = slice(sub * WIDTH, (sub + 1) * WIDTH)
            out = outs[sub]
            o_ref[0, at : at + CHUNK, lanes] = out
            scale = lax.rsqrt(jnp.mean(out * out, -1, keepdims=True) + 1e-05)
            onb_ref[0, at : at + CHUNK, lanes] = (out * scale * gain_ref[0:1]).astype(BF16)

    @pl.when(mine == 0)
    def _():
        for sub in range(PAIR):
            head = step * PAIR + sub
            outbox[head] = carried[sub]
            hand_over(head).start()

    @pl.when((step == pl.num_programs(0) - 1) & (mine == 0))
    def _():
        for head in range(outbox.shape[0]):
            hand_over(head).wait_send()


def mixer_bwd_kernel(
    tokens, tiles, lin_ref, aux_ref, seg_ref, taps_ref, gain_ref,
    o_ref, n_ref, t_ref, s_ref, donb_ref, *refs,
):
    moves = None
    if tiles:
        grads_ref, refs = refs[0], refs[1:]
    dlin_ref, dbl_ref, dtaps_ref, dgain_ref, *refs = refs
    if tiles:
        sums, refs = refs[:4], refs[4:]
    state, extended, outbox, inbox, tailbox, headbox = refs[:6]
    send_sem, recv_sem, tail_send, tail_recv, *refs = refs[6:]
    if tiles:
        boxes = 5 * len(tiles)
        columns = 3 * (sums[0].shape[1] // WIDTH)
        put = put_turns(sums[:3], sums[3], columns)
        moves = Scatter(tiles, [grads_ref], put, refs[:boxes], refs[boxes:])
    step = pl.program_id(0)
    mine = lax.axis_index("tensor")
    chunks = tokens // CHUNK

    @pl.when(step == 0)
    def _():
        if moves:
            moves.begin()
        else:
            greet(1 - mine)
        dbl_ref[...] = jnp.zeros_like(dbl_ref)
        dgain_ref[...] = jnp.zeros_like(dgain_ref)

    def hand_over(head):
        return pltpu.make_async_remote_copy(
            src_ref=outbox.at[head],
            dst_ref=inbox.at[head],
            send_sem=send_sem.at[head],
            recv_sem=recv_sem.at[head],
            device_id={"tensor": 1 - mine},
            device_id_type=MESH,
        )

    def hand_tail(head):
        return pltpu.make_async_remote_copy(
            src_ref=tailbox.at[head],
            dst_ref=headbox.at[head],
            send_sem=tail_send.at[head],
            recv_sem=tail_recv.at[head],
            device_id={"tensor": 1 - mine},
            device_id_type=MESH,
        )

    if moves:
        moves.step(step * MOVES)

    aux = aux_ref[...]
    seg_row = seg_ref[...]
    keeps = [None] + [aux[:tokens, 2 + off : 3 + off] for off in range(1, TAPS)]
    heads, inner = [], []
    for sub in range(PAIR):
        lanes = slice(sub * WIDTH, (sub + 1) * WIDTH)
        taps = taps_ref[:, lanes]
        beta = head_column(aux[:tokens], 16 + step * PAIR + sub)
        mixes, sigs, acts = [], [], []
        for index in range(3):
            mixed = conv_of(lin_ref, HALO, third(sub, index), taps, index * TAPS, keeps, tokens)
            mixes.append(mixed)
            sigs.append(jax.nn.sigmoid(mixed))
            acts.append(mixed * sigs[-1])
        rho_q = lax.rsqrt(jnp.sum(acts[0] * acts[0], -1, keepdims=True) + 1e-06)
        rho_k = lax.rsqrt(jnp.sum(acts[1] * acts[1], -1, keepdims=True) + 1e-06)
        q = acts[0] * (rho_q * WIDTH ** (-0.5))
        k = acts[1] * rho_k
        out = o_ref[0, :, lanes]
        don = donb_ref[0, :, lanes]
        scale = lax.rsqrt(jnp.mean(out * out, -1, keepdims=True) + 1e-05)
        dgain_ref[0:1] += jnp.sum(don * out * scale, 0, keepdims=True)
        du = don * gain_ref[0:1]
        dout = scale * du - out * (scale * scale * scale) * jnp.mean(
            out * du, -1, keepdims=True
        )
        heads.append((q, k, acts, beta, mixes, sigs, rho_q, rho_k, dout))
    spots = [(sub, c) for sub in range(PAIR) for c in range(chunks)]
    masks = [chunk_masks(aux, seg_row, c * CHUNK) for c in range(chunks)]
    firsts = [aux[c * CHUNK : (c + 1) * CHUNK, 1:2] for c in range(chunks)]

    def cut(values, c):
        return values[c * CHUNK : (c + 1) * CHUNK]

    lows = [
        (q.astype(BF16), k.astype(BF16), dout.astype(BF16))
        for q, k, _, _, _, _, _, _, dout in heads
    ]
    grams = [
        mm_t(jnp.concatenate([cut(lows[s][1], c), cut(lows[s][0], c)], 0), cut(lows[s][1], c))
        for s, c in spots
    ]
    turned = [
        mm_t(cut(lows[s][2], c), jnp.concatenate([n_ref[s, c], s_ref[s, c]], 0)) for s, c in spots
    ]
    scores_of = [
        jnp.where(masks[c][1], gram[CHUNK:], 0.0).astype(BF16)
        for (s, c), gram in zip(spots, grams)
    ]
    dscores_of = [
        jnp.where(masks[c][1], turn[:, :CHUNK], 0.0).astype(BF16)
        for (s, c), turn in zip(spots, turned)
    ]
    reads = [mm(cut(lows[s][1], c), s_ref[s, c]) for s, c in spots]
    pulls = [t_mm(scores, cut(lows[s][2], c)) for (s, c), scores in zip(spots, scores_of)]
    reaches = [
        t_mm(firsts[c] * cut(heads[s][0], c), cut(lows[s][2], c)) for s, c in spots
    ]
    dqs = [
        firsts[c] * turn[:, CHUNK:] + mm(dscores, cut(lows[s][1], c))
        for (s, c), turn, dscores in zip(spots, turned, dscores_of)
    ]
    dks = [t_mm(dscores, cut(lows[s][0], c)) for (s, c), dscores in zip(spots, dscores_of)]
    gaps = [
        cut(heads[s][2][2], c) - firsts[c] * read for (s, c), read in zip(spots, reads)
    ]
    inner = [
        (gram[:CHUNK], masks[c][0], pull, reach, dq, dk, gap)
        for (s, c), gram, pull, reach, dq, dk, gap in zip(
            spots, grams, pulls, reaches, dqs, dks, gaps
        )
    ]

    if moves:
        for more in range(1, MOVES):
            moves.step(step * MOVES + more)

    @pl.when(mine == 1)
    def _():
        state[...] = jnp.zeros_like(state)

    @pl.when(mine == 0)
    def _():
        for sub in range(PAIR):
            head = step * PAIR + sub
            hand_over(head).wait_recv()
            state[sub] = inbox[head]

    carried = [state[sub] for sub in range(PAIR)]
    pieces = [[None] * chunks for _ in range(PAIR)]
    for c in reversed(range(chunks)):
        at = c * CHUNK
        first = aux[at : at + CHUNK, 1:2]
        last = aux[at : at + CHUNK, 2:3]
        keep = aux[at + CHUNK - 1 : at + CHUNK, 1:2]
        subs = range(PAIR)
        parts = [inner[sub * chunks + c] for sub in subs]
        betas = [cut(heads[sub][3], c) for sub in subs]
        afters = [carried[sub].astype(BF16) for sub in subs]
        dnews = [
            parts[sub][2] + mm(last * cut(heads[sub][1], c), afters[sub]) for sub in subs
        ]
        backs = [t_mm(t_ref[sub, c], dnews[sub]) for sub in subs]
        dvs = [betas[sub] * backs[sub] for sub in subs]
        dreads = [(-(first * dvs[sub])).astype(BF16) for sub in subs]
        carried = [
            keep * carried[sub] + parts[sub][3] + t_mm(cut(lows[sub][1], c), dreads[sub])
            for sub in subs
        ]
        for sub in subs:
            kk, strict, _, _, dq, dk, gap = parts[sub]
            before, new = s_ref[sub, c], n_ref[sub, c]
            kc = cut(lows[sub][1], c)
            back = backs[sub]
            dsystem = jnp.where(strict, -mm_t(back, new), 0.0)
            dbeta = jnp.sum(back * gap + dsystem * kk, -1, keepdims=True)
            grow = (betas[sub] * dsystem).astype(BF16)
            dk = (
                dk
                + last * mm_t(new, afters[sub])
                + mm_t(dreads[sub], before)
                + mm(grow, kc)
                + t_mm(grow, kc)
            )
            pieces[sub][c] = (dq, dk, dvs[sub], dbeta)

    @pl.when(mine == 1)
    def _():
        for sub in range(PAIR):
            head = step * PAIR + sub
            outbox[head] = carried[sub]
            hand_over(head).start()

    lane_ids = lax.broadcasted_iota(jnp.int32, (tokens, WIDTH), 1)
    for sub in range(PAIR):
        head = step * PAIR + sub
        q, k, acts, beta, mixes, sigs, rho_q, rho_k, dout = heads[sub]
        dq, dk, dv, dbeta = (
            jnp.concatenate([pieces[sub][c][item] for c in range(chunks)], 0)
            for item in range(4)
        )
        dbl_ref[...] += jnp.where(lane_ids == head, dbeta * beta * (1.0 - beta), 0.0)
        dq = dq * WIDTH ** (-0.5)
        dacts = (
            rho_q * dq
            - acts[0] * (rho_q * rho_q * rho_q) * jnp.sum(acts[0] * dq, -1, keepdims=True),
            rho_k * dk
            - acts[1] * (rho_k * rho_k * rho_k) * jnp.sum(acts[1] * dk, -1, keepdims=True),
            dv,
        )
        for index in range(3):
            sig = sigs[index]
            dmix = dacts[index] * sig * (1.0 + mixes[index] * (1.0 - sig))
            extended[sub, index, 0:tokens] = dmix
            tailbox[head, index] = dmix[0:8]

    @pl.when(mine == 1)
    def _():
        extended[:, :, tokens : tokens + 8] = jnp.zeros((PAIR, 3, 8, WIDTH), F32)
        for sub in range(PAIR):
            hand_tail(step * PAIR + sub).start()

    @pl.when(mine == 0)
    def _():
        for sub in range(PAIR):
            head = step * PAIR + sub
            hand_tail(head).wait_recv()
            extended[sub, :, tokens : tokens + 8] = headbox[head]

    later = [None] + [aux[:, 5 + off : 6 + off] for off in range(1, TAPS)]
    for sub in range(PAIR):
        lanes = slice(sub * WIDTH, (sub + 1) * WIDTH)
        taps = taps_ref[:, lanes]
        for index in range(3):
            row = index * TAPS
            dmix = extended[sub, index, 0:tokens]
            dlin = dmix * taps[row : row + 1]
            dtaps_ref[row : row + 1, lanes] = jnp.sum(
                dmix * lin_ref[0, HALO : HALO + tokens, third(sub, index)], 0, keepdims=True
            )
            for off in range(1, TAPS):
                dlin = dlin + taps[row + off : row + off + 1] * (
                    extended[sub, index, off : off + tokens] * later[off]
                )
                dtaps_ref[row + off : row + off + 1, lanes] = jnp.sum(
                    dmix
                    * keeps[off]
                    * lin_ref[0, HALO - off : HALO - off + tokens, third(sub, index)],
                    0,
                    keepdims=True,
                )
            dlin_ref[0, :, third(sub, index)] = dlin.astype(BF16)
        dtaps_ref[12:16, lanes] = jnp.zeros((4, WIDTH), F32)

    if moves:

        @pl.when(step == pl.num_programs(0) - 1)
        def _():
            done = outbox.shape[0] // PAIR * MOVES
            lax.fori_loop(done, moves.steps, lambda i, _: (moves.step(i), 0)[1], 0)
            moves.finish()

    @pl.when((step == pl.num_programs(0) - 1) & (mine == 1))
    def _():
        for head in range(outbox.shape[0]):
            hand_over(head).wait_send()
            hand_tail(head).wait_send()


def mixer_fwd(linear, aux, seg_row, taps, gain):
    halves, rows, cols = linear.shape
    tokens = rows - HALO
    half_heads = cols // 3 // WIDTH
    heads = halves * half_heads
    per_half = half_heads // PAIR
    chunks = tokens // CHUNK
    lanes = PAIR * WIDTH

    def whole(shape):
        return pl.BlockSpec(shape, lambda i: (0,) * len(shape))

    token_spec = pl.BlockSpec((1, tokens, lanes), lambda i: (i // per_half, 0, i % per_half))
    square = pl.BlockSpec((PAIR, chunks, CHUNK, WIDTH), lambda i: (i, 0, 0, 0))
    square_shape = jax.ShapeDtypeStruct((heads, chunks, CHUNK, WIDTH), BF16)
    return pl.pallas_call(
        functools.partial(mixer_fwd_kernel, tokens),
        grid=(heads // PAIR,),
        in_specs=[
            pl.BlockSpec((1, rows, 3 * lanes), lambda i: (i // per_half, 0, i % per_half)),
            whole(aux.shape),
            whole(seg_row.shape),
            pl.BlockSpec((16, lanes), lambda i: (0, i)),
            whole(gain.shape),
        ],
        out_specs=[token_spec, token_spec, square, square, square],
        out_shape=[
            jax.ShapeDtypeStruct((halves, tokens, half_heads * WIDTH), BF16),
            jax.ShapeDtypeStruct((halves, tokens, half_heads * WIDTH), F32),
            square_shape,
            square_shape,
            square_shape,
        ],
        scratch_shapes=[
            pltpu.VMEM((PAIR, WIDTH, WIDTH), F32),
            pltpu.VMEM((heads, WIDTH, WIDTH), F32),
            pltpu.VMEM((heads, WIDTH, WIDTH), F32),
            pltpu.SemaphoreType.DMA((heads,)),
            pltpu.SemaphoreType.DMA((heads,)),
        ],
        compiler_params=pltpu.CompilerParams(
            collective_id=0, has_side_effects=True, vmem_limit_bytes=VMEM_LIMIT
        ),
        name="mixer_fwd",
    )(linear, aux, seg_row, taps, gain)


def mixer_bwd(linear, aux, seg_row, taps, gain, out, new, inverse, before, donb, grads, units):
    halves, rows, cols = linear.shape
    tokens = rows - HALO
    half_heads = cols // 3 // WIDTH
    heads = halves * half_heads
    per_half = half_heads // PAIR
    chunks = tokens // CHUNK
    lanes = PAIR * WIDTH

    def whole(shape):
        return pl.BlockSpec(shape, lambda i: (0,) * len(shape))

    token_spec = pl.BlockSpec((1, tokens, lanes), lambda i: (i // per_half, 0, i % per_half))
    square = pl.BlockSpec((PAIR, chunks, CHUNK, WIDTH), lambda i: (i, 0, 0, 0))
    taps_spec = pl.BlockSpec((16, lanes), lambda i: (0, i))
    tiles, grad_args, grad_specs, sum_shapes, boxes = None, [], [], [], []
    if on_grid():
        block_rows = grads.shape[1] // lax.axis_size("dp")
        tiles = split_tiles(grads.shape[2], block_rows, 2 * WIDTH)
        grad_args, grad_specs = [blocks_of(grads)], [pl.BlockSpec(memory_space=pl.ANY)]
        sum_shapes = [(block_rows, units)] * 3 + [(block_rows, grads.shape[2] - 3 * units)]
        boxes = Scatter.boxes(tiles, [grads.dtype]) + Scatter.sems(tiles)
    results = pl.pallas_call(
        functools.partial(mixer_bwd_kernel, tokens, tiles),
        grid=(heads // PAIR,),
        in_specs=[
            pl.BlockSpec((1, rows, 3 * lanes), lambda i: (i // per_half, 0, i % per_half)),
            whole(aux.shape),
            whole(seg_row.shape),
            taps_spec,
            whole(gain.shape),
            token_spec,
            square,
            square,
            square,
            token_spec,
        ]
        + grad_specs,
        out_specs=[
            pl.BlockSpec((1, tokens, 3 * lanes), lambda i: (i // per_half, 0, i % per_half)),
            whole((tokens, WIDTH)),
            taps_spec,
            whole((8, WIDTH)),
        ]
        + [whole(shape) for shape in sum_shapes],
        out_shape=[
            jax.ShapeDtypeStruct((halves, tokens, cols), BF16),
            jax.ShapeDtypeStruct((tokens, WIDTH), F32),
            jax.ShapeDtypeStruct((16, heads * WIDTH), F32),
            jax.ShapeDtypeStruct((8, WIDTH), F32),
        ]
        + [jax.ShapeDtypeStruct(shape, F32) for shape in sum_shapes],
        scratch_shapes=[
            pltpu.VMEM((PAIR, WIDTH, WIDTH), F32),
            pltpu.VMEM((PAIR, 3, tokens + 8, WIDTH), F32),
            pltpu.VMEM((heads, WIDTH, WIDTH), F32),
            pltpu.VMEM((heads, WIDTH, WIDTH), F32),
            pltpu.VMEM((heads, 3, 8, WIDTH), F32),
            pltpu.VMEM((heads, 3, 8, WIDTH), F32),
            pltpu.SemaphoreType.DMA((heads,)),
            pltpu.SemaphoreType.DMA((heads,)),
            pltpu.SemaphoreType.DMA((heads,)),
            pltpu.SemaphoreType.DMA((heads,)),
        ]
        + boxes,
        compiler_params=pltpu.CompilerParams(
            collective_id=1, has_side_effects=True, vmem_limit_bytes=VMEM_LIMIT
        ),
        name="mixer_bwd",
    )(linear, aux, seg_row, taps, gain, out, new, inverse, before, donb, *grad_args)
    if tiles:
        return results
    second = plain_scatter(grads)
    return list(results) + list(apart(second[:, : 3 * units], 3)) + [second[:, 3 * units :]]


def mlp_kernel(
    count, inputs_ref, onb_ref, weight_ref, *refs,
):
    wo_refs, refs = refs[:4], refs[4:]
    gain_ref, mask_ref, teacher_ref, cot_ref, coef_ref = refs[:5]
    out_ref, square_ref, grad_ref, donb_ref, dhidden_ref, dgain_ref = refs[5:11]
    hidden, normed, normed_t, total, dtotal, dmlp, dmlp_t, gates, uppers, inners = refs[11:]
    step = pl.program_id(0)
    unit = WIDTH

    def out_weight(half):
        return jnp.concatenate([ref[half] for ref in wo_refs], 1)

    def rho_of(values):
        return lax.rsqrt(jnp.mean(values * values, -1, keepdims=True) + 1e-05)

    def spans(first, parts):
        return [weight_ref[half, :, (first + part) * unit : (first + part + 1) * unit]
                for half in range(2) for part in range(parts)]

    @pl.when(step == 0)
    def _():
        rows = inputs_ref[...].astype(F32)
        for half in range(2):
            rows = rows + mm_t(onb_ref[half], out_weight(half))
        hidden[...] = rows
        xn = rows * rho_of(rows) * gain_ref[0:1]
        normed[...] = xn.astype(BF16)
        normed_t[...] = xn.astype(BF16).T
        total[...] = jnp.zeros_like(total)

    @pl.when(step < count)
    def _():
        both_w = jnp.concatenate(spans(0, 2), 1)
        gu = mm(normed[...], both_w)
        gate = jnp.concatenate([gu[:, 0:unit], gu[:, 2 * unit : 3 * unit]], 1)
        upper = jnp.concatenate([gu[:, unit : 2 * unit], gu[:, 3 * unit :]], 1)
        gates[step] = gate
        uppers[step] = upper
        inner = (gate * jax.nn.sigmoid(gate) * upper).astype(BF16)
        inners[step] = inner
        total[...] += mm_t(inner, jnp.concatenate(spans(2, 1), 1))

    @pl.when(step == count - 1)
    def _():
        rows = hidden[...] + total[...]
        out_ref[...] = rows.astype(BF16)
        differ = rows - teacher_ref[...].astype(F32)
        masked = mask_ref[...] * differ
        square_ref[...] = jnp.sum(
            jnp.sum(masked * differ, 1, keepdims=True), 0, keepdims=True
        )
        dout = cot_ref[...].astype(F32) + masked * coef_ref[0:1, 0:1]
        dhidden_ref[...] = dout
        dmlp[...] = dout.astype(BF16)
        dmlp_t[...] = dout.astype(BF16).T
        dtotal[...] = jnp.zeros_like(dtotal)

    @pl.when((step >= count) & (step < 2 * count))
    def _():
        tile = step - count
        dinner = mm(dmlp[...], jnp.concatenate(spans(2, 1), 1))
        gate, upper = gates[tile], uppers[tile]
        sig = jax.nn.sigmoid(gate)
        dgate = (dinner * upper * sig * (1.0 + gate * (1.0 - sig))).astype(BF16)
        dupper = (dinner * (gate * sig)).astype(BF16)
        dgu = jnp.concatenate(
            [dgate[:, :unit], dupper[:, :unit], dgate[:, unit:], dupper[:, unit:]], 1
        )
        dtotal[...] += mm_t(dgu, jnp.concatenate(spans(0, 2), 1))
        grown = mm(normed_t[...], dgu).astype(BF16)
        down = mm(dmlp_t[...], inners[tile]).astype(BF16)

        for half in range(2):
            grad_ref[half, :, : 2 * unit] = grown[:, half * 2 * unit : (half + 1) * 2 * unit]
            grad_ref[half, :, 2 * unit :] = down[:, half * unit : (half + 1) * unit]

    @pl.when(step == 2 * count)
    def _():
        rows = hidden[...]
        rho = rho_of(rows)
        unit_rows = rows * rho
        drows = dtotal[...]
        du = drows * gain_ref[0:1]
        dgain_ref[...] = jnp.sum(drows * unit_rows, 0, keepdims=True)
        dh = dhidden_ref[...] + rho * (du - unit_rows * jnp.mean(du * unit_rows, -1, keepdims=True))
        dhidden_ref[...] = dh
        dattn = dh.astype(BF16)
        dmlp_t[...] = dattn.T
        for half in range(2):
            donb_ref[half] = mm(dattn, out_weight(half))
            grad_ref[half] = mm(dmlp_t[...], onb_ref[half, :, : 3 * unit]).astype(BF16)

    @pl.when(step == 2 * count + 1)
    def _():
        for half in range(2):
            grad_ref[half, :, :unit] = mm(dmlp_t[...], onb_ref[half, :, 3 * unit :]).astype(BF16)


def mlp(inputs, onb, mixer_weights, weights, gain, mask, teacher, cotangent, coef):
    tokens, width_d = inputs.shape
    halves, _, cols = weights.shape
    half_cols = onb.shape[2]
    count = cols // (3 * WIDTH)
    first_out = (mixer_weights.shape[2] - half_cols) // WIDTH

    def whole(shape):
        return pl.BlockSpec(shape, lambda i: (0,) * len(shape))

    def tile(i):
        return (0, 0, jnp.where(i < count, i, jnp.minimum(i - count, count - 1)))

    wide = (halves, width_d, 3 * WIDTH)
    return pl.pallas_call(
        functools.partial(mlp_kernel, count),
        grid=(2 * count + 2,),
        in_specs=[whole(inputs.shape), whole(onb.shape), pl.BlockSpec(wide, tile)]
        + [
            pl.BlockSpec((halves, width_d, WIDTH), functools.partial(lambda n, i: (0, 0, n), first_out + n))
            for n in range(4)
        ]
        + [whole(gain.shape), whole(mask.shape), whole(teacher.shape), whole(cotangent.shape), whole(coef.shape)],
        out_specs=[
            whole((tokens, width_d)),
            whole((1, 1)),
            pl.BlockSpec(wide, lambda i: (0, 0, jnp.maximum(i - count, 0))),
            whole((halves, tokens, half_cols)),
            whole((tokens, width_d)),
            whole((1, width_d)),
        ],
        out_shape=[
            jax.ShapeDtypeStruct((tokens, width_d), BF16),
            jax.ShapeDtypeStruct((1, 1), F32),
            jax.ShapeDtypeStruct((halves, width_d, cols + half_cols), BF16),
            jax.ShapeDtypeStruct((halves, tokens, half_cols), F32),
            jax.ShapeDtypeStruct((tokens, width_d), F32),
            jax.ShapeDtypeStruct((1, width_d), F32),
        ],
        scratch_shapes=[
            pltpu.VMEM((tokens, width_d), F32),
            pltpu.VMEM((tokens, width_d), BF16),
            pltpu.VMEM((width_d, tokens), BF16),
            pltpu.VMEM((tokens, width_d), F32),
            pltpu.VMEM((tokens, width_d), F32),
            pltpu.VMEM((tokens, width_d), BF16),
            pltpu.VMEM((width_d, tokens), BF16),
            pltpu.VMEM((count, tokens, 2 * WIDTH), F32),
            pltpu.VMEM((count, tokens, 2 * WIDTH), F32),
            pltpu.VMEM((count, tokens, 2 * WIDTH), BF16),
        ],
        compiler_params=pltpu.CompilerParams(vmem_limit_bytes=VMEM_LIMIT),
        name="mlp",
    )(inputs, onb, weights, *[mixer_weights] * 4, gain, mask, teacher, cotangent, coef)


def project_back_kernel(
    dlin_ref, weight_ref, inputs_ref, gain_ref, dbl_ref, beta_ref, dhidden_ref,
    grad_ref, dinput_ref, dgain_ref, dbeta_ref,
    normed_t, total,
):
    step = pl.program_id(0)

    def unit():
        rows = inputs_ref[...].astype(F32)
        rho = lax.rsqrt(jnp.mean(rows * rows, -1, keepdims=True) + 1e-05)
        return rows * rho, rho

    @pl.when(step == 0)
    def _():
        normed_t[...] = (unit()[0] * gain_ref[0:1]).astype(BF16).T
        dbl = dbl_ref[...].astype(BF16)
        total[...] = mm_t(dbl, beta_ref[...])
        dbeta_ref[...] = mm(normed_t[...], dbl)

    total[...] += mm_t(dlin_ref[0], weight_ref[0])
    grad_ref[0] = mm(normed_t[...], dlin_ref[0]).astype(BF16)

    @pl.when(step == pl.num_programs(0) - 1)
    def _():
        rows, rho = unit()
        drows = total[...]
        du = drows * gain_ref[0:1]
        dgain_ref[...] = jnp.sum(drows * rows, 0, keepdims=True)
        dinput_ref[...] = dhidden_ref[...] + rho * (
            du - rows * jnp.mean(du * rows, -1, keepdims=True)
        )


def project_back(dlin, weights, inputs, gain, dbl, beta_w, dhidden):
    halves, tokens, cols = dlin.shape
    width_d = inputs.shape[1]
    kinds = 2
    part = cols // kinds

    def whole(shape):
        return pl.BlockSpec(shape, lambda i: (0,) * len(shape))

    columns = pl.BlockSpec((1, width_d, part), lambda i: (i // kinds, 0, i % kinds))
    return pl.pallas_call(
        project_back_kernel,
        grid=(halves * kinds,),
        in_specs=[
            pl.BlockSpec((1, tokens, part), lambda i: (i // kinds, 0, i % kinds)),
            columns,
            whole(inputs.shape),
            whole(gain.shape),
            whole(dbl.shape),
            whole(beta_w.shape),
            whole(dhidden.shape),
        ],
        out_specs=[columns, whole(dhidden.shape), whole((1, width_d)), whole((width_d, WIDTH))],
        out_shape=[
            jax.ShapeDtypeStruct((halves, width_d, cols), BF16),
            jax.ShapeDtypeStruct((tokens, width_d), F32),
            jax.ShapeDtypeStruct((1, width_d), F32),
            jax.ShapeDtypeStruct((width_d, WIDTH), F32),
        ],
        scratch_shapes=[
            pltpu.VMEM((width_d, tokens), BF16),
            pltpu.VMEM((tokens, width_d), F32),
        ],
        compiler_params=pltpu.CompilerParams(vmem_limit_bytes=VMEM_LIMIT),
        name="project_back",
    )(dlin, weights, inputs, gain, dbl, beta_w, dhidden)


def finish_kernel(count, *refs):
    for source, ref in zip(refs[:count], refs[count:]):
        ref[...] = source[...]


def finish(*sums):
    return pl.pallas_call(
        functools.partial(finish_kernel, len(sums)),
        out_shape=[jax.ShapeDtypeStruct(a.shape, F32) for a in sums],
        name="finish",
    )(*sums)


def mixer_tables(segments, length, beta, tokens):
    mine = lax.axis_index("tensor")
    seg = segments[0]
    position = jnp.arange(length)

    def behind(off):
        return jnp.where(position >= off, jnp.roll(seg, off), -1)

    ends = jnp.repeat(seg[CHUNK - 1 :: CHUNK], CHUNK)
    previous = jnp.where(position >= CHUNK, jnp.roll(ends, CHUNK), -1)
    columns = [seg, seg == previous, seg == ends]
    keeps = [behind(off) == seg for off in range(1, TAPS)]
    columns += keeps
    for off in range(1, TAPS):
        columns.append(jnp.where(position < length - off, jnp.roll(keeps[off - 1], -off), False))
    table = jnp.stack([c.astype(F32) for c in columns], 1)
    table = lax.dynamic_slice_in_dim(table, mine * tokens, tokens, 0)
    aux = jnp.concatenate(
        [
            table,
            jnp.zeros((tokens, 16 - table.shape[1]), F32),
            beta,
            jnp.zeros((tokens, WIDTH - 16 - beta.shape[1]), F32),
        ],
        1,
    )
    row = lax.dynamic_slice_in_dim(seg.astype(F32), mine * tokens, tokens, 0)
    return aux, row[None]


def by_thirds(first, second, third_one):
    rows = first.shape[0]
    tiles = jnp.stack([a.reshape(rows, -1, WIDTH) for a in (first, second, third_one)], 2)
    return tiles.reshape(rows, -1)


def apart(values, count):
    rows = values.shape[0]
    tiles = values.reshape(rows, -1, count, WIDTH)
    return tuple(tiles[:, :, i].reshape(rows, -1) for i in range(count))


def padded_rows(parts, multiple):
    flat = jnp.concatenate([p.reshape(-1) for p in parts])
    size = -(-flat.shape[0] // (multiple * WIDTH)) * multiple * WIDTH
    return jnp.pad(flat, (0, size - flat.shape[0])).reshape(-1, WIDTH)


def local(
    layer_input, segments, valid_mask, teacher, out_grad, norm_gain, w_query, w_key, w_value,
    w_beta, conv_weight, head_gain, w_out, mlp_gain, w_gate, w_up, w_down,
):
    parts, halves = lax.axis_size("dp"), lax.axis_size("tensor")
    tokens, width_d = layer_input.shape[1:]
    length = segments.shape[1]
    tokens_all = tokens * parts * halves
    half_heads = w_beta.shape[1]
    heads = half_heads * halves
    half_cols = w_query.shape[1]
    rows = w_query.shape[0]
    inputs_low = layer_input[0]

    valid = jnp.sum(valid_mask)
    counts = jnp.stack([valid // 64, valid % 64]).astype(BF16)
    small_parts = [w_beta, conv_weight, norm_gain, mlp_gain, head_gain, counts]
    small = padded_rows(small_parts, 16)
    first_shard = jnp.concatenate([by_thirds(w_query, w_key, w_value), w_out.T], 1)
    second_shard = by_thirds(w_gate, w_up, w_down.T)
    first_w, small = gather(
        [first_shard, small],
        split_tiles(first_shard.shape[1], rows)
        + [Tiles(1, "zxy", 0, small.shape[0], 0, WIDTH, WIDTH, 1, 0)],
        2,
    )
    second_w = lax.all_gather(second_shard, ("tensor", "dp"), axis=0, tiled=True).reshape(
        halves, width_d, second_shard.shape[1]
    )

    small = small.reshape(halves, parts, -1)
    marks = [0]
    for part in small_parts:
        marks.append(marks[-1] + part.size)
    beta_w, conv_w, gain_one, gain_two, gain_head, counts = (
        small[:, :, marks[i] : marks[i + 1]] for i in range(len(small_parts))
    )
    beta_w = beta_w.reshape(halves, width_d, half_heads).transpose(1, 0, 2).reshape(width_d, heads)
    beta_w = jnp.pad(beta_w, ((0, 0), (0, WIDTH - heads)))
    taps = conv_w.reshape((halves, parts) + conv_weight.shape).transpose(2, 3, 0, 4, 1, 5)
    taps = taps.reshape(12, heads * WIDTH).astype(F32)
    taps = jnp.concatenate([taps, jnp.zeros((4, heads * WIDTH), F32)], 0)
    gain_one = gain_one[0].reshape(1, width_d).astype(F32)
    gain_two = gain_two[0].reshape(1, width_d).astype(F32)
    gain_head = gain_head[0].reshape(1, WIDTH).astype(F32)
    counts = jnp.sum(counts.astype(F32), (0, 1))
    valid_sum = counts[0] * 64.0 + counts[1]

    halo = lax.ppermute(inputs_low[-HALO:], "tensor", [(0, 1), (1, 0)])
    spread = jnp.concatenate([halo, inputs_low], 0).astype(F32)
    rho_one = lax.rsqrt(jnp.mean(spread * spread, -1, keepdims=True) + 1e-05)
    spread = (spread * rho_one * gain_one[0:1]).astype(BF16)
    linear = jnp.einsum(
        "td,jdc->jtc", spread, first_w[:, :, : 3 * half_cols], preferred_element_type=F32
    )
    strength = jax.nn.sigmoid(
        jnp.dot(spread[HALO:], beta_w[:, :heads], preferred_element_type=F32)
    )
    aux, seg_row = mixer_tables(segments, length, strength, tokens)
    onb, out, new, inverse, before = mixer_fwd(linear, aux, seg_row, taps, gain_head)
    coef = ((tokens_all / 4.0) / valid_sum).reshape(1, 1)
    mask = valid_mask[0].astype(F32)[:, None]
    outputs, squares, second_g, donb, d_hidden, grad_gain_two = mlp(
        inputs_low, onb, first_w, second_w, gain_two, mask, teacher[0], out_grad[0], coef
    )
    dlin, dbl, dtaps, dgain, g_gate, g_up, g_down, g_out = mixer_bwd(
        linear, aux, seg_row, taps, gain_head, out, new, inverse, before, donb,
        second_g, w_gate.shape[1],
    )
    first_g, d_input, grad_gain_one, grad_beta = project_back(
        dlin, first_w, inputs_low, gain_one, dbl, beta_w, d_hidden
    )

    def shares(values):
        return jnp.broadcast_to(values.reshape(1, parts, -1), (halves, parts, values.size // parts))

    tail_parts = [
        grad_beta[:, :heads].reshape(parts, rows, halves, half_heads).transpose(2, 0, 1, 3),
        dtaps[:12]
        .reshape(12, halves, half_heads, parts, WIDTH // parts)
        .transpose(1, 3, 0, 2, 4),
        shares(grad_gain_one),
        shares(grad_gain_two),
        shares(dgain[0]),
        jnp.broadcast_to(squares.reshape(1, 1, 1), (halves, parts, 1)),
    ]
    tail = jnp.concatenate([p.reshape(halves, parts, -1) for p in tail_parts], 2)
    tail_rows = -(-tail.shape[2] // (8 * WIDTH)) * 8
    tail = jnp.pad(tail, ((0, 0), (0, 0), (0, tail_rows * WIDTH - tail.shape[2])))
    g_query, g_key, g_value, tail = scatter(
        first_g, tail.reshape(halves, parts * tail_rows, WIDTH), 3
    )
    g_gate, g_up, g_down, g_out, g_query, g_key, g_value = finish(
        g_gate, g_up, g_down, g_out, g_query, g_key, g_value
    )
    tail = tail.reshape(-1)
    sizes = [w_beta.size, conv_weight.size, norm_gain.size, mlp_gain.size, head_gain.size, 1]
    cuts = [sum(sizes[:i]) for i in range(7)]
    g_beta, g_conv, g_one, g_two, g_head, squares = (tail[cuts[i] : cuts[i + 1]] for i in range(6))
    return (
        outputs[None],
        squares[0] / (width_d * valid_sum),
        d_input[None],
        g_one,
        g_query,
        g_key,
        g_value,
        g_beta.reshape(w_beta.shape),
        g_conv.reshape(conv_weight.shape),
        g_head,
        g_out.T,
        g_two,
        g_gate,
        g_up,
        g_down.T,
    )


def solution(mesh):
    in_specs = (
        P("dp", "tensor", None),
        P("dp", None),
        P("dp", "tensor"),
        P("dp", "tensor", None),
        P("dp", "tensor", None),
        P("dp"),
        P("dp", "tensor"),
        P("dp", "tensor"),
        P("dp", "tensor"),
        P("dp", "tensor"),
        P(None, None, "tensor", "dp"),
        P("dp"),
        P("tensor", "dp"),
        P("dp"),
        P("dp", "tensor"),
        P("dp", "tensor"),
        P("tensor", "dp"),
    )
    out_specs = (
        P("dp", "tensor", None),
        P(),
        P("dp", "tensor", None),
        P("dp"),
        P("dp", "tensor"),
        P("dp", "tensor"),
        P("dp", "tensor"),
        P("dp", "tensor"),
        P(None, None, "tensor", "dp"),
        P("dp"),
        P("tensor", "dp"),
        P("dp"),
        P("dp", "tensor"),
        P("dp", "tensor"),
        P("tensor", "dp"),
    )
    return jax.shard_map(local, mesh=mesh, in_specs=in_specs, out_specs=out_specs, check_vma=False)
```

```python
import collections
import functools

import jax
import jax.numpy as jnp
from jax import lax
from jax.experimental import pallas as pl
from jax.experimental.pallas import tpu as pltpu
from jax.sharding import PartitionSpec as P

F32, BF16 = jnp.float32, jnp.bfloat16
MESH = pl.DeviceIdType.MESH
CHUNK = 128
HALO = 16
WIDTH = 128
PAIR = 2
MOVES = 2
TAPS = 4
VMEM_LIMIT = 60 * 1024 * 1024

GRID = (4, 2, 2)
DEPTH = GRID[0] - 1 + 2
LAGS = DEPTH + 2
Tiles = collections.namedtuple(
    "Tiles", ["array", "order", "row", "rows", "col", "stride", "cols", "count", "start"]
)


def on_grid():
    return lax.axis_size("dp") == GRID[0] * GRID[1] * GRID[2] and lax.axis_size("tensor") == 2


def position():
    mine = lax.axis_index("dp")
    _, size_x, size_c = GRID
    return {
        "y": lax.axis_index("tensor"),
        "z": mine // (size_x * size_c),
        "x": (mine // size_c) % size_x,
        "c": mine % size_c,
    }


def device_of(at):
    _, size_x, size_c = GRID
    return {"dp": (at["z"] * size_x + at["x"]) * size_c + at["c"], "tensor": at["y"]}


def inside(z):
    return (z >= 0) & (z < GRID[0])


def across(at, link):
    axis, way = link
    return dict(at, z=at["z"] + way) if axis == "z" else dict(at, **{axis: 1 - at[axis]})


def greet_all(at):
    barrier = pltpu.get_barrier_semaphore()
    for link in (("x", 0), ("y", 0), ("c", 0)):
        pl.semaphore_signal(
            barrier, inc=1, device_id=device_of(across(at, link)), device_id_type=MESH
        )
    for way in (-1, 1):

        @pl.when(inside(at["z"] + way))
        def _():
            pl.semaphore_signal(
                barrier,
                inc=1,
                device_id=device_of(across(at, ("z", way))),
                device_id_type=MESH,
            )

    peers = 3 + inside(at["z"] - 1).astype(jnp.int32) + inside(at["z"] + 1).astype(jnp.int32)
    pl.semaphore_wait(barrier, peers)


def remote(src, dst, send_sem, recv_sem, to):
    return pltpu.make_async_remote_copy(
        src_ref=src, dst_ref=dst, send_sem=send_sem, recv_sem=recv_sem,
        device_id=device_of(to), device_id_type=MESH,
    )


def when(test, action):
    if test is None:
        action()
    else:
        pl.when(test)(action)


def both(first, second):
    if first is None or second is None:
        return second if first is None else first
    return first & second


def split_tiles(cols, rows, unit=WIDTH, array=0, start=0):
    half = rows // 2
    count = cols // (3 * unit)
    out = [
        Tiles(array, "zxy", 0, half, 0, 3 * unit, unit, count, start),
        Tiles(array, "zyx", half, half, 0, 3 * unit, unit, count, start),
        Tiles(array, "xzy", 0, half, unit, 3 * unit, 2 * unit, count, start),
        Tiles(array, "yzx", half, half, unit, 3 * unit, 2 * unit, count, start),
    ]
    rest = cols - 3 * unit * count
    if rest:
        out.append(Tiles(array, "xzy", 0, half, cols - rest, rest, rest, 1, start))
        out.append(Tiles(array, "yzx", half, half, cols - rest, rest, rest, 1, start))
    return out


def window(tile, group):
    start = tile.col + group * tile.stride
    if not isinstance(start, int):
        start = pl.multiple_of(start, 128)
    return pl.ds(tile.row, tile.rows), pl.ds(start, tile.cols)


def steps_of(tiles):
    return max(tile.start + tile.count for tile in tiles) + LAGS - 1


def first_slots(tiles):
    return [sum(tile.count for tile in tiles[:i]) for i in range(len(tiles))]


def order_of(tile):
    first, last = [axis for axis in tile.order if axis != "z"]
    return first, last, tile.order[0] == "z"


def distances():
    return range(1 - GRID[0], GRID[0])


def ways(distance):
    return (1, -1) if distance == 0 else ((1,) if distance < 0 else (-1,))


class Gather:
    def __init__(self, tiles, shards, fulls, sems):
        self.tiles, self.shards, self.fulls = tiles, shards, fulls
        self.send_sem, self.recv_sem, self.core_send, self.core_recv, self.own_sem = sems
        self.at = position()
        self.steps = steps_of(tiles)

    @staticmethod
    def sems(tiles, arrays):
        slots = sum(tile.count for tile in tiles)
        return [
            pltpu.SemaphoreType.DMA((len(tiles), 2, 4, GRID[0])),
            pltpu.SemaphoreType.DMA((slots, 3, GRID[0])),
            pltpu.SemaphoreType.DMA((slots,)),
            pltpu.SemaphoreType.DMA((slots,)),
            pltpu.SemaphoreType.DMA((arrays,)),
        ]

    def begin(self):
        at = self.at
        copies = [
            pltpu.make_async_copy(
                shard, full.at[at["y"], at["z"], at["x"], at["c"]], self.own_sem.at[i]
            )
            for i, (shard, full) in enumerate(zip(self.shards, self.fulls))
        ]
        for copy in copies:
            copy.start()
        greet_all(at)
        for copy in copies:
            copy.wait()

    def copy(self, index, group, slot, z, link, own=False):
        at, tile = self.at, self.tiles[index]
        first, last, z_first = order_of(tile)
        rows, cols = window(tile, group)
        pair = link == 3 or (link < 2 and not z_first)
        spot = {"y": at["y"], "x": at["x"]}
        if pair:
            spot[first] = slice(None)
        ref = self.fulls[tile.array].at[spot["y"], z, spot["x"], at["c"], rows, cols]
        to = ("z", 1 - 2 * link) if link < 2 else (first if link == 2 else last, 0)
        return remote(
            self.shards[tile.array].at[rows, cols] if own else ref,
            ref,
            self.send_sem.at[index, group % 2, link, z],
            self.recv_sem.at[slot, max(link - 1, 0), z],
            across(at, to),
        )

    def send(self, index, group, slot, z, link, own=False):
        def go():
            one = self.copy(index, group, slot, z, link, own)
            pl.when(group >= 2)(one.wait_send)
            one.start()

        when(inside(self.at["z"] + 1 - 2 * link) if link < 2 else None, go)

    def visit(self, index, group, slot, lag):
        at, tile = self.at, self.tiles[index]
        _, _, z_first = order_of(tile)
        offset = 0 if z_first else 1
        for far in distances():
            z = at["z"] + far

            def handle():
                if z_first and lag == abs(far):
                    if far:
                        self.copy(index, group, slot, z, 0).wait_recv()
                    for way in ways(far):
                        self.send(index, group, slot, z, (1 - way) // 2, far == 0)
                    self.send(index, group, slot, z, 2, far == 0)
                if z_first and lag == abs(far) + 1:
                    self.copy(index, group, slot, z, 2).wait_recv()
                    self.send(index, group, slot, z, 3)
                if not z_first and far == 0 and lag == 0:
                    self.send(index, group, slot, z, 2, True)
                if not z_first and lag == abs(far) + 1:
                    self.copy(index, group, slot, z, 0 if far else 2).wait_recv()
                    for way in ways(far):
                        self.send(index, group, slot, z, (1 - way) // 2)
                    self.send(index, group, slot, z, 3)
                if lag == abs(far) + 2:
                    self.copy(index, group, slot, z, 3).wait_recv()

            if any(lag == abs(far) + more for more in range(3)):
                when(inside(z) if far else None, handle)
        if lag >= DEPTH:
            rows, cols = window(tile, group)
            part = self.fulls[tile.array].at[:, :, :, at["c"], rows, cols]
            pair = remote(
                part, part, self.core_send.at[slot], self.core_recv.at[slot], across(at, ("c", 0))
            )
            pair.start() if lag == DEPTH else pair.wait()

    def step(self, step):
        for lag in range(LAGS):
            for index, (tile, first) in enumerate(zip(self.tiles, first_slots(self.tiles))):
                group = step - lag - tile.start
                pl.when((group >= 0) & (group < tile.count))(
                    functools.partial(self.visit, index, group, first + group, lag)
                )

    def finish(self):
        for index, tile in enumerate(self.tiles):
            _, _, z_first = order_of(tile)
            for group in range(max(0, tile.count - 2), tile.count):
                for far in distances():
                    z = self.at["z"] + far
                    here = inside(z) if far else None
                    for way in ways(far):
                        one = self.copy(index, group, 0, z, (1 - way) // 2)
                        when(both(here, inside(self.at["z"] + way)), one.wait_send)
                    if z_first or far == 0:
                        when(here, self.copy(index, group, 0, z, 2).wait_send)
                    when(here, self.copy(index, group, 0, z, 3).wait_send)


class Scatter:
    def __init__(self, tiles, grads, put, boxes, sems):
        self.tiles, self.grads, self.put = tiles, grads, put
        self.sums, self.pairs, self.from_z, self.from_first, self.from_last = (
            boxes[i * len(tiles) : (i + 1) * len(tiles)] for i in range(5)
        )
        self.send_sem, self.recv_sem, self.core_send, self.core_recv, self.own_sem = sems
        self.at = position()
        self.steps = steps_of(tiles)

    @staticmethod
    def boxes(tiles, dtypes):
        whole, from_z, from_first, from_last = [], [], [], []
        for tile in tiles:
            z_first = order_of(tile)[2]
            dtype, shape = dtypes[tile.array], (tile.rows, tile.cols)
            whole.append(pltpu.VMEM((tile.count, 2) + GRID[:2] + shape, dtype))
            from_z.append(
                pltpu.VMEM((tile.count, 2, GRID[0]) + (() if z_first else (2,)) + shape, dtype)
            )
            from_first.append(
                pltpu.VMEM((tile.count,) + ((GRID[0],) if z_first else ()) + shape, dtype)
            )
            from_last.append(pltpu.VMEM((tile.count, GRID[0], 2) + shape, dtype))
        return whole + whole + from_z + from_first + from_last

    @staticmethod
    def sems(tiles):
        slots = sum(tile.count for tile in tiles)
        return [
            pltpu.SemaphoreType.DMA((len(tiles), 2, 3, GRID[0])),
            pltpu.SemaphoreType.DMA((slots, 4, GRID[0])),
            pltpu.SemaphoreType.DMA((slots,)),
            pltpu.SemaphoreType.DMA((slots,)),
            pltpu.SemaphoreType.DMA((slots,)),
        ]

    def begin(self):
        greet_all(self.at)

    def spot(self, index, group, z, kind, other=False):
        first, last, z_first = order_of(self.tiles[index])
        spot = {"y": self.at["y"], "x": self.at["x"]}
        if kind == "last" or (kind == "z" and not z_first):
            spot[first] = slice(None)
        if other:
            axis = first if kind == "first" else last
            spot[axis] = 1 - self.at[axis]
        return (group, spot["y"], z, spot["x"])

    def copy(self, index, group, slot, z, kind, way=0):
        first, last, z_first = order_of(self.tiles[index])
        if kind == "z":
            label = (1 + way) // 2
            to, dst = ("z", way), self.from_z[index].at[group, label, z]
        elif kind == "first":
            label, to = 2, (first, 0)
            dst = self.from_first[index].at[(group, z) if z_first else group]
        else:
            label, to, dst = 3, (last, 0), self.from_last[index].at[group, z]
        return remote(
            self.sums[index].at[self.spot(index, group, z, kind, kind != "z")],
            dst,
            self.send_sem.at[index, group % 2, max(label - 1, 0), z],
            self.recv_sem.at[slot, label, z],
            across(self.at, to),
        )

    def send(self, index, group, slot, z, kind, way=0):
        one = self.copy(index, group, slot, z, kind, way)
        pl.when(group >= 2)(one.wait_send)
        one.start()

    def add(self, index, group, slot, z, kind, way=0):
        self.copy(index, group, slot, z, kind, -way).wait_recv()
        z_first = order_of(self.tiles[index])[2]
        if kind == "z":
            came = self.from_z[index][group, (1 - way) // 2, z]
        elif kind == "first":
            came = self.from_first[index][(group, z) if z_first else group]
        else:
            came = self.from_last[index][group, z]
        spot = self.spot(index, group, z, kind)
        total = self.sums[index][spot].astype(F32) + came.astype(F32)
        self.sums[index][spot] = total.astype(self.sums[index].dtype)

    def visit(self, index, group, slot, stage):
        at, tile = self.at, self.tiles[index]
        rows, cols = window(tile, group)
        grad, sums = self.grads[tile.array], self.sums[index]
        _, _, z_first = order_of(tile)
        if stage <= 1:
            pair = remote(
                grad.at[:, :, :, 1 - at["c"], rows, cols],
                self.pairs[index].at[group],
                self.core_send.at[slot],
                self.core_recv.at[slot],
                across(at, ("c", 0)),
            )
            own = pltpu.make_async_copy(
                grad.at[:, :, :, at["c"], rows, cols], sums.at[group], self.own_sem.at[slot]
            )
        if stage == 0:
            pair.start()
            own.start()
            return
        if stage == 1:
            own.wait()
            pair.wait()
            sums[group] = (
                sums[group].astype(F32) + self.pairs[index][group].astype(F32)
            ).astype(sums.dtype)
        lag = DEPTH + 1 - stage

        def along_z(z, far):
            for way in ways(far):
                pl.when(inside(at["z"] + way))(
                    functools.partial(self.add, index, group, slot, z, "z", way)
                )
            if far:
                self.send(index, group, slot, z, "z", 1 if far > 0 else -1)

        for far in distances():
            z = at["z"] + far

            def handle():
                if lag == abs(far) + 2:
                    self.send(index, group, slot, z, "last")
                if lag == abs(far) + 1:
                    self.add(index, group, slot, z, "last")
                    if z_first:
                        self.send(index, group, slot, z, "first")
                    else:
                        along_z(z, far)
                        if far == 0:
                            self.send(index, group, slot, z, "first")
                if lag == abs(far) and (z_first or far == 0):
                    self.add(index, group, slot, z, "first")
                    if z_first:
                        along_z(z, far)
                    if far == 0:
                        self.put(tile, group, sums[group, at["y"], at["z"], at["x"]].astype(F32))

            if any(lag == abs(far) + more for more in range(3)):
                when(inside(z) if far else None, handle)

    def step(self, step):
        for stage in range(LAGS):
            for index, (tile, first) in enumerate(zip(self.tiles, first_slots(self.tiles))):
                group = step - stage - tile.start
                pl.when((group >= 0) & (group < tile.count))(
                    functools.partial(self.visit, index, group, first + group, stage)
                )

    def finish(self):
        for index, tile in enumerate(self.tiles):
            z_first = order_of(tile)[2]
            for group in range(max(0, tile.count - 2), tile.count):
                for far in distances():
                    z = self.at["z"] + far
                    here = inside(z) if far else None
                    if far:
                        one = self.copy(index, group, 0, z, "z", 1 if far > 0 else -1)
                        when(here, one.wait_send)
                    if z_first or far == 0:
                        when(here, self.copy(index, group, 0, z, "first").wait_send)
                    when(here, self.copy(index, group, 0, z, "last").wait_send)


def run_all(moves):
    moves.begin()
    lax.fori_loop(0, moves.steps, lambda step, _: (moves.step(step), 0)[1], 0)
    moves.finish()


def gather_kernel(tiles, arrays, *refs):
    run_all(Gather(tiles, refs[:arrays], refs[arrays : 2 * arrays], refs[2 * arrays :]))


def gather(shards, tiles, ident):
    halves = lax.axis_size("tensor")
    if not on_grid():
        return [
            lax.all_gather(shard, ("tensor", "dp"), axis=0, tiled=False).reshape(
                (halves, -1) + shard.shape[1:]
            )
            for shard in shards
        ]
    hbm = pl.BlockSpec(memory_space=pl.ANY)
    arrays = len(shards)
    fulls = pl.pallas_call(
        functools.partial(gather_kernel, tiles, arrays),
        in_specs=[hbm] * arrays,
        out_specs=[hbm] * arrays,
        out_shape=[
            jax.ShapeDtypeStruct((halves,) + GRID + shard.shape, shard.dtype) for shard in shards
        ],
        scratch_shapes=Gather.sems(tiles, arrays),
        compiler_params=pltpu.CompilerParams(collective_id=ident, has_side_effects=True),
        name="gather",
    )(*shards)
    return [full.reshape(halves, -1, full.shape[-1]) for full in fulls]


def put_turns(turns, rest, columns):
    def put(tile, group, total):
        rows = pl.ds(tile.row, tile.rows)
        for i in range(tile.cols // WIDTH):
            piece = total[:, i * WIDTH : (i + 1) * WIDTH]
            at = tile.col // WIDTH + i
            column = at + group * (tile.stride // WIDTH)

            def inner():
                lanes = pl.multiple_of(lax.div(column, len(turns)) * WIDTH, WIDTH)
                turns[at % len(turns)][rows, pl.ds(lanes, WIDTH)] = piece

            if rest is None:
                inner()
                continue
            if tile.count > 1 or at < columns:
                pl.when(column < columns)(inner)

            @pl.when(column >= columns)
            def _():
                lanes = pl.multiple_of((column - columns) * WIDTH, WIDTH)
                rest[rows, pl.ds(lanes, WIDTH)] = piece

    return put


def scatter_kernel(tiles, first_ref, small_grad_ref, query, key, value, small_ref, *rest):
    boxes = 5 * len(tiles)
    turns = put_turns((query, key, value), None, 0)

    def put(tile, group, total):
        if tile.array == 1:
            small_ref[...] = total
        else:
            turns(tile, group, total)

    run_all(Scatter(tiles, [first_ref, small_grad_ref], put, rest[:boxes], rest[boxes:]))


def blocks_of(grad):
    return grad.reshape((2,) + GRID + (-1, grad.shape[-1]))


def plain_scatter(grad):
    return lax.psum_scatter(
        grad.reshape(-1, grad.shape[-1]), ("tensor", "dp"), scatter_dimension=0, tiled=True
    ).astype(F32)


def scatter(first, small, ident):
    rows = first.shape[1] // lax.axis_size("dp")
    if not on_grid():
        return apart(plain_scatter(first), 3) + (plain_scatter(small),)
    grads = [blocks_of(first), blocks_of(small)]
    tiles = split_tiles(first.shape[2], rows)
    small_rows = grads[1].shape[-2]
    tiles.append(Tiles(1, "zxy", 0, small_rows, 0, WIDTH, WIDTH, 1, 0))
    hbm = pl.BlockSpec(memory_space=pl.ANY)
    shapes = [(rows, first.shape[2] // 3)] * 3 + [(small_rows, WIDTH)]
    return pl.pallas_call(
        functools.partial(scatter_kernel, tiles),
        in_specs=[hbm] * 2,
        out_specs=[pl.BlockSpec(memory_space=pltpu.VMEM)] * len(shapes),
        out_shape=[jax.ShapeDtypeStruct(shape, F32) for shape in shapes],
        scratch_shapes=Scatter.boxes(tiles, [grad.dtype for grad in grads]) + Scatter.sems(tiles),
        compiler_params=pltpu.CompilerParams(
            collective_id=ident, has_side_effects=True, vmem_limit_bytes=VMEM_LIMIT
        ),
        name="scatter",
    )(*grads)


def contract(left, right, dim_left, dim_right):
    return lax.dot_general(
        left.astype(BF16),
        right.astype(BF16),
        (((dim_left,), (dim_right,)), ((), ())),
        preferred_element_type=F32,
    )


def mm(left, right):
    return contract(left, right, 1, 0)


def mm_t(left, right):
    return contract(left, right, 1, 1)


def t_mm(left, right):
    return contract(left, right, 0, 0)


def tri_inverses(systems):
    rows = lax.broadcasted_iota(jnp.int32, (CHUNK, CHUNK), 0)
    cols = lax.broadcasted_iota(jnp.int32, (CHUNK, CHUNK), 1)
    inverses = None
    size = 1
    while size < CHUNK:
        link = (
            (rows // (2 * size) == cols // (2 * size))
            & ((rows // size) % 2 == 1)
            & ((cols // size) % 2 == 0)
        )
        parts = [jnp.where(link, system, 0.0) for system in systems]
        if size == 1:
            eye = (rows == cols).astype(F32)
            inverses = [eye - part for part in parts]
        else:
            lows = [inverse.astype(BF16) for inverse in inverses]
            middles = [mm(part, low) for part, low in zip(parts, lows)]
            inverses = [
                inverse - mm(low, middle)
                for inverse, low, middle in zip(inverses, lows, middles)
            ]
        size *= 2
    return inverses


def conv_of(lin_ref, base, lanes, taps, row, keeps, tokens):
    total = lin_ref[0, base : base + tokens, lanes] * taps[row : row + 1]
    for off in range(1, TAPS):
        total = total + taps[row + off : row + off + 1] * (
            lin_ref[0, base - off : base - off + tokens, lanes] * keeps[off]
        )
    return total


def third(sub, index):
    first = (sub * 3 + index) * WIDTH
    return slice(first, first + WIDTH)


def head_column(aux, lane):
    lanes = lax.broadcasted_iota(jnp.int32, aux.shape, 1)
    return jnp.sum(jnp.where(lanes == lane, aux, 0.0), axis=1, keepdims=True)


def greet(partner):
    barrier = pltpu.get_barrier_semaphore()
    pl.semaphore_signal(
        barrier, inc=1, device_id={"tensor": partner}, device_id_type=MESH
    )
    pl.semaphore_wait(barrier, 1)


def chunk_masks(aux, seg_row, at):
    rows = lax.broadcasted_iota(jnp.int32, (CHUNK, CHUNK), 0)
    cols = lax.broadcasted_iota(jnp.int32, (CHUNK, CHUNK), 1)
    same = aux[at : at + CHUNK, 0:1] == seg_row[0:1, at : at + CHUNK]
    return same & (rows > cols), same & (rows >= cols)


def mixer_fwd_kernel(
    tokens, lin_ref, aux_ref, seg_ref, taps_ref, gain_ref,
    onb_ref, o_ref, n_ref, t_ref, s_ref,
    state, outbox, inbox, send_sem, recv_sem,
):
    step = pl.program_id(0)
    mine = lax.axis_index("tensor")
    chunks = tokens // CHUNK

    @pl.when(step == 0)
    def _():
        greet(1 - mine)

    def hand_over(head):
        return pltpu.make_async_remote_copy(
            src_ref=outbox.at[head],
            dst_ref=inbox.at[head],
            send_sem=send_sem.at[head],
            recv_sem=recv_sem.at[head],
            device_id={"tensor": 1 - mine},
            device_id_type=MESH,
        )

    aux = aux_ref[...]
    seg_row = seg_ref[...]
    keeps = [None] + [aux[:, 2 + off : 3 + off] for off in range(1, TAPS)]
    heads = []
    for sub in range(PAIR):
        lanes = slice(sub * WIDTH, (sub + 1) * WIDTH)
        taps = taps_ref[:, lanes]
        beta = head_column(aux, 16 + step * PAIR + sub)
        acts = []
        for index in range(3):
            mixed = conv_of(lin_ref, HALO, third(sub, index), taps, index * TAPS, keeps, tokens)
            acts.append(mixed * jax.nn.sigmoid(mixed))
        q = acts[0] * (
            lax.rsqrt(jnp.sum(acts[0] * acts[0], -1, keepdims=True) + 1e-06) * WIDTH ** (-0.5)
        )
        k = acts[1] * lax.rsqrt(jnp.sum(acts[1] * acts[1], -1, keepdims=True) + 1e-06)
        heads.append((q, k, acts[2], beta))
    spots = [(sub, c) for sub in range(PAIR) for c in range(chunks)]
    masks = [chunk_masks(aux, seg_row, c * CHUNK) for c in range(chunks)]

    def cut(values, c):
        return values[c * CHUNK : (c + 1) * CHUNK]

    lows = [(q.astype(BF16), k.astype(BF16)) for q, k, _, _ in heads]
    systems = [
        jnp.where(
            masks[c][0],
            cut(heads[sub][3], c) * mm_t(cut(lows[sub][1], c), cut(lows[sub][1], c)),
            0.0,
        )
        for sub, c in spots
    ]
    scores_of = [
        jnp.where(masks[c][1], mm_t(cut(lows[sub][0], c), cut(lows[sub][1], c)), 0.0).astype(BF16)
        for sub, c in spots
    ]
    inner = []
    for (sub, c), inverse, scores in zip(spots, tri_inverses(systems), scores_of):
        inverse = inverse.astype(BF16)
        t_ref[sub, c] = inverse
        inner.append((inverse, scores))

    @pl.when(mine == 0)
    def _():
        state[...] = jnp.zeros_like(state)

    @pl.when(mine == 1)
    def _():
        for sub in range(PAIR):
            head = step * PAIR + sub
            hand_over(head).wait_recv()
            state[sub] = inbox[head]

    carried = [state[sub] for sub in range(PAIR)]
    for c in range(chunks):
        at = c * CHUNK
        first = aux[at : at + CHUNK, 1:2]
        last = aux[at : at + CHUNK, 2:3]
        keep = aux[at + CHUNK - 1 : at + CHUNK, 1:2]
        subs = range(PAIR)
        befores = [carried[sub].astype(BF16) for sub in subs]
        reads = [
            mm(jnp.concatenate([cut(lows[sub][1], c), cut(lows[sub][0], c)], 0), befores[sub])
            for sub in subs
        ]
        news = [
            mm(
                inner[sub * chunks + c][0],
                cut(heads[sub][3], c) * (cut(heads[sub][2], c) - first * reads[sub][:CHUNK]),
            ).astype(BF16)
            for sub in subs
        ]
        carried = [
            keep * carried[sub] + t_mm(last * cut(heads[sub][1], c), news[sub]) for sub in subs
        ]
        outs = [
            first * reads[sub][CHUNK:] + mm(inner[sub * chunks + c][1], news[sub]) for sub in subs
        ]
        for sub in subs:
            s_ref[sub, c] = befores[sub]
            n_ref[sub, c] = news[sub]
            lanes = slice(sub * WIDTH, (sub + 1) * WIDTH)
            out = outs[sub]
            o_ref[0, at : at + CHUNK, lanes] = out
            scale = lax.rsqrt(jnp.mean(out * out, -1, keepdims=True) + 1e-05)
            onb_ref[0, at : at + CHUNK, lanes] = (out * scale * gain_ref[0:1]).astype(BF16)

    @pl.when(mine == 0)
    def _():
        for sub in range(PAIR):
            head = step * PAIR + sub
            outbox[head] = carried[sub]
            hand_over(head).start()

    @pl.when((step == pl.num_programs(0) - 1) & (mine == 0))
    def _():
        for head in range(outbox.shape[0]):
            hand_over(head).wait_send()


def mixer_bwd_kernel(
    tokens, tiles, lin_ref, aux_ref, seg_ref, taps_ref, gain_ref,
    o_ref, n_ref, t_ref, s_ref, donb_ref, *refs,
):
    moves = None
    if tiles:
        grads_ref, refs = refs[0], refs[1:]
    dlin_ref, dbl_ref, dtaps_ref, dgain_ref, *refs = refs
    if tiles:
        sums, refs = refs[:4], refs[4:]
    state, extended, outbox, inbox, tailbox, headbox = refs[:6]
    send_sem, recv_sem, tail_send, tail_recv, *refs = refs[6:]
    if tiles:
        boxes = 5 * len(tiles)
        columns = 3 * (sums[0].shape[1] // WIDTH)
        put = put_turns(sums[:3], sums[3], columns)
        moves = Scatter(tiles, [grads_ref], put, refs[:boxes], refs[boxes:])
    step = pl.program_id(0)
    mine = lax.axis_index("tensor")
    chunks = tokens // CHUNK

    @pl.when(step == 0)
    def _():
        if moves:
            moves.begin()
        else:
            greet(1 - mine)
        dbl_ref[...] = jnp.zeros_like(dbl_ref)
        dgain_ref[...] = jnp.zeros_like(dgain_ref)

    def hand_over(head):
        return pltpu.make_async_remote_copy(
            src_ref=outbox.at[head],
            dst_ref=inbox.at[head],
            send_sem=send_sem.at[head],
            recv_sem=recv_sem.at[head],
            device_id={"tensor": 1 - mine},
            device_id_type=MESH,
        )

    def hand_tail(head):
        return pltpu.make_async_remote_copy(
            src_ref=tailbox.at[head],
            dst_ref=headbox.at[head],
            send_sem=tail_send.at[head],
            recv_sem=tail_recv.at[head],
            device_id={"tensor": 1 - mine},
            device_id_type=MESH,
        )

    if moves:
        moves.step(step * MOVES)

    aux = aux_ref[...]
    seg_row = seg_ref[...]
    keeps = [None] + [aux[:tokens, 2 + off : 3 + off] for off in range(1, TAPS)]
    heads, inner = [], []
    for sub in range(PAIR):
        lanes = slice(sub * WIDTH, (sub + 1) * WIDTH)
        taps = taps_ref[:, lanes]
        beta = head_column(aux[:tokens], 16 + step * PAIR + sub)
        mixes, sigs, acts = [], [], []
        for index in range(3):
            mixed = conv_of(lin_ref, HALO, third(sub, index), taps, index * TAPS, keeps, tokens)
            mixes.append(mixed)
            sigs.append(jax.nn.sigmoid(mixed))
            acts.append(mixed * sigs[-1])
        rho_q = lax.rsqrt(jnp.sum(acts[0] * acts[0], -1, keepdims=True) + 1e-06)
        rho_k = lax.rsqrt(jnp.sum(acts[1] * acts[1], -1, keepdims=True) + 1e-06)
        q = acts[0] * (rho_q * WIDTH ** (-0.5))
        k = acts[1] * rho_k
        out = o_ref[0, :, lanes]
        don = donb_ref[0, :, lanes]
        scale = lax.rsqrt(jnp.mean(out * out, -1, keepdims=True) + 1e-05)
        dgain_ref[0:1] += jnp.sum(don * out * scale, 0, keepdims=True)
        du = don * gain_ref[0:1]
        dout = scale * du - out * (scale * scale * scale) * jnp.mean(
            out * du, -1, keepdims=True
        )
        heads.append((q, k, acts, beta, mixes, sigs, rho_q, rho_k, dout))
    spots = [(sub, c) for sub in range(PAIR) for c in range(chunks)]
    masks = [chunk_masks(aux, seg_row, c * CHUNK) for c in range(chunks)]
    firsts = [aux[c * CHUNK : (c + 1) * CHUNK, 1:2] for c in range(chunks)]

    def cut(values, c):
        return values[c * CHUNK : (c + 1) * CHUNK]

    lows = [
        (q.astype(BF16), k.astype(BF16), dout.astype(BF16))
        for q, k, _, _, _, _, _, _, dout in heads
    ]
    grams = [
        mm_t(jnp.concatenate([cut(lows[s][1], c), cut(lows[s][0], c)], 0), cut(lows[s][1], c))
        for s, c in spots
    ]
    turned = [
        mm_t(cut(lows[s][2], c), jnp.concatenate([n_ref[s, c], s_ref[s, c]], 0)) for s, c in spots
    ]
    scores_of = [
        jnp.where(masks[c][1], gram[CHUNK:], 0.0).astype(BF16)
        for (s, c), gram in zip(spots, grams)
    ]
    dscores_of = [
        jnp.where(masks[c][1], turn[:, :CHUNK], 0.0).astype(BF16)
        for (s, c), turn in zip(spots, turned)
    ]
    reads = [mm(cut(lows[s][1], c), s_ref[s, c]) for s, c in spots]
    pulls = [t_mm(scores, cut(lows[s][2], c)) for (s, c), scores in zip(spots, scores_of)]
    reaches = [
        t_mm(firsts[c] * cut(heads[s][0], c), cut(lows[s][2], c)) for s, c in spots
    ]
    dqs = [
        firsts[c] * turn[:, CHUNK:] + mm(dscores, cut(lows[s][1], c))
        for (s, c), turn, dscores in zip(spots, turned, dscores_of)
    ]
    dks = [t_mm(dscores, cut(lows[s][0], c)) for (s, c), dscores in zip(spots, dscores_of)]
    gaps = [
        cut(heads[s][2][2], c) - firsts[c] * read for (s, c), read in zip(spots, reads)
    ]
    inner = [
        (gram[:CHUNK], masks[c][0], pull, reach, dq, dk, gap)
        for (s, c), gram, pull, reach, dq, dk, gap in zip(
            spots, grams, pulls, reaches, dqs, dks, gaps
        )
    ]

    if moves:
        for more in range(1, MOVES):
            moves.step(step * MOVES + more)

    @pl.when(mine == 1)
    def _():
        state[...] = jnp.zeros_like(state)

    @pl.when(mine == 0)
    def _():
        for sub in range(PAIR):
            head = step * PAIR + sub
            hand_over(head).wait_recv()
            state[sub] = inbox[head]

    carried = [state[sub] for sub in range(PAIR)]
    pieces = [[None] * chunks for _ in range(PAIR)]
    for c in reversed(range(chunks)):
        at = c * CHUNK
        first = aux[at : at + CHUNK, 1:2]
        last = aux[at : at + CHUNK, 2:3]
        keep = aux[at + CHUNK - 1 : at + CHUNK, 1:2]
        subs = range(PAIR)
        parts = [inner[sub * chunks + c] for sub in subs]
        betas = [cut(heads[sub][3], c) for sub in subs]
        afters = [carried[sub].astype(BF16) for sub in subs]
        dnews = [
            parts[sub][2] + mm(last * cut(heads[sub][1], c), afters[sub]) for sub in subs
        ]
        backs = [t_mm(t_ref[sub, c], dnews[sub]) for sub in subs]
        dvs = [betas[sub] * backs[sub] for sub in subs]
        dreads = [(-(first * dvs[sub])).astype(BF16) for sub in subs]
        carried = [
            keep * carried[sub] + parts[sub][3] + t_mm(cut(lows[sub][1], c), dreads[sub])
            for sub in subs
        ]
        for sub in subs:
            kk, strict, _, _, dq, dk, gap = parts[sub]
            before, new = s_ref[sub, c], n_ref[sub, c]
            kc = cut(lows[sub][1], c)
            back = backs[sub]
            dsystem = jnp.where(strict, -mm_t(back, new), 0.0)
            dbeta = jnp.sum(back * gap + dsystem * kk, -1, keepdims=True)
            grow = (betas[sub] * dsystem).astype(BF16)
            dk = (
                dk
                + last * mm_t(new, afters[sub])
                + mm_t(dreads[sub], before)
                + mm(grow, kc)
                + t_mm(grow, kc)
            )
            pieces[sub][c] = (dq, dk, dvs[sub], dbeta)

    @pl.when(mine == 1)
    def _():
        for sub in range(PAIR):
            head = step * PAIR + sub
            outbox[head] = carried[sub]
            hand_over(head).start()

    lane_ids = lax.broadcasted_iota(jnp.int32, (tokens, WIDTH), 1)
    for sub in range(PAIR):
        head = step * PAIR + sub
        q, k, acts, beta, mixes, sigs, rho_q, rho_k, dout = heads[sub]
        dq, dk, dv, dbeta = (
            jnp.concatenate([pieces[sub][c][item] for c in range(chunks)], 0)
            for item in range(4)
        )
        dbl_ref[...] += jnp.where(lane_ids == head, dbeta * beta * (1.0 - beta), 0.0)
        dq = dq * WIDTH ** (-0.5)
        dacts = (
            rho_q * dq
            - acts[0] * (rho_q * rho_q * rho_q) * jnp.sum(acts[0] * dq, -1, keepdims=True),
            rho_k * dk
            - acts[1] * (rho_k * rho_k * rho_k) * jnp.sum(acts[1] * dk, -1, keepdims=True),
            dv,
        )
        for index in range(3):
            sig = sigs[index]
            dmix = dacts[index] * sig * (1.0 + mixes[index] * (1.0 - sig))
            extended[sub, index, 0:tokens] = dmix
            tailbox[head, index] = dmix[0:8]

    @pl.when(mine == 1)
    def _():
        extended[:, :, tokens : tokens + 8] = jnp.zeros((PAIR, 3, 8, WIDTH), F32)
        for sub in range(PAIR):
            hand_tail(step * PAIR + sub).start()

    @pl.when(mine == 0)
    def _():
        for sub in range(PAIR):
            head = step * PAIR + sub
            hand_tail(head).wait_recv()
            extended[sub, :, tokens : tokens + 8] = headbox[head]

    later = [None] + [aux[:, 5 + off : 6 + off] for off in range(1, TAPS)]
    for sub in range(PAIR):
        lanes = slice(sub * WIDTH, (sub + 1) * WIDTH)
        taps = taps_ref[:, lanes]
        for index in range(3):
            row = index * TAPS
            dmix = extended[sub, index, 0:tokens]
            dlin = dmix * taps[row : row + 1]
            dtaps_ref[row : row + 1, lanes] = jnp.sum(
                dmix * lin_ref[0, HALO : HALO + tokens, third(sub, index)], 0, keepdims=True
            )
            for off in range(1, TAPS):
                dlin = dlin + taps[row + off : row + off + 1] * (
                    extended[sub, index, off : off + tokens] * later[off]
                )
                dtaps_ref[row + off : row + off + 1, lanes] = jnp.sum(
                    dmix
                    * keeps[off]
                    * lin_ref[0, HALO - off : HALO - off + tokens, third(sub, index)],
                    0,
                    keepdims=True,
                )
            dlin_ref[0, :, third(sub, index)] = dlin.astype(BF16)
        dtaps_ref[12:16, lanes] = jnp.zeros((4, WIDTH), F32)

    if moves:

        @pl.when(step == pl.num_programs(0) - 1)
        def _():
            done = outbox.shape[0] // PAIR * MOVES
            lax.fori_loop(done, moves.steps, lambda i, _: (moves.step(i), 0)[1], 0)
            moves.finish()

    @pl.when((step == pl.num_programs(0) - 1) & (mine == 1))
    def _():
        for head in range(outbox.shape[0]):
            hand_over(head).wait_send()
            hand_tail(head).wait_send()


def mixer_fwd(linear, aux, seg_row, taps, gain):
    halves, rows, cols = linear.shape
    tokens = rows - HALO
    half_heads = cols // 3 // WIDTH
    heads = halves * half_heads
    per_half = half_heads // PAIR
    chunks = tokens // CHUNK
    lanes = PAIR * WIDTH

    def whole(shape):
        return pl.BlockSpec(shape, lambda i: (0,) * len(shape))

    token_spec = pl.BlockSpec((1, tokens, lanes), lambda i: (i // per_half, 0, i % per_half))
    square = pl.BlockSpec((PAIR, chunks, CHUNK, WIDTH), lambda i: (i, 0, 0, 0))
    square_shape = jax.ShapeDtypeStruct((heads, chunks, CHUNK, WIDTH), BF16)
    return pl.pallas_call(
        functools.partial(mixer_fwd_kernel, tokens),
        grid=(heads // PAIR,),
        in_specs=[
            pl.BlockSpec((1, rows, 3 * lanes), lambda i: (i // per_half, 0, i % per_half)),
            whole(aux.shape),
            whole(seg_row.shape),
            pl.BlockSpec((16, lanes), lambda i: (0, i)),
            whole(gain.shape),
        ],
        out_specs=[token_spec, token_spec, square, square, square],
        out_shape=[
            jax.ShapeDtypeStruct((halves, tokens, half_heads * WIDTH), BF16),
            jax.ShapeDtypeStruct((halves, tokens, half_heads * WIDTH), F32),
            square_shape,
            square_shape,
            square_shape,
        ],
        scratch_shapes=[
            pltpu.VMEM((PAIR, WIDTH, WIDTH), F32),
            pltpu.VMEM((heads, WIDTH, WIDTH), F32),
            pltpu.VMEM((heads, WIDTH, WIDTH), F32),
            pltpu.SemaphoreType.DMA((heads,)),
            pltpu.SemaphoreType.DMA((heads,)),
        ],
        compiler_params=pltpu.CompilerParams(
            collective_id=0, has_side_effects=True, vmem_limit_bytes=VMEM_LIMIT
        ),
        name="mixer_fwd",
    )(linear, aux, seg_row, taps, gain)


def mixer_bwd(linear, aux, seg_row, taps, gain, out, new, inverse, before, donb, grads, units):
    halves, rows, cols = linear.shape
    tokens = rows - HALO
    half_heads = cols // 3 // WIDTH
    heads = halves * half_heads
    per_half = half_heads // PAIR
    chunks = tokens // CHUNK
    lanes = PAIR * WIDTH

    def whole(shape):
        return pl.BlockSpec(shape, lambda i: (0,) * len(shape))

    token_spec = pl.BlockSpec((1, tokens, lanes), lambda i: (i // per_half, 0, i % per_half))
    square = pl.BlockSpec((PAIR, chunks, CHUNK, WIDTH), lambda i: (i, 0, 0, 0))
    taps_spec = pl.BlockSpec((16, lanes), lambda i: (0, i))
    tiles, grad_args, grad_specs, sum_shapes, boxes = None, [], [], [], []
    if on_grid():
        block_rows = grads.shape[1] // lax.axis_size("dp")
        tiles = split_tiles(grads.shape[2], block_rows, 2 * WIDTH)
        grad_args, grad_specs = [blocks_of(grads)], [pl.BlockSpec(memory_space=pl.ANY)]
        sum_shapes = [(block_rows, units)] * 3 + [(block_rows, grads.shape[2] - 3 * units)]
        boxes = Scatter.boxes(tiles, [grads.dtype]) + Scatter.sems(tiles)
    results = pl.pallas_call(
        functools.partial(mixer_bwd_kernel, tokens, tiles),
        grid=(heads // PAIR,),
        in_specs=[
            pl.BlockSpec((1, rows, 3 * lanes), lambda i: (i // per_half, 0, i % per_half)),
            whole(aux.shape),
            whole(seg_row.shape),
            taps_spec,
            whole(gain.shape),
            token_spec,
            square,
            square,
            square,
            token_spec,
        ]
        + grad_specs,
        out_specs=[
            pl.BlockSpec((1, tokens, 3 * lanes), lambda i: (i // per_half, 0, i % per_half)),
            whole((tokens, WIDTH)),
            taps_spec,
            whole((8, WIDTH)),
        ]
        + [whole(shape) for shape in sum_shapes],
        out_shape=[
            jax.ShapeDtypeStruct((halves, tokens, cols), BF16),
            jax.ShapeDtypeStruct((tokens, WIDTH), F32),
            jax.ShapeDtypeStruct((16, heads * WIDTH), F32),
            jax.ShapeDtypeStruct((8, WIDTH), F32),
        ]
        + [jax.ShapeDtypeStruct(shape, F32) for shape in sum_shapes],
        scratch_shapes=[
            pltpu.VMEM((PAIR, WIDTH, WIDTH), F32),
            pltpu.VMEM((PAIR, 3, tokens + 8, WIDTH), F32),
            pltpu.VMEM((heads, WIDTH, WIDTH), F32),
            pltpu.VMEM((heads, WIDTH, WIDTH), F32),
            pltpu.VMEM((heads, 3, 8, WIDTH), F32),
            pltpu.VMEM((heads, 3, 8, WIDTH), F32),
            pltpu.SemaphoreType.DMA((heads,)),
            pltpu.SemaphoreType.DMA((heads,)),
            pltpu.SemaphoreType.DMA((heads,)),
            pltpu.SemaphoreType.DMA((heads,)),
        ]
        + boxes,
        compiler_params=pltpu.CompilerParams(
            collective_id=1, has_side_effects=True, vmem_limit_bytes=VMEM_LIMIT
        ),
        name="mixer_bwd",
    )(linear, aux, seg_row, taps, gain, out, new, inverse, before, donb, *grad_args)
    if tiles:
        return results
    second = plain_scatter(grads)
    return list(results) + list(apart(second[:, : 3 * units], 3)) + [second[:, 3 * units :]]


def mlp_kernel(
    count, inputs_ref, onb_ref, weight_ref, *refs,
):
    wo_refs, refs = refs[:4], refs[4:]
    gain_ref, mask_ref, teacher_ref, cot_ref, coef_ref = refs[:5]
    out_ref, square_ref, grad_ref, donb_ref, dhidden_ref, dgain_ref = refs[5:11]
    hidden, normed, normed_t, total, dtotal, dmlp, dmlp_t, gates, uppers, inners = refs[11:]
    step = pl.program_id(0)
    unit = WIDTH

    def out_weight(half):
        return jnp.concatenate([ref[half] for ref in wo_refs], 1)

    def rho_of(values):
        return lax.rsqrt(jnp.mean(values * values, -1, keepdims=True) + 1e-05)

    def spans(first, parts):
        return [weight_ref[half, :, (first + part) * unit : (first + part + 1) * unit]
                for half in range(2) for part in range(parts)]

    @pl.when(step == 0)
    def _():
        rows = inputs_ref[...].astype(F32)
        for half in range(2):
            rows = rows + mm_t(onb_ref[half], out_weight(half))
        hidden[...] = rows
        xn = rows * rho_of(rows) * gain_ref[0:1]
        normed[...] = xn.astype(BF16)
        normed_t[...] = xn.astype(BF16).T
        total[...] = jnp.zeros_like(total)

    @pl.when(step < count)
    def _():
        both_w = jnp.concatenate(spans(0, 2), 1)
        gu = mm(normed[...], both_w)
        gate = jnp.concatenate([gu[:, 0:unit], gu[:, 2 * unit : 3 * unit]], 1)
        upper = jnp.concatenate([gu[:, unit : 2 * unit], gu[:, 3 * unit :]], 1)
        gates[step] = gate
        uppers[step] = upper
        inner = (gate * jax.nn.sigmoid(gate) * upper).astype(BF16)
        inners[step] = inner
        total[...] += mm_t(inner, jnp.concatenate(spans(2, 1), 1))

    @pl.when(step == count - 1)
    def _():
        rows = hidden[...] + total[...]
        out_ref[...] = rows.astype(BF16)
        differ = rows - teacher_ref[...].astype(F32)
        masked = mask_ref[...] * differ
        square_ref[...] = jnp.sum(
            jnp.sum(masked * differ, 1, keepdims=True), 0, keepdims=True
        )
        dout = cot_ref[...].astype(F32) + masked * coef_ref[0:1, 0:1]
        dhidden_ref[...] = dout
        dmlp[...] = dout.astype(BF16)
        dmlp_t[...] = dout.astype(BF16).T
        dtotal[...] = jnp.zeros_like(dtotal)

    @pl.when((step >= count) & (step < 2 * count))
    def _():
        tile = step - count
        dinner = mm(dmlp[...], jnp.concatenate(spans(2, 1), 1))
        gate, upper = gates[tile], uppers[tile]
        sig = jax.nn.sigmoid(gate)
        dgate = (dinner * upper * sig * (1.0 + gate * (1.0 - sig))).astype(BF16)
        dupper = (dinner * (gate * sig)).astype(BF16)
        dgu = jnp.concatenate(
            [dgate[:, :unit], dupper[:, :unit], dgate[:, unit:], dupper[:, unit:]], 1
        )
        dtotal[...] += mm_t(dgu, jnp.concatenate(spans(0, 2), 1))
        grown = mm(normed_t[...], dgu).astype(BF16)
        down = mm(dmlp_t[...], inners[tile]).astype(BF16)

        for half in range(2):
            grad_ref[half, :, : 2 * unit] = grown[:, half * 2 * unit : (half + 1) * 2 * unit]
            grad_ref[half, :, 2 * unit :] = down[:, half * unit : (half + 1) * unit]

    @pl.when(step == 2 * count)
    def _():
        rows = hidden[...]
        rho = rho_of(rows)
        unit_rows = rows * rho
        drows = dtotal[...]
        du = drows * gain_ref[0:1]
        dgain_ref[...] = jnp.sum(drows * unit_rows, 0, keepdims=True)
        dh = dhidden_ref[...] + rho * (du - unit_rows * jnp.mean(du * unit_rows, -1, keepdims=True))
        dhidden_ref[...] = dh
        dattn = dh.astype(BF16)
        dmlp_t[...] = dattn.T
        for half in range(2):
            donb_ref[half] = mm(dattn, out_weight(half))
            grad_ref[half] = mm(dmlp_t[...], onb_ref[half, :, : 3 * unit]).astype(BF16)

    @pl.when(step == 2 * count + 1)
    def _():
        for half in range(2):
            grad_ref[half, :, :unit] = mm(dmlp_t[...], onb_ref[half, :, 3 * unit :]).astype(BF16)


def mlp(inputs, onb, out_weights, weights, gain, mask, teacher, cotangent, coef):
    tokens, width_d = inputs.shape
    halves, _, cols = weights.shape
    half_cols = onb.shape[2]
    count = cols // (3 * WIDTH)

    def whole(shape):
        return pl.BlockSpec(shape, lambda i: (0,) * len(shape))

    def tile(i):
        return (0, 0, jnp.where(i < count, i, jnp.minimum(i - count, count - 1)))

    wide = (halves, width_d, 3 * WIDTH)
    return pl.pallas_call(
        functools.partial(mlp_kernel, count),
        grid=(2 * count + 2,),
        in_specs=[whole(inputs.shape), whole(onb.shape), pl.BlockSpec(wide, tile)]
        + [
            pl.BlockSpec((halves, width_d, WIDTH), functools.partial(lambda n, i: (0, 0, n), n))
            for n in range(4)
        ]
        + [whole(gain.shape), whole(mask.shape), whole(teacher.shape), whole(cotangent.shape), whole(coef.shape)],
        out_specs=[
            whole((tokens, width_d)),
            whole((1, 1)),
            pl.BlockSpec(wide, lambda i: (0, 0, jnp.maximum(i - count, 0))),
            whole((halves, tokens, half_cols)),
            whole((tokens, width_d)),
            whole((1, width_d)),
        ],
        out_shape=[
            jax.ShapeDtypeStruct((tokens, width_d), BF16),
            jax.ShapeDtypeStruct((1, 1), F32),
            jax.ShapeDtypeStruct((halves, width_d, cols + half_cols), BF16),
            jax.ShapeDtypeStruct((halves, tokens, half_cols), F32),
            jax.ShapeDtypeStruct((tokens, width_d), F32),
            jax.ShapeDtypeStruct((1, width_d), F32),
        ],
        scratch_shapes=[
            pltpu.VMEM((tokens, width_d), F32),
            pltpu.VMEM((tokens, width_d), BF16),
            pltpu.VMEM((width_d, tokens), BF16),
            pltpu.VMEM((tokens, width_d), F32),
            pltpu.VMEM((tokens, width_d), F32),
            pltpu.VMEM((tokens, width_d), BF16),
            pltpu.VMEM((width_d, tokens), BF16),
            pltpu.VMEM((count, tokens, 2 * WIDTH), F32),
            pltpu.VMEM((count, tokens, 2 * WIDTH), F32),
            pltpu.VMEM((count, tokens, 2 * WIDTH), BF16),
        ],
        compiler_params=pltpu.CompilerParams(vmem_limit_bytes=VMEM_LIMIT),
        name="mlp",
    )(inputs, onb, weights, *[out_weights] * 4, gain, mask, teacher, cotangent, coef)


def project_back_kernel(
    dlin_ref, weight_ref, inputs_ref, gain_ref, dbl_ref, beta_ref, dhidden_ref,
    grad_ref, dinput_ref, dgain_ref, dbeta_ref,
    normed_t, total,
):
    step = pl.program_id(0)

    def unit():
        rows = inputs_ref[...].astype(F32)
        rho = lax.rsqrt(jnp.mean(rows * rows, -1, keepdims=True) + 1e-05)
        return rows * rho, rho

    @pl.when(step == 0)
    def _():
        normed_t[...] = (unit()[0] * gain_ref[0:1]).astype(BF16).T
        dbl = dbl_ref[...].astype(BF16)
        total[...] = mm_t(dbl, beta_ref[...])
        dbeta_ref[...] = mm(normed_t[...], dbl)

    total[...] += mm_t(dlin_ref[0], weight_ref[0])
    grad_ref[0] = mm(normed_t[...], dlin_ref[0]).astype(BF16)

    @pl.when(step == pl.num_programs(0) - 1)
    def _():
        rows, rho = unit()
        drows = total[...]
        du = drows * gain_ref[0:1]
        dgain_ref[...] = jnp.sum(drows * rows, 0, keepdims=True)
        dinput_ref[...] = dhidden_ref[...] + rho * (
            du - rows * jnp.mean(du * rows, -1, keepdims=True)
        )


def project_back(dlin, weights, inputs, gain, dbl, beta_w, dhidden):
    halves, tokens, cols = dlin.shape
    width_d = inputs.shape[1]
    kinds = 2
    part = cols // kinds

    def whole(shape):
        return pl.BlockSpec(shape, lambda i: (0,) * len(shape))

    columns = pl.BlockSpec((1, width_d, part), lambda i: (i // kinds, 0, i % kinds))
    return pl.pallas_call(
        project_back_kernel,
        grid=(halves * kinds,),
        in_specs=[
            pl.BlockSpec((1, tokens, part), lambda i: (i // kinds, 0, i % kinds)),
            columns,
            whole(inputs.shape),
            whole(gain.shape),
            whole(dbl.shape),
            whole(beta_w.shape),
            whole(dhidden.shape),
        ],
        out_specs=[columns, whole(dhidden.shape), whole((1, width_d)), whole((width_d, WIDTH))],
        out_shape=[
            jax.ShapeDtypeStruct((halves, width_d, cols), BF16),
            jax.ShapeDtypeStruct((tokens, width_d), F32),
            jax.ShapeDtypeStruct((1, width_d), F32),
            jax.ShapeDtypeStruct((width_d, WIDTH), F32),
        ],
        scratch_shapes=[
            pltpu.VMEM((width_d, tokens), BF16),
            pltpu.VMEM((tokens, width_d), F32),
        ],
        compiler_params=pltpu.CompilerParams(vmem_limit_bytes=VMEM_LIMIT),
        name="project_back",
    )(dlin, weights, inputs, gain, dbl, beta_w, dhidden)


def finish_kernel(spans, count, small_ref, scale_ref, *refs):
    outs = refs[count:]
    for source, ref in zip(refs[:count], outs):
        ref[...] = source[...]
    for (start, size), ref in zip(spans, outs[count:]):
        row, lane = start // WIDTH, start % WIDTH
        ref[...] = small_ref[row : row + 1, lane : lane + size]
    outs[-1][...] = outs[-1][...] * scale_ref[...]


def finish(sums, small, spans, scale):
    shapes = [a.shape for a in sums] + [(1, size) for _, size in spans]
    return pl.pallas_call(
        functools.partial(finish_kernel, spans, len(sums)),
        out_shape=[jax.ShapeDtypeStruct(shape, F32) for shape in shapes],
        name="finish",
    )(small, scale, *sums)


def mixer_tables(segments, length, beta, tokens):
    mine = lax.axis_index("tensor")
    seg = segments[0]
    position = jnp.arange(length)

    def behind(off):
        return jnp.where(position >= off, jnp.roll(seg, off), -1)

    ends = jnp.repeat(seg[CHUNK - 1 :: CHUNK], CHUNK)
    previous = jnp.where(position >= CHUNK, jnp.roll(ends, CHUNK), -1)
    columns = [seg, seg == previous, seg == ends]
    keeps = [behind(off) == seg for off in range(1, TAPS)]
    columns += keeps
    for off in range(1, TAPS):
        columns.append(jnp.where(position < length - off, jnp.roll(keeps[off - 1], -off), False))
    table = jnp.stack([c.astype(F32) for c in columns], 1)
    table = lax.dynamic_slice_in_dim(table, mine * tokens, tokens, 0)
    aux = jnp.concatenate(
        [
            table,
            jnp.zeros((tokens, 16 - table.shape[1]), F32),
            beta,
            jnp.zeros((tokens, WIDTH - 16 - beta.shape[1]), F32),
        ],
        1,
    )
    row = lax.dynamic_slice_in_dim(seg.astype(F32), mine * tokens, tokens, 0)
    return aux, row[None]


def by_thirds(first, second, third_one):
    rows = first.shape[0]
    tiles = jnp.stack([a.reshape(rows, -1, WIDTH) for a in (first, second, third_one)], 2)
    return tiles.reshape(rows, -1)


def apart(values, count):
    rows = values.shape[0]
    tiles = values.reshape(rows, -1, count, WIDTH)
    return tuple(tiles[:, :, i].reshape(rows, -1) for i in range(count))


def padded_rows(parts, multiple):
    flat = jnp.concatenate([p.reshape(-1) for p in parts])
    size = -(-flat.shape[0] // (multiple * WIDTH)) * multiple * WIDTH
    return jnp.pad(flat, (0, size - flat.shape[0])).reshape(-1, WIDTH)


def local(
    layer_input, segments, valid_mask, teacher, out_grad, norm_gain, w_query, w_key, w_value,
    w_beta, conv_weight, head_gain, w_out, mlp_gain, w_gate, w_up, w_down,
):
    parts, halves = lax.axis_size("dp"), lax.axis_size("tensor")
    tokens, width_d = layer_input.shape[1:]
    length = segments.shape[1]
    tokens_all = tokens * parts * halves
    half_heads = w_beta.shape[1]
    heads = half_heads * halves
    half_cols = w_query.shape[1]
    rows = w_query.shape[0]
    inputs_low = layer_input[0]

    valid = jnp.sum(valid_mask)
    counts = jnp.stack([valid // 64, valid % 64]).astype(BF16)
    small_parts = [w_beta, conv_weight, norm_gain, mlp_gain, head_gain, counts]
    small = padded_rows(small_parts, 16)
    first_shard = by_thirds(w_query, w_key, w_value)
    second_shard = by_thirds(w_gate, w_up, w_down.T)
    tiles = split_tiles(first_shard.shape[1], rows)
    tiles += split_tiles(half_cols, rows, array=1, start=tiles[0].count)
    tiles.append(Tiles(2, "zxy", 0, small.shape[0], 0, WIDTH, WIDTH, 1, 0))
    first_w, out_w, small = gather([first_shard, w_out.T, small], tiles, 2)
    second_w = lax.all_gather(second_shard, ("tensor", "dp"), axis=0, tiled=True).reshape(
        halves, width_d, second_shard.shape[1]
    )

    small = small.reshape(halves, parts, -1)
    marks = [0]
    for part in small_parts:
        marks.append(marks[-1] + part.size)
    beta_w, conv_w, gain_one, gain_two, gain_head, counts = (
        small[:, :, marks[i] : marks[i + 1]] for i in range(len(small_parts))
    )
    beta_w = beta_w.reshape(halves, width_d, half_heads).transpose(1, 0, 2).reshape(width_d, heads)
    beta_w = jnp.pad(beta_w, ((0, 0), (0, WIDTH - heads)))
    taps = conv_w.reshape((halves, parts) + conv_weight.shape).transpose(2, 3, 0, 4, 1, 5)
    taps = taps.reshape(12, heads * WIDTH).astype(F32)
    taps = jnp.concatenate([taps, jnp.zeros((4, heads * WIDTH), F32)], 0)
    gain_one = gain_one[0].reshape(1, width_d).astype(F32)
    gain_two = gain_two[0].reshape(1, width_d).astype(F32)
    gain_head = gain_head[0].reshape(1, WIDTH).astype(F32)
    counts = jnp.sum(counts.astype(F32), (0, 1))
    valid_sum = counts[0] * 64.0 + counts[1]

    halo = lax.ppermute(inputs_low[-HALO:], "tensor", [(0, 1), (1, 0)])
    spread = jnp.concatenate([halo, inputs_low], 0).astype(F32)
    rho_one = lax.rsqrt(jnp.mean(spread * spread, -1, keepdims=True) + 1e-05)
    spread = (spread * rho_one * gain_one[0:1]).astype(BF16)
    linear = jnp.einsum("td,jdc->jtc", spread, first_w, preferred_element_type=F32)
    strength = jax.nn.sigmoid(
        jnp.dot(spread[HALO:], beta_w[:, :heads], preferred_element_type=F32)
    )
    aux, seg_row = mixer_tables(segments, length, strength, tokens)
    onb, out, new, inverse, before = mixer_fwd(linear, aux, seg_row, taps, gain_head)
    coef = ((tokens_all / 4.0) / valid_sum).reshape(1, 1)
    mask = valid_mask[0].astype(F32)[:, None]
    outputs, squares, second_g, donb, d_hidden, grad_gain_two = mlp(
        inputs_low, onb, out_w, second_w, gain_two, mask, teacher[0], out_grad[0], coef
    )
    dlin, dbl, dtaps, dgain, g_gate, g_up, g_down, g_out = mixer_bwd(
        linear, aux, seg_row, taps, gain_head, out, new, inverse, before, donb,
        second_g, w_gate.shape[1],
    )
    first_g, d_input, grad_gain_one, grad_beta = project_back(
        dlin, first_w, inputs_low, gain_one, dbl, beta_w, d_hidden
    )

    def shares(values):
        return jnp.broadcast_to(values.reshape(1, parts, -1), (halves, parts, values.size // parts))

    tail_parts = [
        grad_beta[:, :heads].reshape(parts, rows, halves, half_heads).transpose(2, 0, 3, 1),
        dtaps[:12]
        .reshape(12, halves, half_heads, parts, WIDTH // parts)
        .transpose(1, 3, 0, 2, 4),
        shares(grad_gain_one),
        shares(grad_gain_two),
        shares(dgain[0]),
        jnp.broadcast_to(squares.reshape(1, 1, 1), (halves, parts, 1)),
    ]
    tail = jnp.concatenate([p.reshape(halves, parts, -1) for p in tail_parts], 2)
    tail_rows = -(-tail.shape[2] // (8 * WIDTH)) * 8
    tail = jnp.pad(tail, ((0, 0), (0, 0), (0, tail_rows * WIDTH - tail.shape[2])))
    g_query, g_key, g_value, tail = scatter(
        first_g, tail.reshape(halves, parts * tail_rows, WIDTH), 3
    )
    sizes = [w_beta.size, conv_weight.size, norm_gain.size, mlp_gain.size, head_gain.size, 1]
    cuts = [sum(sizes[:i]) for i in range(7)]
    g_gate, g_up, g_down, g_out, g_query, g_key, g_value, g_one, g_two, g_head, loss = finish(
        [g_gate, g_up, g_down, g_out, g_query, g_key, g_value],
        tail,
        list(zip(cuts, sizes))[2:],
        (1.0 / (width_d * valid_sum)).reshape(1, 1),
    )
    tail = tail.reshape(-1)
    g_beta, g_conv = tail[: cuts[1]], tail[cuts[1] : cuts[2]]
    return (
        outputs[None],
        loss.reshape(()),
        d_input[None],
        g_one.reshape(-1),
        g_query,
        g_key,
        g_value,
        g_beta.reshape(half_heads, rows).T,
        g_conv.reshape(conv_weight.shape),
        g_head.reshape(-1),
        g_out.T,
        g_two.reshape(-1),
        g_gate,
        g_up,
        g_down.T,
    )


def solution(mesh):
    in_specs = (
        P("dp", "tensor", None),
        P("dp", None),
        P("dp", "tensor"),
        P("dp", "tensor", None),
        P("dp", "tensor", None),
        P("dp"),
        P("dp", "tensor"),
        P("dp", "tensor"),
        P("dp", "tensor"),
        P("dp", "tensor"),
        P(None, None, "tensor", "dp"),
        P("dp"),
        P("tensor", "dp"),
        P("dp"),
        P("dp", "tensor"),
        P("dp", "tensor"),
        P("tensor", "dp"),
    )
    out_specs = (
        P("dp", "tensor", None),
        P(),
        P("dp", "tensor", None),
        P("dp"),
        P("dp", "tensor"),
        P("dp", "tensor"),
        P("dp", "tensor"),
        P("dp", "tensor"),
        P(None, None, "tensor", "dp"),
        P("dp"),
        P("tensor", "dp"),
        P("dp"),
        P("dp", "tensor"),
        P("dp", "tensor"),
        P("tensor", "dp"),
    )
    return jax.shard_map(local, mesh=mesh, in_specs=in_specs, out_specs=out_specs, check_vma=False)
```

```python
import collections
import functools

import jax
import jax.numpy as jnp
from jax import lax
from jax.experimental import pallas as pl
from jax.experimental.pallas import tpu as pltpu
from jax.sharding import PartitionSpec as P

F32, BF16 = jnp.float32, jnp.bfloat16
MESH = pl.DeviceIdType.MESH
CHUNK = 128
HALO = 16
WIDTH = 128
PAIR = 2
MOVES = 2
TAPS = 4
VMEM_LIMIT = 60 * 1024 * 1024

GRID = (4, 2, 2)
DEPTH = GRID[0] - 1 + 2
LAGS = DEPTH + 2
Tiles = collections.namedtuple(
    "Tiles", ["array", "order", "row", "rows", "col", "stride", "cols", "count", "start"]
)


def on_grid():
    return lax.axis_size("dp") == GRID[0] * GRID[1] * GRID[2] and lax.axis_size("tensor") == 2


def position():
    mine = lax.axis_index("dp")
    _, size_x, size_c = GRID
    return {
        "y": lax.axis_index("tensor"),
        "z": mine // (size_x * size_c),
        "x": (mine // size_c) % size_x,
        "c": mine % size_c,
    }


def device_of(at):
    _, size_x, size_c = GRID
    return {"dp": (at["z"] * size_x + at["x"]) * size_c + at["c"], "tensor": at["y"]}


def inside(z):
    return (z >= 0) & (z < GRID[0])


def across(at, link):
    axis, way = link
    return dict(at, z=at["z"] + way) if axis == "z" else dict(at, **{axis: 1 - at[axis]})


def greet_all(at):
    barrier = pltpu.get_barrier_semaphore()
    for link in (("x", 0), ("y", 0), ("c", 0)):
        pl.semaphore_signal(
            barrier, inc=1, device_id=device_of(across(at, link)), device_id_type=MESH
        )
    for way in (-1, 1):

        @pl.when(inside(at["z"] + way))
        def _():
            pl.semaphore_signal(
                barrier,
                inc=1,
                device_id=device_of(across(at, ("z", way))),
                device_id_type=MESH,
            )

    peers = 3 + inside(at["z"] - 1).astype(jnp.int32) + inside(at["z"] + 1).astype(jnp.int32)
    pl.semaphore_wait(barrier, peers)


def remote(src, dst, send_sem, recv_sem, to):
    return pltpu.make_async_remote_copy(
        src_ref=src, dst_ref=dst, send_sem=send_sem, recv_sem=recv_sem,
        device_id=device_of(to), device_id_type=MESH,
    )


def when(test, action):
    if test is None:
        action()
    else:
        pl.when(test)(action)


def both(first, second):
    if first is None or second is None:
        return second if first is None else first
    return first & second


def split_tiles(cols, rows, unit=WIDTH, array=0, start=0):
    half = rows // 2
    count = cols // (3 * unit)
    out = [
        Tiles(array, "zxy", 0, half, 0, 3 * unit, unit, count, start),
        Tiles(array, "zyx", half, half, 0, 3 * unit, unit, count, start),
        Tiles(array, "xzy", 0, half, unit, 3 * unit, 2 * unit, count, start),
        Tiles(array, "yzx", half, half, unit, 3 * unit, 2 * unit, count, start),
    ]
    rest = cols - 3 * unit * count
    if rest:
        out.append(Tiles(array, "xzy", 0, half, cols - rest, rest, rest, 1, start))
        out.append(Tiles(array, "yzx", half, half, cols - rest, rest, rest, 1, start))
    return out


def window(tile, group):
    start = tile.col + group * tile.stride
    if not isinstance(start, int):
        start = pl.multiple_of(start, 128)
    return pl.ds(tile.row, tile.rows), pl.ds(start, tile.cols)


def steps_of(tiles):
    return max(tile.start + tile.count for tile in tiles) + LAGS - 1


def first_slots(tiles):
    return [sum(tile.count for tile in tiles[:i]) for i in range(len(tiles))]


def order_of(tile):
    first, last = [axis for axis in tile.order if axis != "z"]
    return first, last, tile.order[0] == "z"


def distances():
    return range(1 - GRID[0], GRID[0])


def ways(distance):
    return (1, -1) if distance == 0 else ((1,) if distance < 0 else (-1,))


class Gather:
    def __init__(self, tiles, shards, fulls, sems):
        self.tiles, self.shards, self.fulls = tiles, shards, fulls
        self.send_sem, self.recv_sem, self.core_send, self.core_recv, self.own_sem = sems
        self.at = position()
        self.steps = steps_of(tiles)

    @staticmethod
    def sems(tiles, arrays):
        slots = sum(tile.count for tile in tiles)
        return [
            pltpu.SemaphoreType.DMA((len(tiles), 2, 4, GRID[0])),
            pltpu.SemaphoreType.DMA((slots, 3, GRID[0])),
            pltpu.SemaphoreType.DMA((slots,)),
            pltpu.SemaphoreType.DMA((slots,)),
            pltpu.SemaphoreType.DMA((arrays,)),
        ]

    def begin(self):
        at = self.at
        copies = [
            pltpu.make_async_copy(
                shard, full.at[at["y"], at["z"], at["x"], at["c"]], self.own_sem.at[i]
            )
            for i, (shard, full) in enumerate(zip(self.shards, self.fulls))
        ]
        for copy in copies:
            copy.start()
        greet_all(at)
        for copy in copies:
            copy.wait()

    def copy(self, index, group, slot, z, link, own=False):
        at, tile = self.at, self.tiles[index]
        first, last, z_first = order_of(tile)
        rows, cols = window(tile, group)
        pair = link == 3 or (link < 2 and not z_first)
        spot = {"y": at["y"], "x": at["x"]}
        if pair:
            spot[first] = slice(None)
        ref = self.fulls[tile.array].at[spot["y"], z, spot["x"], at["c"], rows, cols]
        to = ("z", 1 - 2 * link) if link < 2 else (first if link == 2 else last, 0)
        return remote(
            self.shards[tile.array].at[rows, cols] if own else ref,
            ref,
            self.send_sem.at[index, group % 2, link, z],
            self.recv_sem.at[slot, max(link - 1, 0), z],
            across(at, to),
        )

    def send(self, index, group, slot, z, link, own=False):
        def go():
            one = self.copy(index, group, slot, z, link, own)
            pl.when(group >= 2)(one.wait_send)
            one.start()

        when(inside(self.at["z"] + 1 - 2 * link) if link < 2 else None, go)

    def visit(self, index, group, slot, lag):
        at, tile = self.at, self.tiles[index]
        _, _, z_first = order_of(tile)
        offset = 0 if z_first else 1
        for far in distances():
            z = at["z"] + far

            def handle():
                if z_first and lag == abs(far):
                    if far:
                        self.copy(index, group, slot, z, 0).wait_recv()
                    for way in ways(far):
                        self.send(index, group, slot, z, (1 - way) // 2, far == 0)
                    self.send(index, group, slot, z, 2, far == 0)
                if z_first and lag == abs(far) + 1:
                    self.copy(index, group, slot, z, 2).wait_recv()
                    self.send(index, group, slot, z, 3)
                if not z_first and far == 0 and lag == 0:
                    self.send(index, group, slot, z, 2, True)
                if not z_first and lag == abs(far) + 1:
                    self.copy(index, group, slot, z, 0 if far else 2).wait_recv()
                    for way in ways(far):
                        self.send(index, group, slot, z, (1 - way) // 2)
                    self.send(index, group, slot, z, 3)
                if lag == abs(far) + 2:
                    self.copy(index, group, slot, z, 3).wait_recv()

            if any(lag == abs(far) + more for more in range(3)):
                when(inside(z) if far else None, handle)
        if lag >= DEPTH:
            rows, cols = window(tile, group)
            part = self.fulls[tile.array].at[:, :, :, at["c"], rows, cols]
            pair = remote(
                part, part, self.core_send.at[slot], self.core_recv.at[slot], across(at, ("c", 0))
            )
            pair.start() if lag == DEPTH else pair.wait()

    def step(self, step):
        for lag in range(LAGS):
            for index, (tile, first) in enumerate(zip(self.tiles, first_slots(self.tiles))):
                group = step - lag - tile.start
                pl.when((group >= 0) & (group < tile.count))(
                    functools.partial(self.visit, index, group, first + group, lag)
                )

    def finish(self):
        for index, tile in enumerate(self.tiles):
            _, _, z_first = order_of(tile)
            for group in range(max(0, tile.count - 2), tile.count):
                for far in distances():
                    z = self.at["z"] + far
                    here = inside(z) if far else None
                    for way in ways(far):
                        one = self.copy(index, group, 0, z, (1 - way) // 2)
                        when(both(here, inside(self.at["z"] + way)), one.wait_send)
                    if z_first or far == 0:
                        when(here, self.copy(index, group, 0, z, 2).wait_send)
                    when(here, self.copy(index, group, 0, z, 3).wait_send)


class Scatter:
    def __init__(self, tiles, grads, put, boxes, sems):
        self.tiles, self.grads, self.put = tiles, grads, put
        self.sums, self.pairs, self.from_z, self.from_first, self.from_last = (
            boxes[i * len(tiles) : (i + 1) * len(tiles)] for i in range(5)
        )
        self.send_sem, self.recv_sem, self.core_send, self.core_recv, self.own_sem = sems
        self.at = position()
        self.steps = steps_of(tiles)

    @staticmethod
    def boxes(tiles, dtypes):
        whole, from_z, from_first, from_last = [], [], [], []
        for tile in tiles:
            z_first = order_of(tile)[2]
            dtype, shape = dtypes[tile.array], (tile.rows, tile.cols)
            whole.append(pltpu.VMEM((tile.count, 2) + GRID[:2] + shape, dtype))
            from_z.append(
                pltpu.VMEM((tile.count, 2, GRID[0]) + (() if z_first else (2,)) + shape, dtype)
            )
            from_first.append(
                pltpu.VMEM((tile.count,) + ((GRID[0],) if z_first else ()) + shape, dtype)
            )
            from_last.append(pltpu.VMEM((tile.count, GRID[0], 2) + shape, dtype))
        return whole + whole + from_z + from_first + from_last

    @staticmethod
    def sems(tiles):
        slots = sum(tile.count for tile in tiles)
        return [
            pltpu.SemaphoreType.DMA((len(tiles), 2, 3, GRID[0])),
            pltpu.SemaphoreType.DMA((slots, 4, GRID[0])),
            pltpu.SemaphoreType.DMA((slots,)),
            pltpu.SemaphoreType.DMA((slots,)),
            pltpu.SemaphoreType.DMA((slots,)),
        ]

    def begin(self):
        greet_all(self.at)

    def spot(self, index, group, z, kind, other=False):
        first, last, z_first = order_of(self.tiles[index])
        spot = {"y": self.at["y"], "x": self.at["x"]}
        if kind == "last" or (kind == "z" and not z_first):
            spot[first] = slice(None)
        if other:
            axis = first if kind == "first" else last
            spot[axis] = 1 - self.at[axis]
        return (group, spot["y"], z, spot["x"])

    def copy(self, index, group, slot, z, kind, way=0):
        first, last, z_first = order_of(self.tiles[index])
        if kind == "z":
            label = (1 + way) // 2
            to, dst = ("z", way), self.from_z[index].at[group, label, z]
        elif kind == "first":
            label, to = 2, (first, 0)
            dst = self.from_first[index].at[(group, z) if z_first else group]
        else:
            label, to, dst = 3, (last, 0), self.from_last[index].at[group, z]
        return remote(
            self.sums[index].at[self.spot(index, group, z, kind, kind != "z")],
            dst,
            self.send_sem.at[index, group % 2, max(label - 1, 0), z],
            self.recv_sem.at[slot, label, z],
            across(self.at, to),
        )

    def send(self, index, group, slot, z, kind, way=0):
        one = self.copy(index, group, slot, z, kind, way)
        pl.when(group >= 2)(one.wait_send)
        one.start()

    def add(self, index, group, slot, z, kind, way=0):
        self.copy(index, group, slot, z, kind, -way).wait_recv()
        z_first = order_of(self.tiles[index])[2]
        if kind == "z":
            came = self.from_z[index][group, (1 - way) // 2, z]
        elif kind == "first":
            came = self.from_first[index][(group, z) if z_first else group]
        else:
            came = self.from_last[index][group, z]
        spot = self.spot(index, group, z, kind)
        total = self.sums[index][spot].astype(F32) + came.astype(F32)
        self.sums[index][spot] = total.astype(self.sums[index].dtype)

    def visit(self, index, group, slot, stage):
        at, tile = self.at, self.tiles[index]
        rows, cols = window(tile, group)
        grad, sums = self.grads[tile.array], self.sums[index]
        _, _, z_first = order_of(tile)
        if stage <= 1:
            pair = remote(
                grad.at[:, :, :, 1 - at["c"], rows, cols],
                self.pairs[index].at[group],
                self.core_send.at[slot],
                self.core_recv.at[slot],
                across(at, ("c", 0)),
            )
            own = pltpu.make_async_copy(
                grad.at[:, :, :, at["c"], rows, cols], sums.at[group], self.own_sem.at[slot]
            )
        if stage == 0:
            pair.start()
            own.start()
            return
        if stage == 1:
            own.wait()
            pair.wait()
            sums[group] = (
                sums[group].astype(F32) + self.pairs[index][group].astype(F32)
            ).astype(sums.dtype)
        lag = DEPTH + 1 - stage

        def along_z(z, far):
            for way in ways(far):
                pl.when(inside(at["z"] + way))(
                    functools.partial(self.add, index, group, slot, z, "z", way)
                )
            if far:
                self.send(index, group, slot, z, "z", 1 if far > 0 else -1)

        for far in distances():
            z = at["z"] + far

            def handle():
                if lag == abs(far) + 2:
                    self.send(index, group, slot, z, "last")
                if lag == abs(far) + 1:
                    self.add(index, group, slot, z, "last")
                    if z_first:
                        self.send(index, group, slot, z, "first")
                    else:
                        along_z(z, far)
                        if far == 0:
                            self.send(index, group, slot, z, "first")
                if lag == abs(far) and (z_first or far == 0):
                    self.add(index, group, slot, z, "first")
                    if z_first:
                        along_z(z, far)
                    if far == 0:
                        self.put(tile, group, sums[group, at["y"], at["z"], at["x"]].astype(F32))

            if any(lag == abs(far) + more for more in range(3)):
                when(inside(z) if far else None, handle)

    def step(self, step):
        for stage in range(LAGS):
            for index, (tile, first) in enumerate(zip(self.tiles, first_slots(self.tiles))):
                group = step - stage - tile.start
                pl.when((group >= 0) & (group < tile.count))(
                    functools.partial(self.visit, index, group, first + group, stage)
                )

    def finish(self):
        for index, tile in enumerate(self.tiles):
            z_first = order_of(tile)[2]
            for group in range(max(0, tile.count - 2), tile.count):
                for far in distances():
                    z = self.at["z"] + far
                    here = inside(z) if far else None
                    if far:
                        one = self.copy(index, group, 0, z, "z", 1 if far > 0 else -1)
                        when(here, one.wait_send)
                    if z_first or far == 0:
                        when(here, self.copy(index, group, 0, z, "first").wait_send)
                    when(here, self.copy(index, group, 0, z, "last").wait_send)


def run_all(moves):
    moves.begin()
    lax.fori_loop(0, moves.steps, lambda step, _: (moves.step(step), 0)[1], 0)
    moves.finish()


def gather_kernel(tiles, arrays, inputs_ref, *refs):
    shards, fulls, edge_ref = refs[:arrays], refs[arrays : 2 * arrays], refs[2 * arrays]
    *sems, edge_sem = refs[2 * arrays + 1 :]
    moves = Gather(tiles, shards, fulls, sems)
    moves.begin()
    edge = remote(
        inputs_ref.at[pl.ds(inputs_ref.shape[0] - HALO, HALO)],
        edge_ref,
        edge_sem.at[0],
        edge_sem.at[1],
        across(moves.at, ("y", 0)),
    )
    edge.start()
    lax.fori_loop(0, moves.steps, lambda step, _: (moves.step(step), 0)[1], 0)
    moves.finish()
    edge.wait()


def gather(shards, inputs, tiles, ident):
    halves = lax.axis_size("tensor")
    if not on_grid():
        fulls = [
            lax.all_gather(shard, ("tensor", "dp"), axis=0, tiled=False).reshape(
                (halves, -1) + shard.shape[1:]
            )
            for shard in shards
        ]
        return fulls + [lax.ppermute(inputs[-HALO:], "tensor", [(0, 1), (1, 0)])]
    hbm = pl.BlockSpec(memory_space=pl.ANY)
    arrays = len(shards)
    *fulls, edge = pl.pallas_call(
        functools.partial(gather_kernel, tiles, arrays),
        in_specs=[hbm] * (arrays + 1),
        out_specs=[hbm] * (arrays + 1),
        out_shape=[
            jax.ShapeDtypeStruct((halves,) + GRID + shard.shape, shard.dtype) for shard in shards
        ]
        + [jax.ShapeDtypeStruct((HALO, inputs.shape[1]), inputs.dtype)],
        scratch_shapes=Gather.sems(tiles, arrays) + [pltpu.SemaphoreType.DMA((2,))],
        compiler_params=pltpu.CompilerParams(collective_id=ident, has_side_effects=True),
        name="gather",
    )(inputs, *shards)
    return [full.reshape(halves, -1, full.shape[-1]) for full in fulls] + [edge]


def put_turns(turns, rest, columns):
    def put(tile, group, total):
        rows = pl.ds(tile.row, tile.rows)
        for i in range(tile.cols // WIDTH):
            piece = total[:, i * WIDTH : (i + 1) * WIDTH]
            at = tile.col // WIDTH + i
            column = at + group * (tile.stride // WIDTH)

            def inner():
                lanes = pl.multiple_of(lax.div(column, len(turns)) * WIDTH, WIDTH)
                turns[at % len(turns)][rows, pl.ds(lanes, WIDTH)] = piece

            if rest is None:
                inner()
                continue
            if tile.count > 1 or at < columns:
                pl.when(column < columns)(inner)

            @pl.when(column >= columns)
            def _():
                lanes = pl.multiple_of((column - columns) * WIDTH, WIDTH)
                rest[rows, pl.ds(lanes, WIDTH)] = piece

    return put


def scatter_kernel(tiles, first_ref, small_grad_ref, query, key, value, small_ref, *rest):
    boxes = 5 * len(tiles)
    turns = put_turns((query, key, value), None, 0)

    def put(tile, group, total):
        if tile.array == 1:
            small_ref[...] = total
        else:
            turns(tile, group, total)

    run_all(Scatter(tiles, [first_ref, small_grad_ref], put, rest[:boxes], rest[boxes:]))


def blocks_of(grad):
    return grad.reshape((2,) + GRID + (-1, grad.shape[-1]))


def plain_scatter(grad):
    return lax.psum_scatter(
        grad.reshape(-1, grad.shape[-1]), ("tensor", "dp"), scatter_dimension=0, tiled=True
    ).astype(F32)


def scatter(first, small, ident):
    rows = first.shape[1] // lax.axis_size("dp")
    if not on_grid():
        return apart(plain_scatter(first), 3) + (plain_scatter(small),)
    grads = [blocks_of(first), blocks_of(small)]
    tiles = split_tiles(first.shape[2], rows)
    small_rows = grads[1].shape[-2]
    tiles.append(Tiles(1, "zxy", 0, small_rows, 0, WIDTH, WIDTH, 1, 0))
    hbm = pl.BlockSpec(memory_space=pl.ANY)
    shapes = [(rows, first.shape[2] // 3)] * 3 + [(small_rows, WIDTH)]
    return pl.pallas_call(
        functools.partial(scatter_kernel, tiles),
        in_specs=[hbm] * 2,
        out_specs=[pl.BlockSpec(memory_space=pltpu.VMEM)] * len(shapes),
        out_shape=[jax.ShapeDtypeStruct(shape, F32) for shape in shapes],
        scratch_shapes=Scatter.boxes(tiles, [grad.dtype for grad in grads]) + Scatter.sems(tiles),
        compiler_params=pltpu.CompilerParams(
            collective_id=ident, has_side_effects=True, vmem_limit_bytes=VMEM_LIMIT
        ),
        name="scatter",
    )(*grads)


def contract(left, right, dim_left, dim_right):
    return lax.dot_general(
        left.astype(BF16),
        right.astype(BF16),
        (((dim_left,), (dim_right,)), ((), ())),
        preferred_element_type=F32,
    )


def mm(left, right):
    return contract(left, right, 1, 0)


def mm_t(left, right):
    return contract(left, right, 1, 1)


def t_mm(left, right):
    return contract(left, right, 0, 0)


def tri_inverses(systems):
    rows = lax.broadcasted_iota(jnp.int32, (CHUNK, CHUNK), 0)
    cols = lax.broadcasted_iota(jnp.int32, (CHUNK, CHUNK), 1)
    inverses = None
    size = 1
    while size < CHUNK:
        link = (
            (rows // (2 * size) == cols // (2 * size))
            & ((rows // size) % 2 == 1)
            & ((cols // size) % 2 == 0)
        )
        parts = [jnp.where(link, system, 0.0) for system in systems]
        if size == 1:
            eye = (rows == cols).astype(F32)
            inverses = [eye - part for part in parts]
        else:
            lows = [inverse.astype(BF16) for inverse in inverses]
            middles = [mm(part, low) for part, low in zip(parts, lows)]
            inverses = [
                inverse - mm(low, middle)
                for inverse, low, middle in zip(inverses, lows, middles)
            ]
        size *= 2
    return inverses


def conv_of(lin_ref, base, lanes, taps, row, keeps, tokens):
    total = lin_ref[0, base : base + tokens, lanes] * taps[row : row + 1]
    for off in range(1, TAPS):
        total = total + taps[row + off : row + off + 1] * (
            lin_ref[0, base - off : base - off + tokens, lanes] * keeps[off]
        )
    return total


def third(sub, index):
    first = (sub * 3 + index) * WIDTH
    return slice(first, first + WIDTH)


def head_column(aux, lane):
    lanes = lax.broadcasted_iota(jnp.int32, aux.shape, 1)
    return jnp.sum(jnp.where(lanes == lane, aux, 0.0), axis=1, keepdims=True)


def greet(partner):
    barrier = pltpu.get_barrier_semaphore()
    pl.semaphore_signal(
        barrier, inc=1, device_id={"tensor": partner}, device_id_type=MESH
    )
    pl.semaphore_wait(barrier, 1)


def chunk_masks(aux, seg_row, at):
    rows = lax.broadcasted_iota(jnp.int32, (CHUNK, CHUNK), 0)
    cols = lax.broadcasted_iota(jnp.int32, (CHUNK, CHUNK), 1)
    same = aux[at : at + CHUNK, 0:1] == seg_row[0:1, at : at + CHUNK]
    return same & (rows > cols), same & (rows >= cols)


def mixer_fwd_kernel(
    tokens, lin_ref, aux_ref, seg_ref, taps_ref, gain_ref,
    onb_ref, o_ref, n_ref, t_ref, s_ref,
    state, outbox, inbox, send_sem, recv_sem,
):
    step = pl.program_id(0)
    mine = lax.axis_index("tensor")
    chunks = tokens // CHUNK

    @pl.when(step == 0)
    def _():
        greet(1 - mine)

    def hand_over(head):
        return pltpu.make_async_remote_copy(
            src_ref=outbox.at[head],
            dst_ref=inbox.at[head],
            send_sem=send_sem.at[head],
            recv_sem=recv_sem.at[head],
            device_id={"tensor": 1 - mine},
            device_id_type=MESH,
        )

    aux = aux_ref[...]
    seg_row = seg_ref[...]
    keeps = [None] + [aux[:, 2 + off : 3 + off] for off in range(1, TAPS)]
    heads = []
    for sub in range(PAIR):
        lanes = slice(sub * WIDTH, (sub + 1) * WIDTH)
        taps = taps_ref[:, lanes]
        beta = head_column(aux, 16 + step * PAIR + sub)
        acts = []
        for index in range(3):
            mixed = conv_of(lin_ref, HALO, third(sub, index), taps, index * TAPS, keeps, tokens)
            acts.append(mixed * jax.nn.sigmoid(mixed))
        q = acts[0] * (
            lax.rsqrt(jnp.sum(acts[0] * acts[0], -1, keepdims=True) + 1e-06) * WIDTH ** (-0.5)
        )
        k = acts[1] * lax.rsqrt(jnp.sum(acts[1] * acts[1], -1, keepdims=True) + 1e-06)
        heads.append((q, k, acts[2], beta))
    spots = [(sub, c) for sub in range(PAIR) for c in range(chunks)]
    masks = [chunk_masks(aux, seg_row, c * CHUNK) for c in range(chunks)]

    def cut(values, c):
        return values[c * CHUNK : (c + 1) * CHUNK]

    lows = [(q.astype(BF16), k.astype(BF16)) for q, k, _, _ in heads]
    systems = [
        jnp.where(
            masks[c][0],
            cut(heads[sub][3], c) * mm_t(cut(lows[sub][1], c), cut(lows[sub][1], c)),
            0.0,
        )
        for sub, c in spots
    ]
    scores_of = [
        jnp.where(masks[c][1], mm_t(cut(lows[sub][0], c), cut(lows[sub][1], c)), 0.0).astype(BF16)
        for sub, c in spots
    ]
    inner = []
    for (sub, c), inverse, scores in zip(spots, tri_inverses(systems), scores_of):
        inverse = inverse.astype(BF16)
        t_ref[sub, c] = inverse
        inner.append((inverse, scores))

    @pl.when(mine == 0)
    def _():
        state[...] = jnp.zeros_like(state)

    @pl.when(mine == 1)
    def _():
        for sub in range(PAIR):
            head = step * PAIR + sub
            hand_over(head).wait_recv()
            state[sub] = inbox[head]

    carried = [state[sub] for sub in range(PAIR)]
    for c in range(chunks):
        at = c * CHUNK
        first = aux[at : at + CHUNK, 1:2]
        last = aux[at : at + CHUNK, 2:3]
        keep = aux[at + CHUNK - 1 : at + CHUNK, 1:2]
        subs = range(PAIR)
        befores = [carried[sub].astype(BF16) for sub in subs]
        reads = [
            mm(jnp.concatenate([cut(lows[sub][1], c), cut(lows[sub][0], c)], 0), befores[sub])
            for sub in subs
        ]
        news = [
            mm(
                inner[sub * chunks + c][0],
                cut(heads[sub][3], c) * (cut(heads[sub][2], c) - first * reads[sub][:CHUNK]),
            ).astype(BF16)
            for sub in subs
        ]
        carried = [
            keep * carried[sub] + t_mm(last * cut(heads[sub][1], c), news[sub]) for sub in subs
        ]
        outs = [
            first * reads[sub][CHUNK:] + mm(inner[sub * chunks + c][1], news[sub]) for sub in subs
        ]
        for sub in subs:
            s_ref[sub, c] = befores[sub]
            n_ref[sub, c] = news[sub]
            lanes = slice(sub * WIDTH, (sub + 1) * WIDTH)
            out = outs[sub]
            o_ref[0, at : at + CHUNK, lanes] = out
            scale = lax.rsqrt(jnp.mean(out * out, -1, keepdims=True) + 1e-05)
            onb_ref[0, at : at + CHUNK, lanes] = (out * scale * gain_ref[0:1]).astype(BF16)

    @pl.when(mine == 0)
    def _():
        for sub in range(PAIR):
            head = step * PAIR + sub
            outbox[head] = carried[sub]
            hand_over(head).start()

    @pl.when((step == pl.num_programs(0) - 1) & (mine == 0))
    def _():
        for head in range(outbox.shape[0]):
            hand_over(head).wait_send()


def mixer_bwd_kernel(
    tokens, tiles, lin_ref, aux_ref, seg_ref, taps_ref, gain_ref,
    o_ref, n_ref, t_ref, s_ref, donb_ref, *refs,
):
    moves = None
    if tiles:
        grads_ref, refs = refs[0], refs[1:]
    dlin_ref, dbl_ref, dtaps_ref, dgain_ref, *refs = refs
    if tiles:
        sums, refs = refs[:4], refs[4:]
    state, extended, outbox, inbox, tailbox, headbox = refs[:6]
    send_sem, recv_sem, tail_send, tail_recv, *refs = refs[6:]
    if tiles:
        boxes = 5 * len(tiles)
        columns = 3 * (sums[0].shape[1] // WIDTH)
        put = put_turns(sums[:3], sums[3], columns)
        moves = Scatter(tiles, [grads_ref], put, refs[:boxes], refs[boxes:])
    step = pl.program_id(0)
    mine = lax.axis_index("tensor")
    chunks = tokens // CHUNK

    @pl.when(step == 0)
    def _():
        if moves:
            moves.begin()
        else:
            greet(1 - mine)
        dbl_ref[...] = jnp.zeros_like(dbl_ref)
        dgain_ref[...] = jnp.zeros_like(dgain_ref)

    def hand_over(head):
        return pltpu.make_async_remote_copy(
            src_ref=outbox.at[head],
            dst_ref=inbox.at[head],
            send_sem=send_sem.at[head],
            recv_sem=recv_sem.at[head],
            device_id={"tensor": 1 - mine},
            device_id_type=MESH,
        )

    def hand_tail(head):
        return pltpu.make_async_remote_copy(
            src_ref=tailbox.at[head],
            dst_ref=headbox.at[head],
            send_sem=tail_send.at[head],
            recv_sem=tail_recv.at[head],
            device_id={"tensor": 1 - mine},
            device_id_type=MESH,
        )

    if moves:
        moves.step(step * MOVES)

    aux = aux_ref[...]
    seg_row = seg_ref[...]
    keeps = [None] + [aux[:tokens, 2 + off : 3 + off] for off in range(1, TAPS)]
    heads, inner = [], []
    for sub in range(PAIR):
        lanes = slice(sub * WIDTH, (sub + 1) * WIDTH)
        taps = taps_ref[:, lanes]
        beta = head_column(aux[:tokens], 16 + step * PAIR + sub)
        mixes, sigs, acts = [], [], []
        for index in range(3):
            mixed = conv_of(lin_ref, HALO, third(sub, index), taps, index * TAPS, keeps, tokens)
            mixes.append(mixed)
            sigs.append(jax.nn.sigmoid(mixed))
            acts.append(mixed * sigs[-1])
        rho_q = lax.rsqrt(jnp.sum(acts[0] * acts[0], -1, keepdims=True) + 1e-06)
        rho_k = lax.rsqrt(jnp.sum(acts[1] * acts[1], -1, keepdims=True) + 1e-06)
        q = acts[0] * (rho_q * WIDTH ** (-0.5))
        k = acts[1] * rho_k
        out = o_ref[0, :, lanes]
        don = donb_ref[0, :, lanes]
        scale = lax.rsqrt(jnp.mean(out * out, -1, keepdims=True) + 1e-05)
        dgain_ref[0:1] += jnp.sum(don * out * scale, 0, keepdims=True)
        du = don * gain_ref[0:1]
        dout = scale * du - out * (scale * scale * scale) * jnp.mean(
            out * du, -1, keepdims=True
        )
        heads.append((q, k, acts, beta, mixes, sigs, rho_q, rho_k, dout))
    spots = [(sub, c) for sub in range(PAIR) for c in range(chunks)]
    masks = [chunk_masks(aux, seg_row, c * CHUNK) for c in range(chunks)]
    firsts = [aux[c * CHUNK : (c + 1) * CHUNK, 1:2] for c in range(chunks)]

    def cut(values, c):
        return values[c * CHUNK : (c + 1) * CHUNK]

    lows = [
        (q.astype(BF16), k.astype(BF16), dout.astype(BF16))
        for q, k, _, _, _, _, _, _, dout in heads
    ]
    grams = [
        mm_t(jnp.concatenate([cut(lows[s][1], c), cut(lows[s][0], c)], 0), cut(lows[s][1], c))
        for s, c in spots
    ]
    turned = [
        mm_t(cut(lows[s][2], c), jnp.concatenate([n_ref[s, c], s_ref[s, c]], 0)) for s, c in spots
    ]
    scores_of = [
        jnp.where(masks[c][1], gram[CHUNK:], 0.0).astype(BF16)
        for (s, c), gram in zip(spots, grams)
    ]
    dscores_of = [
        jnp.where(masks[c][1], turn[:, :CHUNK], 0.0).astype(BF16)
        for (s, c), turn in zip(spots, turned)
    ]
    reads = [mm(cut(lows[s][1], c), s_ref[s, c]) for s, c in spots]
    pulls = [t_mm(scores, cut(lows[s][2], c)) for (s, c), scores in zip(spots, scores_of)]
    reaches = [
        t_mm(firsts[c] * cut(heads[s][0], c), cut(lows[s][2], c)) for s, c in spots
    ]
    dqs = [
        firsts[c] * turn[:, CHUNK:] + mm(dscores, cut(lows[s][1], c))
        for (s, c), turn, dscores in zip(spots, turned, dscores_of)
    ]
    dks = [t_mm(dscores, cut(lows[s][0], c)) for (s, c), dscores in zip(spots, dscores_of)]
    gaps = [
        cut(heads[s][2][2], c) - firsts[c] * read for (s, c), read in zip(spots, reads)
    ]
    inner = [
        (gram[:CHUNK], masks[c][0], pull, reach, dq, dk, gap)
        for (s, c), gram, pull, reach, dq, dk, gap in zip(
            spots, grams, pulls, reaches, dqs, dks, gaps
        )
    ]

    if moves:
        for more in range(1, MOVES):
            moves.step(step * MOVES + more)

    @pl.when(mine == 1)
    def _():
        state[...] = jnp.zeros_like(state)

    @pl.when(mine == 0)
    def _():
        for sub in range(PAIR):
            head = step * PAIR + sub
            hand_over(head).wait_recv()
            state[sub] = inbox[head]

    carried = [state[sub] for sub in range(PAIR)]
    pieces = [[None] * chunks for _ in range(PAIR)]
    for c in reversed(range(chunks)):
        at = c * CHUNK
        first = aux[at : at + CHUNK, 1:2]
        last = aux[at : at + CHUNK, 2:3]
        keep = aux[at + CHUNK - 1 : at + CHUNK, 1:2]
        subs = range(PAIR)
        parts = [inner[sub * chunks + c] for sub in subs]
        betas = [cut(heads[sub][3], c) for sub in subs]
        afters = [carried[sub].astype(BF16) for sub in subs]
        dnews = [
            parts[sub][2] + mm(last * cut(heads[sub][1], c), afters[sub]) for sub in subs
        ]
        backs = [t_mm(t_ref[sub, c], dnews[sub]) for sub in subs]
        dvs = [betas[sub] * backs[sub] for sub in subs]
        dreads = [(-(first * dvs[sub])).astype(BF16) for sub in subs]
        carried = [
            keep * carried[sub] + parts[sub][3] + t_mm(cut(lows[sub][1], c), dreads[sub])
            for sub in subs
        ]
        for sub in subs:
            kk, strict, _, _, dq, dk, gap = parts[sub]
            before, new = s_ref[sub, c], n_ref[sub, c]
            kc = cut(lows[sub][1], c)
            back = backs[sub]
            dsystem = jnp.where(strict, -mm_t(back, new), 0.0)
            dbeta = jnp.sum(back * gap + dsystem * kk, -1, keepdims=True)
            grow = (betas[sub] * dsystem).astype(BF16)
            dk = (
                dk
                + last * mm_t(new, afters[sub])
                + mm_t(dreads[sub], before)
                + mm(grow, kc)
                + t_mm(grow, kc)
            )
            pieces[sub][c] = (dq, dk, dvs[sub], dbeta)

    @pl.when(mine == 1)
    def _():
        for sub in range(PAIR):
            head = step * PAIR + sub
            outbox[head] = carried[sub]
            hand_over(head).start()

    lane_ids = lax.broadcasted_iota(jnp.int32, (tokens, WIDTH), 1)
    for sub in range(PAIR):
        head = step * PAIR + sub
        q, k, acts, beta, mixes, sigs, rho_q, rho_k, dout = heads[sub]
        dq, dk, dv, dbeta = (
            jnp.concatenate([pieces[sub][c][item] for c in range(chunks)], 0)
            for item in range(4)
        )
        dbl_ref[...] += jnp.where(lane_ids == head, dbeta * beta * (1.0 - beta), 0.0)
        dq = dq * WIDTH ** (-0.5)
        dacts = (
            rho_q * dq
            - acts[0] * (rho_q * rho_q * rho_q) * jnp.sum(acts[0] * dq, -1, keepdims=True),
            rho_k * dk
            - acts[1] * (rho_k * rho_k * rho_k) * jnp.sum(acts[1] * dk, -1, keepdims=True),
            dv,
        )
        for index in range(3):
            sig = sigs[index]
            dmix = dacts[index] * sig * (1.0 + mixes[index] * (1.0 - sig))
            extended[sub, index, 0:tokens] = dmix
            tailbox[head, index] = dmix[0:8]

    @pl.when(mine == 1)
    def _():
        extended[:, :, tokens : tokens + 8] = jnp.zeros((PAIR, 3, 8, WIDTH), F32)
        for sub in range(PAIR):
            hand_tail(step * PAIR + sub).start()

    @pl.when(mine == 0)
    def _():
        for sub in range(PAIR):
            head = step * PAIR + sub
            hand_tail(head).wait_recv()
            extended[sub, :, tokens : tokens + 8] = headbox[head]

    later = [None] + [aux[:, 5 + off : 6 + off] for off in range(1, TAPS)]
    for sub in range(PAIR):
        lanes = slice(sub * WIDTH, (sub + 1) * WIDTH)
        taps = taps_ref[:, lanes]
        for index in range(3):
            row = index * TAPS
            dmix = extended[sub, index, 0:tokens]
            dlin = dmix * taps[row : row + 1]
            dtaps_ref[row : row + 1, lanes] = jnp.sum(
                dmix * lin_ref[0, HALO : HALO + tokens, third(sub, index)], 0, keepdims=True
            )
            for off in range(1, TAPS):
                dlin = dlin + taps[row + off : row + off + 1] * (
                    extended[sub, index, off : off + tokens] * later[off]
                )
                dtaps_ref[row + off : row + off + 1, lanes] = jnp.sum(
                    dmix
                    * keeps[off]
                    * lin_ref[0, HALO - off : HALO - off + tokens, third(sub, index)],
                    0,
                    keepdims=True,
                )
            dlin_ref[0, :, third(sub, index)] = dlin.astype(BF16)
        dtaps_ref[12:16, lanes] = jnp.zeros((4, WIDTH), F32)

    if moves:

        @pl.when(step == pl.num_programs(0) - 1)
        def _():
            done = outbox.shape[0] // PAIR * MOVES
            lax.fori_loop(done, moves.steps, lambda i, _: (moves.step(i), 0)[1], 0)
            moves.finish()

    @pl.when((step == pl.num_programs(0) - 1) & (mine == 1))
    def _():
        for head in range(outbox.shape[0]):
            hand_over(head).wait_send()
            hand_tail(head).wait_send()


def mixer_fwd(linear, aux, seg_row, taps, gain):
    halves, rows, cols = linear.shape
    tokens = rows - HALO
    half_heads = cols // 3 // WIDTH
    heads = halves * half_heads
    per_half = half_heads // PAIR
    chunks = tokens // CHUNK
    lanes = PAIR * WIDTH

    def whole(shape):
        return pl.BlockSpec(shape, lambda i: (0,) * len(shape))

    token_spec = pl.BlockSpec((1, tokens, lanes), lambda i: (i // per_half, 0, i % per_half))
    square = pl.BlockSpec((PAIR, chunks, CHUNK, WIDTH), lambda i: (i, 0, 0, 0))
    square_shape = jax.ShapeDtypeStruct((heads, chunks, CHUNK, WIDTH), BF16)
    return pl.pallas_call(
        functools.partial(mixer_fwd_kernel, tokens),
        grid=(heads // PAIR,),
        in_specs=[
            pl.BlockSpec((1, rows, 3 * lanes), lambda i: (i // per_half, 0, i % per_half)),
            whole(aux.shape),
            whole(seg_row.shape),
            pl.BlockSpec((16, lanes), lambda i: (0, i)),
            whole(gain.shape),
        ],
        out_specs=[token_spec, token_spec, square, square, square],
        out_shape=[
            jax.ShapeDtypeStruct((halves, tokens, half_heads * WIDTH), BF16),
            jax.ShapeDtypeStruct((halves, tokens, half_heads * WIDTH), F32),
            square_shape,
            square_shape,
            square_shape,
        ],
        scratch_shapes=[
            pltpu.VMEM((PAIR, WIDTH, WIDTH), F32),
            pltpu.VMEM((heads, WIDTH, WIDTH), F32),
            pltpu.VMEM((heads, WIDTH, WIDTH), F32),
            pltpu.SemaphoreType.DMA((heads,)),
            pltpu.SemaphoreType.DMA((heads,)),
        ],
        compiler_params=pltpu.CompilerParams(
            collective_id=0, has_side_effects=True, vmem_limit_bytes=VMEM_LIMIT
        ),
        name="mixer_fwd",
    )(linear, aux, seg_row, taps, gain)


def mixer_bwd(linear, aux, seg_row, taps, gain, out, new, inverse, before, donb, grads, units):
    halves, rows, cols = linear.shape
    tokens = rows - HALO
    half_heads = cols // 3 // WIDTH
    heads = halves * half_heads
    per_half = half_heads // PAIR
    chunks = tokens // CHUNK
    lanes = PAIR * WIDTH

    def whole(shape):
        return pl.BlockSpec(shape, lambda i: (0,) * len(shape))

    token_spec = pl.BlockSpec((1, tokens, lanes), lambda i: (i // per_half, 0, i % per_half))
    square = pl.BlockSpec((PAIR, chunks, CHUNK, WIDTH), lambda i: (i, 0, 0, 0))
    taps_spec = pl.BlockSpec((16, lanes), lambda i: (0, i))
    tiles, grad_args, grad_specs, sum_shapes, boxes = None, [], [], [], []
    if on_grid():
        block_rows = grads.shape[1] // lax.axis_size("dp")
        tiles = split_tiles(grads.shape[2], block_rows, 2 * WIDTH)
        grad_args, grad_specs = [blocks_of(grads)], [pl.BlockSpec(memory_space=pl.ANY)]
        sum_shapes = [(block_rows, units)] * 3 + [(block_rows, grads.shape[2] - 3 * units)]
        boxes = Scatter.boxes(tiles, [grads.dtype]) + Scatter.sems(tiles)
    results = pl.pallas_call(
        functools.partial(mixer_bwd_kernel, tokens, tiles),
        grid=(heads // PAIR,),
        in_specs=[
            pl.BlockSpec((1, rows, 3 * lanes), lambda i: (i // per_half, 0, i % per_half)),
            whole(aux.shape),
            whole(seg_row.shape),
            taps_spec,
            whole(gain.shape),
            token_spec,
            square,
            square,
            square,
            token_spec,
        ]
        + grad_specs,
        out_specs=[
            pl.BlockSpec((1, tokens, 3 * lanes), lambda i: (i // per_half, 0, i % per_half)),
            whole((tokens, WIDTH)),
            taps_spec,
            whole((8, WIDTH)),
        ]
        + [whole(shape) for shape in sum_shapes],
        out_shape=[
            jax.ShapeDtypeStruct((halves, tokens, cols), BF16),
            jax.ShapeDtypeStruct((tokens, WIDTH), F32),
            jax.ShapeDtypeStruct((16, heads * WIDTH), F32),
            jax.ShapeDtypeStruct((8, WIDTH), F32),
        ]
        + [jax.ShapeDtypeStruct(shape, F32) for shape in sum_shapes],
        scratch_shapes=[
            pltpu.VMEM((PAIR, WIDTH, WIDTH), F32),
            pltpu.VMEM((PAIR, 3, tokens + 8, WIDTH), F32),
            pltpu.VMEM((heads, WIDTH, WIDTH), F32),
            pltpu.VMEM((heads, WIDTH, WIDTH), F32),
            pltpu.VMEM((heads, 3, 8, WIDTH), F32),
            pltpu.VMEM((heads, 3, 8, WIDTH), F32),
            pltpu.SemaphoreType.DMA((heads,)),
            pltpu.SemaphoreType.DMA((heads,)),
            pltpu.SemaphoreType.DMA((heads,)),
            pltpu.SemaphoreType.DMA((heads,)),
        ]
        + boxes,
        compiler_params=pltpu.CompilerParams(
            collective_id=1, has_side_effects=True, vmem_limit_bytes=VMEM_LIMIT
        ),
        name="mixer_bwd",
    )(linear, aux, seg_row, taps, gain, out, new, inverse, before, donb, *grad_args)
    if tiles:
        return results
    second = plain_scatter(grads)
    return list(results) + list(apart(second[:, : 3 * units], 3)) + [second[:, 3 * units :]]


def mlp_kernel(
    count, inputs_ref, onb_ref, weight_ref, *refs,
):
    wo_refs, refs = refs[:4], refs[4:]
    gain_ref, mask_ref, teacher_ref, cot_ref, coef_ref = refs[:5]
    out_ref, square_ref, grad_ref, donb_ref, dhidden_ref, dgain_ref = refs[5:11]
    hidden, normed, normed_t, total, dtotal, dmlp, dmlp_t, gates, uppers, inners = refs[11:]
    step = pl.program_id(0)
    unit = WIDTH

    def out_weight(half):
        return jnp.concatenate([ref[half] for ref in wo_refs], 1)

    def rho_of(values):
        return lax.rsqrt(jnp.mean(values * values, -1, keepdims=True) + 1e-05)

    def spans(first, parts):
        return [weight_ref[half, :, (first + part) * unit : (first + part + 1) * unit]
                for half in range(2) for part in range(parts)]

    @pl.when(step == 0)
    def _():
        rows = inputs_ref[...].astype(F32)
        for half in range(2):
            rows = rows + mm_t(onb_ref[half], out_weight(half))
        hidden[...] = rows
        xn = rows * rho_of(rows) * gain_ref[0:1]
        normed[...] = xn.astype(BF16)
        normed_t[...] = xn.astype(BF16).T
        total[...] = jnp.zeros_like(total)

    @pl.when(step < count)
    def _():
        both_w = jnp.concatenate(spans(0, 2), 1)
        gu = mm(normed[...], both_w)
        gate = jnp.concatenate([gu[:, 0:unit], gu[:, 2 * unit : 3 * unit]], 1)
        upper = jnp.concatenate([gu[:, unit : 2 * unit], gu[:, 3 * unit :]], 1)
        gates[step] = gate
        uppers[step] = upper
        inner = (gate * jax.nn.sigmoid(gate) * upper).astype(BF16)
        inners[step] = inner
        total[...] += mm_t(inner, jnp.concatenate(spans(2, 1), 1))

    @pl.when(step == count - 1)
    def _():
        rows = hidden[...] + total[...]
        out_ref[...] = rows.astype(BF16)
        differ = rows - teacher_ref[...].astype(F32)
        masked = mask_ref[...] * differ
        square_ref[...] = jnp.sum(
            jnp.sum(masked * differ, 1, keepdims=True), 0, keepdims=True
        )
        dout = cot_ref[...].astype(F32) + masked * coef_ref[0:1, 0:1]
        dhidden_ref[...] = dout
        dmlp[...] = dout.astype(BF16)
        dmlp_t[...] = dout.astype(BF16).T
        dtotal[...] = jnp.zeros_like(dtotal)

    @pl.when((step >= count) & (step < 2 * count))
    def _():
        tile = step - count
        dinner = mm(dmlp[...], jnp.concatenate(spans(2, 1), 1))
        gate, upper = gates[tile], uppers[tile]
        sig = jax.nn.sigmoid(gate)
        dgate = (dinner * upper * sig * (1.0 + gate * (1.0 - sig))).astype(BF16)
        dupper = (dinner * (gate * sig)).astype(BF16)
        dgu = jnp.concatenate(
            [dgate[:, :unit], dupper[:, :unit], dgate[:, unit:], dupper[:, unit:]], 1
        )
        dtotal[...] += mm_t(dgu, jnp.concatenate(spans(0, 2), 1))
        grown = mm(normed_t[...], dgu).astype(BF16)
        down = mm(dmlp_t[...], inners[tile]).astype(BF16)

        for half in range(2):
            grad_ref[half, :, : 2 * unit] = grown[:, half * 2 * unit : (half + 1) * 2 * unit]
            grad_ref[half, :, 2 * unit :] = down[:, half * unit : (half + 1) * unit]

    @pl.when(step == 2 * count)
    def _():
        rows = hidden[...]
        rho = rho_of(rows)
        unit_rows = rows * rho
        drows = dtotal[...]
        du = drows * gain_ref[0:1]
        dgain_ref[...] = jnp.sum(drows * unit_rows, 0, keepdims=True)
        dh = dhidden_ref[...] + rho * (du - unit_rows * jnp.mean(du * unit_rows, -1, keepdims=True))
        dhidden_ref[...] = dh
        dattn = dh.astype(BF16)
        dmlp_t[...] = dattn.T
        for half in range(2):
            donb_ref[half] = mm(dattn, out_weight(half))
            grad_ref[half] = mm(dmlp_t[...], onb_ref[half, :, : 3 * unit]).astype(BF16)

    @pl.when(step == 2 * count + 1)
    def _():
        for half in range(2):
            grad_ref[half, :, :unit] = mm(dmlp_t[...], onb_ref[half, :, 3 * unit :]).astype(BF16)


def mlp(inputs, onb, out_weights, weights, gain, mask, teacher, cotangent, coef):
    tokens, width_d = inputs.shape
    halves, _, cols = weights.shape
    half_cols = onb.shape[2]
    count = cols // (3 * WIDTH)

    def whole(shape):
        return pl.BlockSpec(shape, lambda i: (0,) * len(shape))

    def tile(i):
        return (0, 0, jnp.where(i < count, i, jnp.minimum(i - count, count - 1)))

    wide = (halves, width_d, 3 * WIDTH)
    return pl.pallas_call(
        functools.partial(mlp_kernel, count),
        grid=(2 * count + 2,),
        in_specs=[whole(inputs.shape), whole(onb.shape), pl.BlockSpec(wide, tile)]
        + [
            pl.BlockSpec((halves, width_d, WIDTH), functools.partial(lambda n, i: (0, 0, n), n))
            for n in range(4)
        ]
        + [whole(gain.shape), whole(mask.shape), whole(teacher.shape), whole(cotangent.shape), whole(coef.shape)],
        out_specs=[
            whole((tokens, width_d)),
            whole((1, 1)),
            pl.BlockSpec(wide, lambda i: (0, 0, jnp.maximum(i - count, 0))),
            whole((halves, tokens, half_cols)),
            whole((tokens, width_d)),
            whole((1, width_d)),
        ],
        out_shape=[
            jax.ShapeDtypeStruct((tokens, width_d), BF16),
            jax.ShapeDtypeStruct((1, 1), F32),
            jax.ShapeDtypeStruct((halves, width_d, cols + half_cols), BF16),
            jax.ShapeDtypeStruct((halves, tokens, half_cols), F32),
            jax.ShapeDtypeStruct((tokens, width_d), F32),
            jax.ShapeDtypeStruct((1, width_d), F32),
        ],
        scratch_shapes=[
            pltpu.VMEM((tokens, width_d), F32),
            pltpu.VMEM((tokens, width_d), BF16),
            pltpu.VMEM((width_d, tokens), BF16),
            pltpu.VMEM((tokens, width_d), F32),
            pltpu.VMEM((tokens, width_d), F32),
            pltpu.VMEM((tokens, width_d), BF16),
            pltpu.VMEM((width_d, tokens), BF16),
            pltpu.VMEM((count, tokens, 2 * WIDTH), F32),
            pltpu.VMEM((count, tokens, 2 * WIDTH), F32),
            pltpu.VMEM((count, tokens, 2 * WIDTH), BF16),
        ],
        compiler_params=pltpu.CompilerParams(vmem_limit_bytes=VMEM_LIMIT),
        name="mlp",
    )(inputs, onb, weights, *[out_weights] * 4, gain, mask, teacher, cotangent, coef)


def project_back_kernel(
    dlin_ref, weight_ref, inputs_ref, gain_ref, dbl_ref, beta_ref, dhidden_ref,
    grad_ref, dinput_ref, dgain_ref, dbeta_ref,
    normed_t, total,
):
    step = pl.program_id(0)

    def unit():
        rows = inputs_ref[...].astype(F32)
        rho = lax.rsqrt(jnp.mean(rows * rows, -1, keepdims=True) + 1e-05)
        return rows * rho, rho

    @pl.when(step == 0)
    def _():
        normed_t[...] = (unit()[0] * gain_ref[0:1]).astype(BF16).T
        dbl = dbl_ref[...].astype(BF16)
        total[...] = mm_t(dbl, beta_ref[...])
        dbeta_ref[...] = mm(normed_t[...], dbl)

    total[...] += mm_t(dlin_ref[0], weight_ref[0])
    grad_ref[0] = mm(normed_t[...], dlin_ref[0]).astype(BF16)

    @pl.when(step == pl.num_programs(0) - 1)
    def _():
        rows, rho = unit()
        drows = total[...]
        du = drows * gain_ref[0:1]
        dgain_ref[...] = jnp.sum(drows * rows, 0, keepdims=True)
        dinput_ref[...] = dhidden_ref[...] + rho * (
            du - rows * jnp.mean(du * rows, -1, keepdims=True)
        )


def project_back(dlin, weights, inputs, gain, dbl, beta_w, dhidden):
    halves, tokens, cols = dlin.shape
    width_d = inputs.shape[1]
    kinds = 2
    part = cols // kinds

    def whole(shape):
        return pl.BlockSpec(shape, lambda i: (0,) * len(shape))

    columns = pl.BlockSpec((1, width_d, part), lambda i: (i // kinds, 0, i % kinds))
    return pl.pallas_call(
        project_back_kernel,
        grid=(halves * kinds,),
        in_specs=[
            pl.BlockSpec((1, tokens, part), lambda i: (i // kinds, 0, i % kinds)),
            columns,
            whole(inputs.shape),
            whole(gain.shape),
            whole(dbl.shape),
            whole(beta_w.shape),
            whole(dhidden.shape),
        ],
        out_specs=[columns, whole(dhidden.shape), whole((1, width_d)), whole((width_d, WIDTH))],
        out_shape=[
            jax.ShapeDtypeStruct((halves, width_d, cols), BF16),
            jax.ShapeDtypeStruct((tokens, width_d), F32),
            jax.ShapeDtypeStruct((1, width_d), F32),
            jax.ShapeDtypeStruct((width_d, WIDTH), F32),
        ],
        scratch_shapes=[
            pltpu.VMEM((width_d, tokens), BF16),
            pltpu.VMEM((tokens, width_d), F32),
        ],
        compiler_params=pltpu.CompilerParams(vmem_limit_bytes=VMEM_LIMIT),
        name="project_back",
    )(dlin, weights, inputs, gain, dbl, beta_w, dhidden)


def finish_kernel(spans, count, small_ref, scale_ref, *refs):
    outs = refs[count:]
    for source, ref in zip(refs[:count], outs):
        ref[...] = source[...]
    for (start, size), ref in zip(spans, outs[count:]):
        row, lane = start // WIDTH, start % WIDTH
        ref[...] = small_ref[row : row + 1, lane : lane + size]
    outs[-1][...] = outs[-1][...] * scale_ref[...]


def finish(sums, small, spans, scale):
    shapes = [a.shape for a in sums] + [(1, size) for _, size in spans]
    return pl.pallas_call(
        functools.partial(finish_kernel, spans, len(sums)),
        out_shape=[jax.ShapeDtypeStruct(shape, F32) for shape in shapes],
        name="finish",
    )(small, scale, *sums)


def mixer_tables(segments, length, beta, tokens):
    mine = lax.axis_index("tensor")
    seg = segments[0]
    position = jnp.arange(length)

    def behind(off):
        return jnp.where(position >= off, jnp.roll(seg, off), -1)

    ends = jnp.repeat(seg[CHUNK - 1 :: CHUNK], CHUNK)
    previous = jnp.where(position >= CHUNK, jnp.roll(ends, CHUNK), -1)
    columns = [seg, seg == previous, seg == ends]
    keeps = [behind(off) == seg for off in range(1, TAPS)]
    columns += keeps
    for off in range(1, TAPS):
        columns.append(jnp.where(position < length - off, jnp.roll(keeps[off - 1], -off), False))
    table = jnp.stack([c.astype(F32) for c in columns], 1)
    table = lax.dynamic_slice_in_dim(table, mine * tokens, tokens, 0)
    aux = jnp.concatenate(
        [
            table,
            jnp.zeros((tokens, 16 - table.shape[1]), F32),
            beta,
            jnp.zeros((tokens, WIDTH - 16 - beta.shape[1]), F32),
        ],
        1,
    )
    row = lax.dynamic_slice_in_dim(seg.astype(F32), mine * tokens, tokens, 0)
    return aux, row[None]


def by_thirds(first, second, third_one):
    rows = first.shape[0]
    tiles = jnp.stack([a.reshape(rows, -1, WIDTH) for a in (first, second, third_one)], 2)
    return tiles.reshape(rows, -1)


def apart(values, count):
    rows = values.shape[0]
    tiles = values.reshape(rows, -1, count, WIDTH)
    return tuple(tiles[:, :, i].reshape(rows, -1) for i in range(count))


def padded_rows(parts, multiple):
    flat = jnp.concatenate([p.reshape(-1) for p in parts])
    size = -(-flat.shape[0] // (multiple * WIDTH)) * multiple * WIDTH
    return jnp.pad(flat, (0, size - flat.shape[0])).reshape(-1, WIDTH)


def local(
    layer_input, segments, valid_mask, teacher, out_grad, norm_gain, w_query, w_key, w_value,
    w_beta, conv_weight, head_gain, w_out, mlp_gain, w_gate, w_up, w_down,
):
    parts, halves = lax.axis_size("dp"), lax.axis_size("tensor")
    tokens, width_d = layer_input.shape[1:]
    length = segments.shape[1]
    tokens_all = tokens * parts * halves
    half_heads = w_beta.shape[1]
    heads = half_heads * halves
    half_cols = w_query.shape[1]
    rows = w_query.shape[0]
    inputs_low = layer_input[0]

    valid = jnp.sum(valid_mask)
    counts = jnp.stack([valid // 64, valid % 64]).astype(BF16)
    small_parts = [w_beta, conv_weight, norm_gain, mlp_gain, head_gain, counts]
    small = padded_rows(small_parts, 16)
    first_shard = by_thirds(w_query, w_key, w_value)
    second_shard = by_thirds(w_gate, w_up, w_down.T)
    tiles = split_tiles(first_shard.shape[1], rows)
    tiles += split_tiles(half_cols, rows, array=1, start=tiles[0].count)
    tiles.append(Tiles(2, "zxy", 0, small.shape[0], 0, WIDTH, WIDTH, 1, 0))
    first_w, out_w, small, halo = gather([first_shard, w_out.T, small], inputs_low, tiles, 2)
    second_w = lax.all_gather(second_shard, ("tensor", "dp"), axis=0, tiled=True).reshape(
        halves, width_d, second_shard.shape[1]
    )

    small = small.reshape(halves, parts, -1)
    marks = [0]
    for part in small_parts:
        marks.append(marks[-1] + part.size)
    beta_w, conv_w, gain_one, gain_two, gain_head, counts = (
        small[:, :, marks[i] : marks[i + 1]] for i in range(len(small_parts))
    )
    beta_w = beta_w.reshape(halves, width_d, half_heads).transpose(1, 0, 2).reshape(width_d, heads)
    beta_w = jnp.pad(beta_w, ((0, 0), (0, WIDTH - heads)))
    taps = conv_w.reshape((halves, parts) + conv_weight.shape).transpose(2, 3, 0, 4, 1, 5)
    taps = taps.reshape(12, heads * WIDTH).astype(F32)
    taps = jnp.concatenate([taps, jnp.zeros((4, heads * WIDTH), F32)], 0)
    gain_one = gain_one[0].reshape(1, width_d).astype(F32)
    gain_two = gain_two[0].reshape(1, width_d).astype(F32)
    gain_head = gain_head[0].reshape(1, WIDTH).astype(F32)
    counts = jnp.sum(counts.astype(F32), (0, 1))
    valid_sum = counts[0] * 64.0 + counts[1]

    spread = jnp.concatenate([halo, inputs_low], 0).astype(F32)
    rho_one = lax.rsqrt(jnp.mean(spread * spread, -1, keepdims=True) + 1e-05)
    spread = (spread * rho_one * gain_one[0:1]).astype(BF16)
    linear = jnp.einsum("td,jdc->jtc", spread, first_w, preferred_element_type=F32)
    strength = jax.nn.sigmoid(
        jnp.dot(spread[HALO:], beta_w[:, :heads], preferred_element_type=F32)
    )
    aux, seg_row = mixer_tables(segments, length, strength, tokens)
    onb, out, new, inverse, before = mixer_fwd(linear, aux, seg_row, taps, gain_head)
    coef = ((tokens_all / 4.0) / valid_sum).reshape(1, 1)
    mask = valid_mask[0].astype(F32)[:, None]
    outputs, squares, second_g, donb, d_hidden, grad_gain_two = mlp(
        inputs_low, onb, out_w, second_w, gain_two, mask, teacher[0], out_grad[0], coef
    )
    dlin, dbl, dtaps, dgain, g_gate, g_up, g_down, g_out = mixer_bwd(
        linear, aux, seg_row, taps, gain_head, out, new, inverse, before, donb,
        second_g, w_gate.shape[1],
    )
    first_g, d_input, grad_gain_one, grad_beta = project_back(
        dlin, first_w, inputs_low, gain_one, dbl, beta_w, d_hidden
    )

    def shares(values):
        return jnp.broadcast_to(values.reshape(1, parts, -1), (halves, parts, values.size // parts))

    tail_parts = [
        grad_beta[:, :heads].reshape(parts, rows, halves, half_heads).transpose(2, 0, 3, 1),
        dtaps[:12]
        .reshape(12, halves, half_heads, parts, WIDTH // parts)
        .transpose(1, 3, 0, 2, 4),
        shares(grad_gain_one),
        shares(grad_gain_two),
        shares(dgain[0]),
        jnp.broadcast_to(squares.reshape(1, 1, 1), (halves, parts, 1)),
    ]
    tail = jnp.concatenate([p.reshape(halves, parts, -1) for p in tail_parts], 2)
    tail_rows = -(-tail.shape[2] // (8 * WIDTH)) * 8
    tail = jnp.pad(tail, ((0, 0), (0, 0), (0, tail_rows * WIDTH - tail.shape[2])))
    g_query, g_key, g_value, tail = scatter(
        first_g, tail.reshape(halves, parts * tail_rows, WIDTH), 3
    )
    sizes = [w_beta.size, conv_weight.size, norm_gain.size, mlp_gain.size, head_gain.size, 1]
    cuts = [sum(sizes[:i]) for i in range(7)]
    g_gate, g_up, g_down, g_out, g_query, g_key, g_value, g_one, g_two, g_head, loss = finish(
        [g_gate, g_up, g_down, g_out, g_query, g_key, g_value],
        tail,
        list(zip(cuts, sizes))[2:],
        (1.0 / (width_d * valid_sum)).reshape(1, 1),
    )
    tail = tail.reshape(-1)
    g_beta, g_conv = tail[: cuts[1]], tail[cuts[1] : cuts[2]]
    return (
        outputs[None],
        loss.reshape(()),
        d_input[None],
        g_one.reshape(-1),
        g_query,
        g_key,
        g_value,
        g_beta.reshape(half_heads, rows).T,
        g_conv.reshape(conv_weight.shape),
        g_head.reshape(-1),
        g_out.T,
        g_two.reshape(-1),
        g_gate,
        g_up,
        g_down.T,
    )


def solution(mesh):
    in_specs = (
        P("dp", "tensor", None),
        P("dp", None),
        P("dp", "tensor"),
        P("dp", "tensor", None),
        P("dp", "tensor", None),
        P("dp"),
        P("dp", "tensor"),
        P("dp", "tensor"),
        P("dp", "tensor"),
        P("dp", "tensor"),
        P(None, None, "tensor", "dp"),
        P("dp"),
        P("tensor", "dp"),
        P("dp"),
        P("dp", "tensor"),
        P("dp", "tensor"),
        P("tensor", "dp"),
    )
    out_specs = (
        P("dp", "tensor", None),
        P(),
        P("dp", "tensor", None),
        P("dp"),
        P("dp", "tensor"),
        P("dp", "tensor"),
        P("dp", "tensor"),
        P("dp", "tensor"),
        P(None, None, "tensor", "dp"),
        P("dp"),
        P("tensor", "dp"),
        P("dp"),
        P("dp", "tensor"),
        P("dp", "tensor"),
        P("tensor", "dp"),
    )
    return jax.shard_map(local, mesh=mesh, in_specs=in_specs, out_specs=out_specs, check_vma=False)
```
